256 devices in a mesh: band: 8 (over x, core), pos: 32 (over y, z).
Axes of the slice: x: 4, y: 4, z: 8, core: 2. Of those that a mesh axis runs over, the one named last changes fastest.
Arguments:
- wigner: float32 [8, 512, 4096], P('band', 'pos'), may hold values from -6 to 6
- past_iterates: float32 [4, 8, 512, 4096], P(None, 'band', 'pos'), may hold values from -6 to 6
- past_residuals: float32 [4, 8, 512, 4096], P(None, 'band', 'pos'), may hold values from -3 to 3
- velocity: float32 [512, 4096], P('pos'), may hold values from 0.5 to 2
- out_rate: float32 [8, 4096], P('band'), may hold values from 0.0009765625 to 1
- inflow: float32 [8, 4096], P('band'), may hold values from -6 to 6
- offsets: int32 [4096], replicated, may hold values from 1 to 16
- directions: int32 [32], replicated, may hold values from 0 to 1
- coupling: int32 [8], replicated, may hold values from 0 to 7, as said below
Outputs:
- mixed: float32 [8, 512, 4096], P('band', 'pos')
- residual: float32 [8, 512, 4096], P('band', 'pos')
The draws below stay inside these ranges and needn't reach their ends.
Inputs may be any that keep to these rules, and one draw needn't show every extreme that they name: directions: 1 marks blocks whose carriers move toward lower positions. coupling is a permutation of the 8 subbands.
All inputs are finite; a program needn't handle non-finite values.
Results may differ from the reference program's by a relative error of at most 0.00009.
Values sent between devices are 32-bit elements; how exact they have to be, the bound alone decides.
No kernel may reach another device: no remote copies, remote signals or barrier semaphores. Data moves between devices by JAX's collectives and lax.ppermute only.
A program may use at most 128 MiB of HBM per device.

```python
import math
import jax
import jax.numpy as jnp
from jax import lax

S = 8
K = 4096
HIST = 4
OFFMAX = 16
DIRBLK = 32
X = 512


def draw_coupling(key, part):
    order_key = jax.random.fold_in(key, 11)
    pick_key = jax.random.fold_in(key, 23)
    ordering = jax.random.permutation(order_key, S).astype(jnp.int32)
    chosen = jax.random.randint(pick_key, (), 0, S, dtype=jnp.int32)
    target = (chosen + S // 2) % S
    holder = jnp.argmax((ordering == target).astype(jnp.int32)).astype(jnp.int32)
    current = ordering[chosen]
    places = jnp.arange(S, dtype=jnp.int32)
    swapped = jnp.where(places == chosen, target, ordering)
    swapped = jnp.where((places == holder) & (holder != chosen), current, swapped)
    return swapped.astype(jnp.int32)


def place_ends(array, own_key, low, largest):
    index_at = [jax.random.randint(jax.random.fold_in(own_key, axis), (), 0, length) for axis, length in enumerate(array.shape)]
    widest = array.shape.index(max(array.shape))
    next_to = index_at[:widest] + [(index_at[widest] + 1) % array.shape[widest]] + index_at[widest + 1:]
    return array.at[tuple(index_at)].set(low).at[tuple(next_to)].set(largest)


def block_levels(rng, dims, cuts, least, top_value):
    factor_of, own = 1.0, jax.random.fold_in(rng, 6)
    for position, blocks in cuts:
        steps = jnp.exp(jax.random.uniform(jax.random.fold_in(own, position), (blocks,), jnp.float32, least / len(cuts), top_value / len(cuts)))
        factor_of = factor_of * jnp.repeat(steps, dims[position] // blocks).reshape([-1 if axis == position else 1 for axis in range(len(dims))])
    return factor_of


def scatter_about(stream_key, extent, deviation, bound, shards=(), kind=jnp.bfloat16):
    loudness = block_levels(stream_key, extent, shards, -0.22, 0.18) if shards else 1.0
    entries = jax.random.normal(stream_key, extent, jnp.float32) * deviation * loudness
    return jnp.minimum(jnp.maximum(entries, -bound), bound).astype(kind)


def setup_inputs(seed: int = 0) -> dict:
    key_list = jax.random.split(jax.random.key(seed), 10)
    wigner = scatter_about(key_list[0], (S, X, K), 1.0, 6.0, ((0, 8), (1, 32)), jnp.float32)
    past_iterates = scatter_about(key_list[1], (HIST, S, X, K), 1.0, 6.0, ((1, 8), (2, 32)), jnp.float32)
    past_residuals = scatter_about(key_list[2], (HIST, S, X, K), 0.5, 3.0, ((1, 8), (2, 32)), jnp.float32)
    velocity = jnp.clip(jnp.exp(math.log(2.0) - 1.3862944 * jax.random.uniform(key_list[3], (X, K), jnp.float32) ** block_levels(key_list[3], (X, K), ((0, 32),), -0.2, 0.2)), 0.5, 2.0)
    out_rate = jnp.clip(jnp.exp(math.log(1.0) - 6.931472 * jax.random.uniform(key_list[4], (S, K), jnp.float32) ** block_levels(key_list[4], (S, K), ((0, 8),), -0.2, 0.2)), 0.0009765625, 1.0)
    inflow = scatter_about(key_list[5], (S, K), 1.0, 6.0, ((0, 8),), jnp.float32)
    offsets = place_ends(jax.random.randint(key_list[6], (K,), 1, OFFMAX + 1), jax.random.fold_in(key_list[6], 1), 1, OFFMAX).astype(jnp.int32)
    directions = place_ends(jax.random.randint(key_list[7], (DIRBLK,), 0, 2), jax.random.fold_in(key_list[7], 1), 0, 1).astype(jnp.int32)
    coupling = draw_coupling(jax.random.fold_in(key_list[9], 71), 0)
    return dict(wigner=wigner, past_iterates=past_iterates, past_residuals=past_residuals, velocity=velocity, out_rate=out_rate, inflow=inflow, offsets=offsets, directions=directions, coupling=coupling)


MIX_STEP = 0.5
RIDGE_SCALE = 0.0001
PRECISE = lax.Precision.HIGHEST

def shifted_mean(source, offsets):
    width = source.shape[-1]
    columns = jnp.arange(width, dtype=jnp.int32)
    upward = columns + offsets.astype(jnp.int32)
    downward = columns - offsets.astype(jnp.int32)
    above_vals = jnp.take(source, jnp.clip(upward, 0, width - 1), axis=-1)
    below_vals = jnp.take(source, jnp.clip(downward, 0, width - 1), axis=-1)
    above_vals = jnp.where(upward < width, above_vals, 0.0)
    below_vals = jnp.where(downward >= 0, below_vals, 0.0)
    return 0.5 * (above_vals + below_vals)

def mixing_weights(gram):
    count = gram.shape[0]
    scale = jnp.trace(gram) / count
    ridged = gram + RIDGE_SCALE * scale * jnp.eye(count, dtype=jnp.float32)
    factor = jnp.linalg.cholesky(ridged)
    forward_vals = []
    for row in range(count):
        partial_sum = jnp.float32(1.0)
        for inner in range(row):
            partial_sum = partial_sum - factor[row, inner] * forward_vals[inner]
        forward_vals.append(partial_sum / factor[row, row])
    backward_vals = [None] * count
    for row in reversed(range(count)):
        partial_sum = forward_vals[row]
        for inner in range(row + 1, count):
            partial_sum = partial_sum - factor[inner, row] * backward_vals[inner]
        backward_vals[row] = partial_sum / factor[row, row]
    weights = jnp.stack(backward_vals)
    return weights / jnp.sum(weights)

def reference(wigner, past_iterates, past_residuals, velocity, out_rate, inflow, offsets, directions, coupling):
    spread = shifted_mean(wigner, offsets)
    partner = jnp.take(spread, coupling.astype(jnp.int32), axis=0)
    rate_rows = out_rate[:, None, :]
    divisor = velocity[None] + rate_rows
    slope = velocity[None] / divisor
    offset = rate_rows * 0.5 * (spread + partner) / divisor
    backward = jnp.repeat(directions, K // DIRBLK) == 1
    offset = offset.at[:, 0, :].add(jnp.where(backward, 0.0, slope[:, 0, :] * inflow))
    offset = offset.at[:, -1, :].add(jnp.where(backward, slope[:, -1, :] * inflow, 0.0))

    def advance(carry, column_pair):
        fresh = column_pair[0] * carry + column_pair[1]
        return (fresh, fresh)
    start = jnp.zeros((S, K), jnp.float32)
    slope_rows = jnp.moveaxis(slope, 1, 0)
    offset_rows = jnp.moveaxis(offset, 1, 0)
    _, forward_run = lax.scan(advance, start, (slope_rows, offset_rows))
    _, backward_run = lax.scan(advance, start, (slope_rows, offset_rows), reverse=True)
    drifted = jnp.moveaxis(jnp.where(backward[None, None, :], backward_run, forward_run), 0, 1)
    residual = drifted - wigner
    flat_all = jnp.concatenate([past_residuals.reshape(HIST, -1), residual.reshape(1, -1)], axis=0)
    gram = jnp.dot(flat_all.astype(jnp.float32), flat_all.T.astype(jnp.float32), precision=PRECISE, preferred_element_type=jnp.float32)
    weights = mixing_weights(gram)
    blended = jnp.tensordot(weights[:-1], past_iterates + MIX_STEP * past_residuals, axes=1, precision=PRECISE)
    mixed = blended + weights[-1] * (wigner + MIX_STEP * residual)
    return (mixed, residual)
```

```python
import functools

import jax
import jax.numpy as jnp
from jax import lax
from jax.experimental import pallas as pl
from jax.experimental.pallas import tpu as pltpu
from jax.sharding import Mesh
from jax.sharding import PartitionSpec as P

POS = ("pos_0", "pos_1")
BAND = ("band_0", "band_1")

MIX_STEP = 0.5
RIDGE_SCALE = 0.0001
LANES = 128
ROWS = 8
HIST = 4
PAIRS = [(i, j) for i in range(HIST) for j in range(i, HIST)]

VMEM = pl.BlockSpec(memory_space=pltpu.VMEM)
SMEM = pl.BlockSpec(memory_space=pltpu.SMEM)


def call(kernel, outs, in_specs, flops, nbytes):
    return pl.pallas_call(
        kernel,
        out_shape=outs,
        in_specs=in_specs,
        out_specs=jax.tree.map(lambda _: VMEM, outs),
        compiler_params=pltpu.CompilerParams(vmem_limit_bytes=24 * 2**20),
        cost_estimate=pl.CostEstimate(flops=flops, bytes_accessed=nbytes, transcendentals=0),
    )


def f32(*shape):
    return jax.ShapeDtypeStruct(shape, jnp.float32)


def tile(kb):
    return slice(kb * LANES, (kb + 1) * LANES)


def pick(x, index, axis):
    return jnp.take_along_axis(x, index, axis=axis, mode="promise_in_bounds")


def iota(axis):
    return lax.broadcasted_iota(jnp.int32, (ROWS, LANES), axis)


def spread_kernel(offsets, wigner, spread):
    cells, moments = wigner.shape
    tiles = moments // LANES
    per = spread.shape[2] // LANES
    lane = iota(1)
    zero = jnp.zeros((ROWS, LANES), jnp.float32)
    for kb in range(tiles):
        off = jnp.broadcast_to(offsets[:, tile(kb)], (ROWS, LANES))
        up, down = lane + off, lane - off
        up_in, down_in = up & (LANES - 1), down & (LANES - 1)
        for h in range(cells // ROWS):
            rows = slice(h * ROWS, (h + 1) * ROWS)
            here = wigner[rows, tile(kb)]
            nxt = pick(wigner[rows, tile(kb + 1)], up_in, 1) if kb + 1 < tiles else zero
            prv = pick(wigner[rows, tile(kb - 1)], down_in, 1) if kb else zero
            above = jnp.where(up < LANES, pick(here, up_in, 1), nxt)
            below = jnp.where(down >= 0, pick(here, down_in, 1), prv)
            spread[kb // per, rows, tile(kb % per)] = 0.5 * (above + below)


def route_kernel(coupling, held, routed):
    for s in range(routed.shape[0]):
        routed[s] = held[coupling[s]]


def scan_tile(back, a, b):
    row = iota(0)
    away = jnp.where(back, ROWS - 1 - row, row)
    a = [jnp.where(back, a[1], a[0]), jnp.where(back, a[0], a[1])]
    if b is not None:
        b = [jnp.where(back, b[1], b[0]), jnp.where(back, b[0], b[1])]
    for d in (1, 2, 4):
        source = jnp.where(back, row + d, row - d) & (ROWS - 1)
        keep = away >= d
        for h in range(2):
            if b is not None:
                b[h] = a[h] * jnp.where(keep, pick(b[h], source, 0), 0.0) + b[h]
            a[h] = a[h] * jnp.where(keep, pick(a[h], source, 0), 1.0)
    last = jnp.where(back, 0, ROWS - 1) + jnp.zeros_like(row)
    if b is not None:
        b[1] = a[1] * pick(b[0], last, 0) + b[1]
    a[1] = a[1] * pick(a[0], last, 0)
    ends = [pick(a[1], last, 0)]
    if b is not None:
        ends.append(pick(b[1], last, 0))
        b = [jnp.where(back, b[1], b[0]), jnp.where(back, b[0], b[1])]
    a = [jnp.where(back, a[1], a[0]), jnp.where(back, a[0], a[1])]
    return a, b, ends


def coefficients(velocity, out_rate, kb, h):
    v = velocity[h * ROWS : (h + 1) * ROWS, tile(kb)]
    r = jnp.broadcast_to(out_rate[:, tile(kb)], (ROWS, LANES))
    return v, r, 1.0 / (v + r)


def flag(directions, index):
    return jnp.full((ROWS, LANES), directions[index], jnp.int32) == 1


def down(x):
    return jnp.sum(x, axis=0, keepdims=True)


def early_kernel(directions, velocity, out_rate, past_iterates, past_residuals, sums, blends, gram):
    tiles = velocity.shape[1] // LANES
    halves = range(2)
    acc = [jnp.zeros((ROWS, LANES), jnp.float32) for _ in PAIRS]
    for kb in range(tiles):
        back = flag(directions, kb)
        slope = []
        for h in halves:
            v, _, inv = coefficients(velocity, out_rate, kb, h)
            slope.append(v * inv)
        reach, _, ends = scan_tile(back, slope, None)
        past = [[past_residuals[j, h * ROWS : (h + 1) * ROWS, tile(kb)] for h in halves] for j in range(HIST)]
        for j in range(HIST):
            for h in halves:
                rows = slice(h * ROWS, (h + 1) * ROWS)
                blends[j, rows, tile(kb)] = past_iterates[j, rows, tile(kb)] + MIX_STEP * past[j][h]
        for n, (i, j) in enumerate(PAIRS):
            acc[n] = acc[n] + (past[i][0] * past[j][0] + past[i][1] * past[j][1])
        sums[kb, 0:1, :] = ends[0][0:1]
        sums[kb, 1:2, :] = jnp.zeros((1, LANES), jnp.float32)
        for j in range(HIST):
            sums[kb, 2 + j : 3 + j, :] = down(past[j][0] * reach[0] + past[j][1] * reach[1])
        sums[kb, 6:7, :] = down(reach[0] * reach[0] + reach[1] * reach[1])
        sums[kb, 7:8, :] = jnp.zeros((1, LANES), jnp.float32)
    gram[...] = jnp.zeros(gram.shape, jnp.float32)
    for n in range(len(PAIRS)):
        gram[6 + n : 7 + n, :] = down(acc[n])


def local_kernel(
    directions, spread, partner, velocity, out_rate, wigner, past_residuals, early_sums, early_gram, reach_out, rest, sums, gram
):
    tiles = velocity.shape[1] // LANES
    per = spread.shape[2] // LANES
    halves = range(2)
    acc = [jnp.zeros((ROWS, LANES), jnp.float32) for _ in range(HIST + 1)]
    for kb in range(tiles):
        back = flag(directions, kb)
        slope, offset = [], []
        for h in halves:
            rows = slice(h * ROWS, (h + 1) * ROWS)
            v, r, inv = coefficients(velocity, out_rate, kb, h)
            gain = r * 0.5 * (spread[kb // per, rows, tile(kb % per)] + partner[kb // per, rows, tile(kb % per)])
            slope.append(v * inv)
            offset.append(gain * inv)
        reach, run, ends = scan_tile(back, slope, offset)
        left = []
        for h in halves:
            rows = slice(h * ROWS, (h + 1) * ROWS)
            left.append(run[h] - wigner[rows, tile(kb)])
            rest[rows, tile(kb)] = left[h]
            reach_out[rows, tile(kb)] = reach[h]
        for j in range(HIST):
            for h in halves:
                acc[j] = acc[j] + past_residuals[j, h * ROWS : (h + 1) * ROWS, tile(kb)] * left[h]
        acc[HIST] = acc[HIST] + (left[0] * left[0] + left[1] * left[1])
        crossed = down(reach[0] * left[0] + reach[1] * left[1])
        row = iota(0)
        early = early_sums[kb]
        sums[kb] = jnp.where(row == 1, ends[1], jnp.where(row == 7, jnp.broadcast_to(crossed, (ROWS, LANES)), early))
    gram[...] = early_gram[...]
    for n in range(HIST + 1):
        gram[1 + n : 2 + n, :] = down(acc[n])


def carry_kernel(directions, where_at, inflow, sums, gram, message):
    blocks = sums.shape[0]
    at = where_at[0]
    back = directions[at]
    start = pl.multiple_of(at * LANES, LANES)
    carry = inflow[:, pl.ds(start, LANES)]
    row = iota(0)
    acc = jnp.zeros((ROWS, LANES), jnp.float32)
    for step in range(blocks):
        p = jnp.where(back == 1, blocks - 1 - step, step)
        part = sums[p]
        wide = jnp.broadcast_to(carry, (ROWS, LANES))
        message[p, 0:1, :] = carry
        acc = acc + part * jnp.where(row == 6, wide * wide, jnp.where(row == 7, 2.0 * wide, wide))
        carry = part[0:1] * carry + part[1:2]
    terms = jnp.concatenate([acc[2:6], acc[6:7] + acc[7:8]], axis=0) + gram[1:6]
    for p in range(blocks):
        message[p, 1:6, :] = terms
        message[p, 6:, :] = gram[6:]


def finish_kernel(message, reach, rest, wigner, residual, base, gram):
    tiles = wigner.shape[1] // LANES
    total = message[0]
    for kb in range(tiles):
        if kb:
            total = total + message[kb]
        carry = jnp.broadcast_to(message[kb, 0:1, :], (wigner.shape[0], LANES))
        found = rest[:, tile(kb)] + reach[:, tile(kb)] * carry
        residual[:, tile(kb)] = found
        base[:, tile(kb)] = wigner[:, tile(kb)] + MIX_STEP * found
    gram[...] = total


def mixing_weights(entry):
    count = HIST + 1
    scale = sum(entry(i, i) for i in range(count)) / count
    factor = {}
    for i in range(count):
        for j in range(i + 1):
            value = entry(j, i)
            if i == j:
                value = value + RIDGE_SCALE * scale
            for k in range(j):
                value = value - factor[i, k] * factor[j, k]
            factor[i, j] = jnp.sqrt(value) if i == j else value / factor[j, j]
    forward = []
    for row in range(count):
        partial = jnp.ones_like(scale)
        for inner in range(row):
            partial = partial - factor[row, inner] * forward[inner]
        forward.append(partial / factor[row, row])
    backward = [None] * count
    for row in reversed(range(count)):
        partial = forward[row]
        for inner in range(row + 1, count):
            partial = partial - factor[inner, row] * backward[inner]
        backward[row] = partial / factor[row, row]
    total = sum(backward)
    return [z / total for z in backward]


def mix_kernel(gram_0, gram_1, gram_2, gram_3, blends, base, mixed):
    cells, moments = base.shape
    gram = (gram_0[...] + gram_1[...]) + (gram_2[...] + gram_3[...])
    gram = jnp.broadcast_to(jnp.sum(gram, axis=1, keepdims=True), gram.shape)

    def entry(i, j):
        row = 1 + i if j == HIST else 6 + PAIRS.index((i, j))
        return gram[row : row + 1, :]

    weights = [jnp.broadcast_to(w, (cells, LANES)) for w in mixing_weights(entry)]
    for kb in range(moments // LANES):
        total = weights[HIST] * base[:, tile(kb)]
        for j in range(HIST):
            total = total + weights[j] * blends[j, :, tile(kb)]
        mixed[:, tile(kb)] = total


def body(wigner, past_iterates, past_residuals, velocity, out_rate, inflow, offsets, directions, coupling):
    _, cells, moments = wigner.shape
    bands = lax.axis_size(BAND)
    blocks = lax.axis_size(POS)
    where_at = lax.axis_index(POS).astype(jnp.int32).reshape(1)
    wigner = wigner.reshape(cells, moments)
    past_iterates = past_iterates.reshape(HIST, cells, moments)
    past_residuals = past_residuals.reshape(HIST, cells, moments)
    offsets = offsets.reshape(1, moments)
    size = 4 * cells * moments
    share = f32(bands, cells, moments // bands)

    spread = call(spread_kernel, share, [VMEM] * 2, 10 * size, 2 * size)(offsets, wigner)
    held = lax.all_to_all(spread, BAND, 0, 0, tiled=True)
    early_sums, blends, early_gram = call(
        early_kernel,
        (f32(blocks, ROWS, LANES), f32(HIST, cells, moments), f32(16, LANES)),
        [SMEM] + [VMEM] * 4,
        20 * size,
        13 * size,
    )(directions, velocity, out_rate, past_iterates, past_residuals)
    routed = call(route_kernel, share, [SMEM, VMEM], size, 2 * size)(coupling, held)
    partner = lax.all_to_all(routed, BAND, 0, 0, tiled=True)
    reach, rest, sums, gram = call(
        local_kernel,
        (f32(cells, moments), f32(cells, moments), f32(blocks, ROWS, LANES), f32(16, LANES)),
        [SMEM] + [VMEM] * 8,
        20 * size,
        12 * size,
    )(directions, spread, partner, velocity, out_rate, wigner, past_residuals, early_sums, early_gram)
    sums = lax.all_to_all(sums, POS, 0, 0, tiled=True)
    message = call(carry_kernel, f32(blocks, 16, LANES), [SMEM] * 2 + [VMEM] * 3, size, 2 * size)(
        directions, where_at, inflow, sums, gram
    )
    message = lax.all_to_all(message, POS, 0, 0, tiled=True)
    residual, base, gram = call(
        finish_kernel, (f32(cells, moments), f32(cells, moments), f32(16, LANES)), [VMEM] * 4, size, 6 * size
    )(message, reach, rest, wigner)
    gram = gram + lax.ppermute(gram, BAND[1], [(0, 1), (1, 0)])
    chips = lax.axis_size(BAND[0])
    others = [lax.ppermute(gram, BAND[0], [(i, (i + d) % chips) for i in range(chips)]) for d in range(1, chips)]
    mixed = call(mix_kernel, f32(cells, moments), [VMEM] * 6, 3 * size, 6 * size)(gram, *others, blends, base)
    return mixed[None], residual[None]


def solution(mesh):
    finer = Mesh(mesh.devices.reshape(4, 2, 4, 8), ("band_0", "band_1", "pos_0", "pos_1"))
    in_specs = (
        P(BAND, POS, None),
        P(None, BAND, POS, None),
        P(None, BAND, POS, None),
        P(POS, None),
        P(BAND, None),
        P(BAND, None),
        P(),
        P(),
        P(),
    )
    out_specs = (P(BAND, POS, None), P(BAND, POS, None))
    return jax.shard_map(body, mesh=finer, in_specs=in_specs, out_specs=out_specs, check_vma=False)
```

```python
import functools

import jax
import jax.numpy as jnp
from jax import lax
from jax.experimental import pallas as pl
from jax.experimental.pallas import tpu as pltpu
from jax.sharding import Mesh
from jax.sharding import PartitionSpec as P

POS = ("pos_0", "pos_1")
BAND = ("band_0", "band_1")
ALL = BAND + POS

MIX_STEP = 0.5
RIDGE_SCALE = 0.0001
LANES = 128
GROUP = 16
ROWS = 8
HIST = 4
PAIRS = [(i, j) for i in range(HIST) for j in range(i, HIST)]

VMEM = pl.BlockSpec(memory_space=pltpu.VMEM)
SMEM = pl.BlockSpec(memory_space=pltpu.SMEM)
HBM = pl.BlockSpec(memory_space=pltpu.HBM)


def call(kernel, outs, in_specs, flops, nbytes, scratch=(), mib=24):
    return pl.pallas_call(
        kernel,
        out_shape=outs,
        in_specs=in_specs,
        out_specs=jax.tree.map(lambda _: VMEM, outs),
        scratch_shapes=list(scratch),
        compiler_params=pltpu.CompilerParams(vmem_limit_bytes=mib * 2**20),
        cost_estimate=pl.CostEstimate(flops=flops, bytes_accessed=nbytes, transcendentals=0),
    )


def f32(*shape):
    return jax.ShapeDtypeStruct(shape, jnp.float32)


def tile(kb):
    return slice(kb * LANES, (kb + 1) * LANES)


def pick(x, index, axis):
    return jnp.take_along_axis(x, index, axis=axis, mode="promise_in_bounds")


def iota(axis):
    return lax.broadcasted_iota(jnp.int32, (ROWS, LANES), axis)


def scan_tile(back, a, b):
    row = iota(0)
    away = jnp.where(back, ROWS - 1 - row, row)
    a = [jnp.where(back, a[1], a[0]), jnp.where(back, a[0], a[1])]
    if b is not None:
        b = [jnp.where(back, b[1], b[0]), jnp.where(back, b[0], b[1])]
    for d in (1, 2, 4):
        source = jnp.where(back, row + d, row - d) & (ROWS - 1)
        keep = away >= d
        for h in range(2):
            if b is not None:
                b[h] = a[h] * jnp.where(keep, pick(b[h], source, 0), 0.0) + b[h]
            a[h] = a[h] * jnp.where(keep, pick(a[h], source, 0), 1.0)
    last = jnp.where(back, 0, ROWS - 1) + jnp.zeros_like(row)
    if b is not None:
        b[1] = a[1] * pick(b[0], last, 0) + b[1]
    a[1] = a[1] * pick(a[0], last, 0)
    ends = [pick(a[1], last, 0)]
    if b is not None:
        ends.append(pick(b[1], last, 0))
        b = [jnp.where(back, b[1], b[0]), jnp.where(back, b[0], b[1])]
    a = [jnp.where(back, a[1], a[0]), jnp.where(back, a[0], a[1])]
    return a, b, ends


def coefficients(velocity, out_rate, kb, h):
    v = velocity[h * ROWS : (h + 1) * ROWS, tile(kb)]
    r = jnp.broadcast_to(out_rate[:, tile(kb)], (ROWS, LANES))
    return v, r, 1.0 / (v + r)


def flag(directions, index):
    return jnp.full((ROWS, LANES), directions[index], jnp.int32) == 1


def down(x):
    return jnp.sum(x, axis=0, keepdims=True)


def half(h):
    return slice(h * ROWS, (h + 1) * ROWS)


def open_kernel(directions, *refs):
    sources, message, held, arrived = refs[:6], refs[6], refs[7:13], refs[13]
    copies = [pltpu.make_async_copy(a, b, arrived.at[n]) for n, (a, b) in enumerate(zip(sources, held))]
    for copy in copies:
        copy.start()
    offsets, wigner, velocity, out_rate, inflow, past_residuals = held
    tiles = wigner.shape[1] // LANES
    per = message.shape[2] // LANES
    lane = iota(1)
    zero = jnp.zeros((ROWS, LANES), jnp.float32)
    copies[0].wait()
    copies[1].wait()
    for kb in range(tiles):
        off = jnp.broadcast_to(offsets[:, tile(kb)], (ROWS, LANES))
        up, below_at = lane + off, lane - off
        up_in, down_in = up & (LANES - 1), below_at & (LANES - 1)
        for h in range(2):
            here = wigner[half(h), tile(kb)]
            nxt = pick(wigner[half(h), tile(kb + 1)], up_in, 1) if kb + 1 < tiles else zero
            prv = pick(wigner[half(h), tile(kb - 1)], down_in, 1) if kb else zero
            above = jnp.where(up < LANES, pick(here, up_in, 1), nxt)
            below = jnp.where(below_at >= 0, pick(here, down_in, 1), prv)
            message[kb // per, half(h), tile(kb % per)] = 0.5 * (above + below)
    for copy in copies[2:]:
        copy.wait()
    for kb in range(tiles):
        back = flag(directions, kb)
        slope = []
        for h in range(2):
            v, _, inv = coefficients(velocity, out_rate, kb, h)
            slope.append(v * inv)
        reach, _, _ = scan_tile(back, slope, None)

        def put(row, value):
            message[kb // per, 2 * ROWS + row : 2 * ROWS + row + 1, tile(kb % per)] = value

        for j in range(HIST):
            put(j, down(sum(past_residuals[j, half(h), tile(kb)] * reach[h] for h in range(2))))
        put(4, down(sum(reach[h] * reach[h] for h in range(2))))
        put(5, down(sum(reach[h] * wigner[half(h), tile(kb)] for h in range(2))))
        put(6, out_rate[:, tile(kb)])
        put(7, inflow[:, tile(kb)])


def history_kernel(past_iterates, past_residuals, blends, gram):
    tiles = past_residuals.shape[2] // LANES
    acc = [jnp.zeros((ROWS, LANES), jnp.float32) for _ in PAIRS]
    for kb in range(tiles):
        for h in range(2):
            past = [past_residuals[j, half(h), tile(kb)] for j in range(HIST)]
            for j in range(HIST):
                blends[j, half(h), tile(kb)] = past_iterates[j, half(h), tile(kb)] + MIX_STEP * past[j]
            for n, (i, j) in enumerate(PAIRS):
                acc[n] = acc[n] + past[i] * past[j]
    gram[...] = jnp.zeros(gram.shape, jnp.float32)
    for n in range(len(PAIRS)):
        gram[6 + n : 7 + n, :] = down(acc[n])


def at_contact(ids, blocks, back, slope, inflow):
    row = iota(0)
    place = jnp.full((ROWS, LANES), ids[1], jnp.int32)
    first = (place == 0) & (row == 0) & jnp.logical_not(back)
    final = (place == blocks - 1) & (row == ROWS - 1) & back
    wide = jnp.broadcast_to(inflow, (ROWS, LANES))
    return [jnp.where(first, slope[0] * wide, 0.0), jnp.where(final, slope[1] * wide, 0.0)]


def fold_kernel(directions, coupling, ids, held, velocity, message, *shares):
    bands = held.shape[0]
    blocks = message.shape[0]
    per = held.shape[2] // LANES
    row, lane = iota(0), iota(1)
    for d in range(bands):
        s = ids[0] ^ d
        shares[d][...] = held[s, 0 : 2 * ROWS, :] + held[coupling[s], 0 : 2 * ROWS, :]
    for kt in range(per):
        kb = ids[0] * per + kt
        back = flag(directions, kb)
        columns = pl.ds(pl.multiple_of(kb * LANES, LANES), LANES)
        parts = []
        for s in range(bands):
            tail = held[s, 2 * ROWS :, tile(kt)]
            rate = jnp.broadcast_to(tail[6:7], (ROWS, LANES))
            slope, offset = [], []
            for h in range(2):
                v = velocity[half(h), columns]
                inv = 1.0 / (v + rate)
                both = held[s, half(h), tile(kt)] + held[coupling[s], half(h), tile(kt)]
                slope.append(v * inv)
                offset.append(rate * 0.5 * both * inv)
            edge = at_contact(ids, blocks, back, slope, tail[7:8])
            offset = [offset[h] + edge[h] for h in range(2)]
            reach, run, ends = scan_tile(back, slope, offset)
            crossed = jnp.broadcast_to(down(reach[0] * run[0] + reach[1] * run[1]), (ROWS, LANES)) - tail
            parts.append(
                jnp.where(row == 5, crossed, jnp.where(row == 6, ends[0], jnp.where(row == 7, ends[1], tail)))
            )
        for bit in range(3):
            step = 1 << bit
            high = ((lane >> (4 + bit)) & 1) == 1
            swapped = list(parts)
            for s in range(bands):
                if not s & step:
                    swapped[s] = jnp.where(high, pltpu.roll(parts[s + step], GROUP * step, 1), parts[s])
                    swapped[s + step] = jnp.where(high, parts[s + step], pltpu.roll(parts[s], LANES - GROUP * step, 1))
            parts = swapped
        for g in range(bands):
            message[kt * bands + g] = parts[g]


def settle_kernel(directions, ids, *refs):
    shares = refs[:8]
    velocity, out_rate, inflow, wigner, past_residuals, early, marks, reach_out, rest, gram = refs[8:]
    per = shares[0].shape[1] // LANES
    blocks = velocity.shape[1] // LANES
    acc = [jnp.zeros((ROWS, LANES), jnp.float32) for _ in range(HIST + 1)]
    for d in range(len(shares)):
        for kt in range(per):
            kb = (ids[0] ^ d) * per + kt
            back = flag(directions, kb)
            columns = pl.ds(pl.multiple_of(kb * LANES, LANES), LANES)
            rate = jnp.broadcast_to(out_rate[:, columns], (ROWS, LANES))
            slope, offset = [], []
            for h in range(2):
                v = velocity[half(h), columns]
                inv = 1.0 / (v + rate)
                slope.append(v * inv)
                offset.append(rate * 0.5 * shares[d][half(h), tile(kt)] * inv)
            edge = at_contact(ids, blocks, back, slope, inflow[:, columns])
            offset = [offset[h] + edge[h] for h in range(2)]
            reach, run, _ = scan_tile(back, slope, offset)
            for h in range(2):
                left = run[h] - wigner[half(h), columns]
                rest[half(h), columns] = left
                reach_out[half(h), columns] = reach[h]
                for j in range(HIST):
                    acc[j] = acc[j] + past_residuals[j, half(h), columns] * left
                acc[HIST] = acc[HIST] + left * left
    gram[...] = early[...]
    for n in range(HIST + 1):
        gram[n : n + 1, :] = down(acc[n])
    marks[...] = jnp.full((ROWS, LANES), directions[ids[0] * per + ids[1] // ROWS], jnp.int32)


def carry_kernel(marks, sums, gram, message, forth, counter):
    blocks = sums.shape[0]
    row, lane = iota(0), iota(1)
    back = marks[...] == 1
    acc = jnp.zeros((ROWS, LANES), jnp.float32)
    carry = jnp.zeros((1, LANES), jnp.float32)
    for step in range(blocks):
        part = jnp.where(back, sums[blocks - 1 - step], sums[step])
        wide = jnp.broadcast_to(carry, (ROWS, LANES))
        forth[step : step + 1, :] = carry
        counter[blocks - 1 - step : blocks - step, :] = carry
        acc = acc + part * jnp.where(row == 4, wide * wide, jnp.where(row == 5, 2.0 * wide, wide))
        carry = part[6:7] * carry + part[7:8]
    terms = [gram[half(0), :] + jnp.where(row < 6, acc, 0.0), gram[half(1), :]]
    line = jnp.zeros((ROWS, LANES), jnp.float32)
    for h in range(2):
        whole = jnp.broadcast_to(jnp.sum(terms[h], axis=1, keepdims=True), (ROWS, LANES))
        line = line + jnp.where(lane == GROUP + h * ROWS + row, whole, 0.0)
    line = jnp.broadcast_to(down(line), (ROWS, LANES))
    for q in range(blocks // ROWS):
        carries = jnp.where(back, counter[half(q), :], forth[half(q), :])
        for s in range(LANES // GROUP):
            turned = pltpu.roll(carries, LANES - GROUP * s, 1) if s else carries
            message[s * blocks + q * ROWS : s * blocks + (q + 1) * ROWS, :] = jnp.where(lane < GROUP, turned, line)


def mixing_weights(entry):
    count = HIST + 1
    scale = sum(entry(i, i) for i in range(count)) / count
    factor = {}
    for i in range(count):
        for j in range(i + 1):
            value = entry(j, i)
            if i == j:
                value = value + RIDGE_SCALE * scale
            for k in range(j):
                value = value - factor[i, k] * factor[j, k]
            factor[i, j] = jnp.sqrt(value) if i == j else value / factor[j, j]
    forward = []
    for row in range(count):
        partial = jnp.ones_like(scale)
        for inner in range(row):
            partial = partial - factor[row, inner] * forward[inner]
        forward.append(partial / factor[row, row])
    backward = [None] * count
    for row in reversed(range(count)):
        partial = forward[row]
        for inner in range(row + 1, count):
            partial = partial - factor[inner, row] * backward[inner]
        backward[row] = partial / factor[row, row]
    total = sum(backward)
    return [z / total for z in backward]


def finish_kernel(message, reach, rest, wigner, blends, residual, mixed):
    tiles = wigner.shape[1] // LANES
    row, lane = iota(0), iota(1)
    total = message[half(0), :]
    for kb in range(1, tiles):
        total = total + message[half(kb), :]
    total = jnp.broadcast_to(down(total), (ROWS, LANES))

    def term(n):
        return pick(total, jnp.full((ROWS, LANES), GROUP + n, jnp.int32), 1)

    def entry(i, j):
        if j == HIST:
            return term(4) + term(5) if i == HIST else term(i)
        return term(6 + PAIRS.index((i, j)))

    weights = mixing_weights(entry)
    for kb in range(tiles):
        spots = pick(message[half(kb), :], lane & (GROUP - 1), 1)
        carry = jnp.broadcast_to(down(jnp.where((lane >> 4) == row, spots, 0.0)), (ROWS, LANES))
        for h in range(2):
            found = rest[half(h), tile(kb)] + reach[half(h), tile(kb)] * carry
            residual[half(h), tile(kb)] = found
            value = weights[HIST] * (wigner[half(h), tile(kb)] + MIX_STEP * found)
            for j in range(HIST):
                value = value + weights[j] * blends[j, half(h), tile(kb)]
            mixed[half(h), tile(kb)] = value


def body(wigner, past_iterates, past_residuals, velocity, out_rate, inflow, offsets, directions, coupling):
    _, cells, moments = wigner.shape
    bands = lax.axis_size(BAND)
    blocks = lax.axis_size(POS)
    ids = jnp.stack([lax.axis_index(BAND), lax.axis_index(POS)]).astype(jnp.int32)
    wigner = wigner.reshape(cells, moments)
    past_iterates = past_iterates.reshape(HIST, cells, moments)
    past_residuals = past_residuals.reshape(HIST, cells, moments)
    offsets = offsets.reshape(1, moments)
    size = 4 * cells * moments
    share = moments // bands

    sources = (offsets, wigner, velocity, out_rate, inflow, past_residuals)
    message = call(
        open_kernel,
        f32(bands, cells + ROWS, share),
        [SMEM] + [HBM] * 6,
        20 * size,
        8 * size,
        [pltpu.VMEM(x.shape, x.dtype) for x in sources] + [pltpu.SemaphoreType.DMA((6,))],
        mib=60,
    )(directions, *sources)
    held = lax.all_to_all(message, BAND, 0, 0, tiled=True)
    blends, early = call(
        history_kernel, (f32(HIST, cells, moments), f32(16, LANES)), [VMEM] * 2, 8 * size, 12 * size
    )(past_iterates, past_residuals)
    sums, *shares = call(
        fold_kernel,
        (f32(blocks, ROWS, LANES),) + (f32(cells, share),) * bands,
        [SMEM] * 3 + [VMEM] * 2,
        20 * size,
        5 * size,
    )(directions, coupling, ids, held, velocity)
    sums = lax.all_to_all(sums, POS, 0, 0, tiled=True)
    shares = [shares[0]] + [
        lax.ppermute(shares[d], BAND, [(i, i ^ d) for i in range(bands)]) for d in range(1, bands)
    ]
    marks, reach, rest, gram = call(
        settle_kernel,
        (jax.ShapeDtypeStruct((ROWS, LANES), jnp.int32), f32(cells, moments), f32(cells, moments), f32(16, LANES)),
        [SMEM] * 2 + [VMEM] * 14,
        20 * size,
        10 * size,
    )(directions, ids, *shares, velocity, out_rate, inflow, wigner, past_residuals, early)
    message = call(
        carry_kernel,
        f32(bands * blocks, LANES),
        [VMEM] * 3,
        size,
        size,
        [pltpu.VMEM((blocks, LANES), jnp.float32)] * 2,
    )(marks, sums, gram)
    message = lax.all_to_all(message, ALL, 0, 0, tiled=True)
    residual, mixed = call(
        finish_kernel, (f32(cells, moments), f32(cells, moments)), [VMEM] * 5, 8 * size, 10 * size
    )(message, reach, rest, wigner, blends)
    return mixed[None], residual[None]


def solution(mesh):
    finer = Mesh(mesh.devices.reshape(4, 2, 4, 8), ("band_0", "band_1", "pos_0", "pos_1"))
    in_specs = (
        P(BAND, POS, None),
        P(None, BAND, POS, None),
        P(None, BAND, POS, None),
        P(POS, None),
        P(BAND, None),
        P(BAND, None),
        P(),
        P(),
        P(),
    )
    out_specs = (P(BAND, POS, None), P(BAND, POS, None))
    return jax.shard_map(body, mesh=finer, in_specs=in_specs, out_specs=out_specs, check_vma=False)
```

```python
import functools

import jax
import jax.numpy as jnp
from jax import lax
from jax.experimental import pallas as pl
from jax.experimental.pallas import tpu as pltpu
from jax.sharding import Mesh
from jax.sharding import PartitionSpec as P

POS = ("pos_0", "pos_1")
BAND = ("band_0", "band_1")
ALL = BAND + POS

MIX_STEP = 0.5
RIDGE_SCALE = 0.0001
LANES = 128
GROUP = 16
ROWS = 8
HIST = 4
PAIRS = [(i, j) for i in range(HIST) for j in range(i, HIST)]

VMEM = pl.BlockSpec(memory_space=pltpu.VMEM)
HBM = pl.BlockSpec(memory_space=pltpu.HBM)


def call(kernel, outs, in_specs, flops, nbytes, scratch=(), mib=24, out_specs=None):
    return pl.pallas_call(
        kernel,
        out_shape=outs,
        in_specs=in_specs,
        out_specs=jax.tree.map(lambda _: VMEM, outs) if out_specs is None else out_specs,
        scratch_shapes=list(scratch),
        compiler_params=pltpu.CompilerParams(vmem_limit_bytes=mib * 2**20),
        cost_estimate=pl.CostEstimate(flops=flops, bytes_accessed=nbytes, transcendentals=0),
    )


def f32(*shape):
    return jax.ShapeDtypeStruct(shape, jnp.float32)


def tile(kb):
    return slice(kb * LANES, (kb + 1) * LANES)


def pick(x, index, axis):
    return jnp.take_along_axis(x, index, axis=axis, mode="promise_in_bounds")


def iota(axis):
    return lax.broadcasted_iota(jnp.int32, (ROWS, LANES), axis)


def scan_tile(back, a, b):
    row = iota(0)
    away = jnp.where(back, ROWS - 1 - row, row)
    a = [jnp.where(back, a[1], a[0]), jnp.where(back, a[0], a[1])]
    if b is not None:
        b = [jnp.where(back, b[1], b[0]), jnp.where(back, b[0], b[1])]
    for d in (1, 2, 4):
        source = jnp.where(back, row + d, row - d) & (ROWS - 1)
        keep = away >= d
        for h in range(2):
            if b is not None:
                b[h] = a[h] * jnp.where(keep, pick(b[h], source, 0), 0.0) + b[h]
            a[h] = a[h] * jnp.where(keep, pick(a[h], source, 0), 1.0)
    last = jnp.where(back, 0, ROWS - 1) + jnp.zeros_like(row)
    if b is not None:
        b[1] = a[1] * pick(b[0], last, 0) + b[1]
    a[1] = a[1] * pick(a[0], last, 0)
    ends = [pick(a[1], last, 0)]
    if b is not None:
        ends.append(pick(b[1], last, 0))
        b = [jnp.where(back, b[1], b[0]), jnp.where(back, b[0], b[1])]
    a = [jnp.where(back, a[1], a[0]), jnp.where(back, a[0], a[1])]
    return a, b, ends


def coefficients(velocity, out_rate, kb, h):
    v = velocity[h * ROWS : (h + 1) * ROWS, tile(kb)]
    r = jnp.broadcast_to(out_rate[:, tile(kb)], (ROWS, LANES))
    return v, r, 1.0 / (v + r)


def flag(notes, index):
    return jnp.broadcast_to(notes[pl.ds(index, 1), :], (ROWS, LANES)) == 1


def down(x):
    return jnp.sum(x, axis=0, keepdims=True)


def half(h):
    return slice(h * ROWS, (h + 1) * ROWS)


def added_rows(parts):
    row = iota(0)
    parts = parts + [jnp.zeros((ROWS, LANES), jnp.float32)] * (ROWS - len(parts))
    for d in (4, 2, 1):
        low = (row & d) == 0
        count = len(parts) // 2
        parts = [
            jnp.where(low, parts[n], parts[n + count])
            + pick(jnp.where(low, parts[n + count], parts[n]), row ^ d, 0)
            for n in range(count)
        ]
    return parts[0]


def open_kernel(*refs):
    sources, message, notes, held, ready, arrived, gone = refs[:8], refs[8], refs[9], refs[10:18], *refs[18:]
    copies = [pltpu.make_async_copy(a, b, arrived.at[n]) for n, (a, b) in enumerate(zip(sources, held))]
    for copy in copies:
        copy.start()
    offsets, wigner, directions, coupling, velocity, out_rate, inflow, past_residuals = held
    tiles = wigner.shape[1] // LANES
    per = message.shape[2] // LANES
    row, lane = iota(0), iota(1)
    zero = jnp.zeros((ROWS, LANES), jnp.float32)
    copies[0].wait()
    copies[1].wait()
    for kb in range(tiles):
        off = jnp.broadcast_to(offsets[:, tile(kb)], (ROWS, LANES))
        up, below_at = lane + off, lane - off
        up_in, down_in = up & (LANES - 1), below_at & (LANES - 1)
        for h in range(2):
            here = wigner[half(h), tile(kb)]
            nxt = pick(wigner[half(h), tile(kb + 1)], up_in, 1) if kb + 1 < tiles else zero
            prv = pick(wigner[half(h), tile(kb - 1)], down_in, 1) if kb else zero
            above = jnp.where(up < LANES, pick(here, up_in, 1), nxt)
            below = jnp.where(below_at >= 0, pick(here, down_in, 1), prv)
            ready[kb // per, half(h), tile(kb % per)] = 0.5 * (above + below)
    for copy in copies[2:]:
        copy.wait()
    out = [pltpu.make_async_copy(ready.at[b], message.at[b], gone.at[b]) for b in range(message.shape[0])]
    for kb in range(tiles):
        back = jnp.full((ROWS, LANES), directions[kb], jnp.int32) == 1
        slope = []
        for h in range(2):
            v, _, inv = coefficients(velocity, out_rate, kb, h)
            slope.append(v * inv)
        reach, _, _ = scan_tile(back, slope, None)
        parts = [sum(past_residuals[j, half(h), tile(kb)] * reach[h] for h in range(2)) for j in range(HIST)]
        parts.append(sum(reach[h] * reach[h] for h in range(2)))
        parts.append(sum(reach[h] * wigner[half(h), tile(kb)] for h in range(2)))
        rate = jnp.broadcast_to(out_rate[:, tile(kb)], (ROWS, LANES))
        enters = jnp.broadcast_to(inflow[:, tile(kb)], (ROWS, LANES))
        ready[kb // per, 2 * ROWS :, tile(kb % per)] = jnp.where(
            row == 6, rate, jnp.where(row == 7, enters, added_rows(parts))
        )
        if kb % per == per - 1:
            out[kb // per].start()
    known = [directions[n] for n in range(tiles)] + [coupling[n] for n in range(coupling.shape[0])]
    for q in range(len(known) // ROWS):
        rows = jnp.zeros((ROWS, LANES), jnp.int32)
        for n in range(ROWS):
            rows = jnp.where(row == n, known[q * ROWS + n], rows)
        notes[half(q), :] = rows
    for copy in out:
        copy.wait()


def history_kernel(past_residuals, gram):
    tiles = past_residuals.shape[2] // LANES
    acc = [jnp.zeros((ROWS, LANES), jnp.float32) for _ in PAIRS]
    for kb in range(tiles):
        for h in range(2):
            past = [past_residuals[j, half(h), tile(kb)] for j in range(HIST)]
            for n, (i, j) in enumerate(PAIRS):
                acc[n] = acc[n] + past[i] * past[j]
    gram[...] = jnp.zeros(gram.shape, jnp.float32)
    for n in range(len(PAIRS)):
        gram[6 + n : 7 + n, :] = down(acc[n])


def at_contact(blocks, back, slope, inflow):
    row = iota(0)
    place = jnp.full((ROWS, LANES), lax.axis_index(POS), jnp.int32)
    first = (place == 0) & (row == 0) & jnp.logical_not(back)
    final = (place == blocks - 1) & (row == ROWS - 1) & back
    wide = jnp.broadcast_to(inflow, (ROWS, LANES))
    return [jnp.where(first, slope[0] * wide, 0.0), jnp.where(final, slope[1] * wide, 0.0)]


def fold_kernel(notes, held, velocity, message, *refs):
    bands = held.shape[0]
    shares, both, ready, gone = refs[:bands], *refs[bands:]
    blocks = message.shape[0]
    per = held.shape[2] // LANES
    row, lane = iota(0), iota(1)
    band = lax.axis_index(BAND)
    first = blocks
    chosen = [jnp.broadcast_to(notes[first + s : first + s + 1, :], (ROWS, LANES)) for s in range(bands)]
    out = [
        pltpu.make_async_copy(
            ready.at[pl.ds(kt * bands, bands)], message.at[pl.ds(kt * bands, bands)], gone.at[kt]
        )
        for kt in range(per)
    ]
    for kt in range(per):
        kb = band * per + kt
        back = flag(notes, kb)
        columns = pl.ds(pl.multiple_of(kb * LANES, LANES), LANES)
        speeds = [velocity[half(h), columns] for h in range(2)]
        spread = [[held[s, half(h), tile(kt)] for h in range(2)] for s in range(bands)]
        parts = []
        for s in range(bands):
            tail = held[s, 2 * ROWS :, tile(kt)]
            rate = jnp.broadcast_to(tail[6:7], (ROWS, LANES))
            slope, offset = [], []
            for h in range(2):
                partner = spread[0][h]
                for t in range(1, bands):
                    partner = jnp.where(chosen[s] == t, spread[t][h], partner)
                pair = spread[s][h] + partner
                both[s, half(h), tile(kt)] = pair
                inv = 1.0 / (speeds[h] + rate)
                slope.append(speeds[h] * inv)
                offset.append(rate * 0.5 * pair * inv)
            edge = at_contact(blocks, back, slope, tail[7:8])
            offset = [offset[h] + edge[h] for h in range(2)]
            reach, run, ends = scan_tile(back, slope, offset)
            crossed = jnp.broadcast_to(down(reach[0] * run[0] + reach[1] * run[1]), (ROWS, LANES)) - tail
            parts.append(
                jnp.where(row == 5, crossed, jnp.where(row == 6, ends[0], jnp.where(row == 7, ends[1], tail)))
            )
        for bit in range(3):
            step = 1 << bit
            high = ((lane >> (4 + bit)) & 1) == 1
            swapped = list(parts)
            for s in range(bands):
                if not s & step:
                    swapped[s] = jnp.where(high, pltpu.roll(parts[s + step], GROUP * step, 1), parts[s])
                    swapped[s + step] = jnp.where(high, parts[s + step], pltpu.roll(parts[s], LANES - GROUP * step, 1))
            parts = swapped
        for g in range(bands):
            ready[kt * bands + g] = parts[g]
        out[kt].start()
    for d in range(bands):
        shares[d][...] = both[band ^ d]
    for copy in out:
        copy.wait()


def settle_kernel(notes, *refs):
    shares = refs[:8]
    velocity, out_rate, inflow, wigner, past_residuals, early, reach_out, rest, gram = refs[8:]
    per = shares[0].shape[1] // LANES
    blocks = velocity.shape[1] // LANES
    band = lax.axis_index(BAND)
    acc = [jnp.zeros((ROWS, LANES), jnp.float32) for _ in range(HIST + 1)]
    for d in range(len(shares)):
        for kt in range(per):
            kb = (band ^ d) * per + kt
            back = flag(notes, kb)
            columns = pl.ds(pl.multiple_of(kb * LANES, LANES), LANES)
            rate = jnp.broadcast_to(out_rate[:, columns], (ROWS, LANES))
            slope, offset = [], []
            for h in range(2):
                v = velocity[half(h), columns]
                inv = 1.0 / (v + rate)
                slope.append(v * inv)
                offset.append(rate * 0.5 * shares[d][half(h), tile(kt)] * inv)
            edge = at_contact(blocks, back, slope, inflow[:, columns])
            offset = [offset[h] + edge[h] for h in range(2)]
            reach, run, _ = scan_tile(back, slope, offset)
            for h in range(2):
                left = run[h] - wigner[half(h), columns]
                rest[half(h), columns] = left
                reach_out[half(h), columns] = reach[h]
                for j in range(HIST):
                    acc[j] = acc[j] + past_residuals[j, half(h), columns] * left
                acc[HIST] = acc[HIST] + left * left
    gram[half(0), :] = added_rows(acc)
    gram[half(1), :] = early[half(1), :]
    gram[6:8, :] = early[6:8, :]


def carry_kernel(notes, sums, gram, message, forth, counter):
    blocks = sums.shape[0]
    row, lane = iota(0), iota(1)
    back = flag(notes, lax.axis_index(BAND) * (blocks // ROWS) + lax.axis_index(POS) // ROWS)
    acc = jnp.zeros((ROWS, LANES), jnp.float32)
    carry = jnp.zeros((1, LANES), jnp.float32)
    for step in range(blocks):
        part = jnp.where(back, sums[blocks - 1 - step], sums[step])
        wide = jnp.broadcast_to(carry, (ROWS, LANES))
        forth[step : step + 1, :] = carry
        counter[blocks - 1 - step : blocks - step, :] = carry
        acc = acc + part * jnp.where(row == 4, wide * wide, jnp.where(row == 5, 2.0 * wide, wide))
        carry = part[6:7] * carry + part[7:8]
    terms = [gram[half(0), :] + jnp.where(row < 6, acc, 0.0), gram[half(1), :]]
    line = jnp.zeros((ROWS, LANES), jnp.float32)
    for h in range(2):
        whole = jnp.broadcast_to(jnp.sum(terms[h], axis=1, keepdims=True), (ROWS, LANES))
        line = line + jnp.where(lane == GROUP + h * ROWS + row, whole, 0.0)
    line = jnp.broadcast_to(down(line), (ROWS, LANES))
    for q in range(blocks // ROWS):
        carries = jnp.where(back, counter[half(q), :], forth[half(q), :])
        for s in range(LANES // GROUP):
            turned = pltpu.roll(carries, LANES - GROUP * s, 1) if s else carries
            message[s * blocks + q * ROWS : s * blocks + (q + 1) * ROWS, :] = jnp.where(lane < GROUP, turned, line)


def mixing_weights(entry):
    count = HIST + 1
    scale = sum(entry(i, i) for i in range(count)) / count
    factor = {}
    for i in range(count):
        for j in range(i + 1):
            value = entry(j, i)
            if i == j:
                value = value + RIDGE_SCALE * scale
            for k in range(j):
                value = value - factor[i, k] * factor[j, k]
            factor[i, j] = jnp.sqrt(value) if i == j else value / factor[j, j]
    forward = []
    for row in range(count):
        partial = jnp.ones_like(scale)
        for inner in range(row):
            partial = partial - factor[row, inner] * forward[inner]
        forward.append(partial / factor[row, row])
    backward = [None] * count
    for row in reversed(range(count)):
        partial = forward[row]
        for inner in range(row + 1, count):
            partial = partial - factor[inner, row] * backward[inner]
        backward[row] = partial / factor[row, row]
    total = sum(backward)
    return [z / total for z in backward]


def finish_kernel(message, reach, rest, wigner, past_iterates, past_residuals, residual, mixed, found, mixes, gone):
    cells, moments = wigner.shape
    tiles = moments // LANES
    pieces = 4
    row, lane = iota(0), iota(1)
    out = []
    for n, (source, target) in enumerate(((found, residual), (mixes, mixed))):
        for q in range(pieces):
            columns = pl.ds(q * (moments // pieces), moments // pieces)
            out.append(pltpu.make_async_copy(source.at[:, columns], target.at[:, columns], gone.at[n * pieces + q]))
    total = message[half(0), :]
    for kb in range(1, tiles):
        total = total + message[half(kb), :]
    total = jnp.broadcast_to(down(total), (ROWS, LANES))

    def term(n):
        return pick(total, jnp.full((ROWS, LANES), GROUP + n, jnp.int32), 1)

    def entry(i, j):
        if j == HIST:
            return term(4) + term(5) if i == HIST else term(i)
        return term(6 + PAIRS.index((i, j)))

    for kb in range(tiles):
        spots = pick(message[half(kb), :], lane & (GROUP - 1), 1)
        carry = jnp.broadcast_to(down(jnp.where((lane >> 4) == row, spots, 0.0)), (ROWS, LANES))
        for h in range(2):
            found[half(h), tile(kb)] = rest[half(h), tile(kb)] + reach[half(h), tile(kb)] * carry
        if (kb + 1) % (tiles // pieces) == 0:
            out[kb // (tiles // pieces)].start()
    weights = mixing_weights(entry)
    for kb in range(tiles):
        for h in range(2):
            value = weights[HIST] * (wigner[half(h), tile(kb)] + MIX_STEP * found[half(h), tile(kb)])
            for j in range(HIST):
                earlier = past_iterates[j, half(h), tile(kb)] + MIX_STEP * past_residuals[j, half(h), tile(kb)]
                value = value + weights[j] * earlier
            mixes[half(h), tile(kb)] = value
        if (kb + 1) % (tiles // pieces) == 0:
            out[pieces + kb // (tiles // pieces)].start()
    for copy in out:
        copy.wait()


def body(wigner, past_iterates, past_residuals, velocity, out_rate, inflow, offsets, directions, coupling):
    _, cells, moments = wigner.shape
    bands = lax.axis_size(BAND)
    blocks = lax.axis_size(POS)
    wigner = wigner.reshape(cells, moments)
    past_iterates = past_iterates.reshape(HIST, cells, moments)
    past_residuals = past_residuals.reshape(HIST, cells, moments)
    offsets = offsets.reshape(1, moments)
    size = 4 * cells * moments
    share = moments // bands
    field = f32(cells, moments)
    dma = pltpu.SemaphoreType.DMA

    sources = (offsets, wigner, directions, coupling, velocity, out_rate, inflow, past_residuals)
    opened = f32(bands, cells + ROWS, share)
    message, notes = call(
        open_kernel,
        (opened, jax.ShapeDtypeStruct((blocks + bands, LANES), jnp.int32)),
        [HBM] * 8,
        20 * size,
        8 * size,
        [(pltpu.SMEM if x.ndim == 1 else pltpu.VMEM)(x.shape, x.dtype) for x in sources]
        + [pltpu.VMEM(opened.shape, jnp.float32), dma((8,)), dma((bands,))],
        60,
        (HBM, VMEM),
    )(*sources)
    held = lax.all_to_all(message, BAND, 0, 0, tiled=True)
    early = call(history_kernel, f32(16, LANES), [VMEM], 8 * size, 4 * size)(past_residuals)
    held, early = lax.optimization_barrier((held, early))
    sums, *shares = call(
        fold_kernel,
        (f32(blocks, ROWS, LANES),) + (f32(cells, share),) * bands,
        [VMEM] * 3,
        20 * size,
        5 * size,
        [pltpu.VMEM((bands, cells, share), jnp.float32), pltpu.VMEM((blocks, ROWS, LANES), jnp.float32), dma((4,))],
        out_specs=(HBM,) + (VMEM,) * bands,
    )(notes, held, velocity)
    sums = lax.all_to_all(sums, POS, 0, 0, tiled=True)
    shares = [shares[0]] + [
        lax.ppermute(shares[d], BAND, [(i, i ^ d) for i in range(bands)]) for d in range(1, bands)
    ]
    reach, rest, gram = call(
        settle_kernel, (field, field, f32(16, LANES)), [VMEM] * 15, 20 * size, 10 * size
    )(notes, *shares, velocity, out_rate, inflow, wigner, past_residuals, early)
    message = call(
        carry_kernel,
        f32(bands * blocks, LANES),
        [VMEM] * 3,
        size,
        size,
        [pltpu.VMEM((blocks, LANES), jnp.float32)] * 2,
    )(notes, sums, gram)
    message = lax.all_to_all(message, ALL, 0, 0, tiled=True)
    residual, mixed = call(
        finish_kernel,
        (field, field),
        [VMEM] * 6,
        8 * size,
        14 * size,
        [pltpu.VMEM((cells, moments), jnp.float32)] * 2 + [dma((8,))],
        out_specs=(HBM, HBM),
    )(message, reach, rest, wigner, past_iterates, past_residuals)
    return mixed[None], residual[None]


def solution(mesh):
    finer = Mesh(mesh.devices.reshape(4, 2, 4, 8), ("band_0", "band_1", "pos_0", "pos_1"))
    in_specs = (
        P(BAND, POS, None),
        P(None, BAND, POS, None),
        P(None, BAND, POS, None),
        P(POS, None),
        P(BAND, None),
        P(BAND, None),
        P(),
        P(),
        P(),
    )
    out_specs = (P(BAND, POS, None), P(BAND, POS, None))
    return jax.shard_map(body, mesh=finer, in_specs=in_specs, out_specs=out_specs, check_vma=False)
```

```python
import functools

import jax
import jax.numpy as jnp
from jax import lax
from jax.experimental import pallas as pl
from jax.experimental.pallas import tpu as pltpu
from jax.sharding import Mesh
from jax.sharding import PartitionSpec as P

POS = ("pos_0", "pos_1")
BAND = ("band_0", "band_1")
ALL = BAND + POS

MIX_STEP = 0.5
RIDGE_SCALE = 0.0001
LANES = 128
GROUP = 16
ROWS = 8
HIST = 4
PAIRS = [(i, j) for i in range(HIST) for j in range(i, HIST)]

VMEM = pl.BlockSpec(memory_space=pltpu.VMEM)
HBM = pl.BlockSpec(memory_space=pltpu.HBM)


def call(kernel, outs, in_specs, flops, nbytes, scratch=(), mib=24, out_specs=None):
    return pl.pallas_call(
        kernel,
        out_shape=outs,
        in_specs=in_specs,
        out_specs=jax.tree.map(lambda _: VMEM, outs) if out_specs is None else out_specs,
        scratch_shapes=list(scratch),
        compiler_params=pltpu.CompilerParams(vmem_limit_bytes=mib * 2**20),
        cost_estimate=pl.CostEstimate(flops=flops, bytes_accessed=nbytes, transcendentals=0),
    )


def f32(*shape):
    return jax.ShapeDtypeStruct(shape, jnp.float32)


def tile(kb):
    return slice(kb * LANES, (kb + 1) * LANES)


def pick(x, index, axis):
    return jnp.take_along_axis(x, index, axis=axis, mode="promise_in_bounds")


def iota(axis):
    return lax.broadcasted_iota(jnp.int32, (ROWS, LANES), axis)


def scan_tile(back, a, b):
    row = iota(0)
    away = jnp.where(back, ROWS - 1 - row, row)
    a = [jnp.where(back, a[1], a[0]), jnp.where(back, a[0], a[1])]
    if b is not None:
        b = [jnp.where(back, b[1], b[0]), jnp.where(back, b[0], b[1])]
    for d in (1, 2, 4):
        source = jnp.where(back, row + d, row - d) & (ROWS - 1)
        keep = away >= d
        for h in range(2):
            if b is not None:
                b[h] = a[h] * jnp.where(keep, pick(b[h], source, 0), 0.0) + b[h]
            a[h] = a[h] * jnp.where(keep, pick(a[h], source, 0), 1.0)
    last = jnp.where(back, 0, ROWS - 1) + jnp.zeros_like(row)
    if b is not None:
        b[1] = a[1] * pick(b[0], last, 0) + b[1]
    a[1] = a[1] * pick(a[0], last, 0)
    ends = [pick(a[1], last, 0)]
    if b is not None:
        ends.append(pick(b[1], last, 0))
        b = [jnp.where(back, b[1], b[0]), jnp.where(back, b[0], b[1])]
    a = [jnp.where(back, a[1], a[0]), jnp.where(back, a[0], a[1])]
    return a, b, ends


def coefficients(velocity, out_rate, kb, h):
    v = velocity[h * ROWS : (h + 1) * ROWS, tile(kb)]
    r = jnp.broadcast_to(out_rate[:, tile(kb)], (ROWS, LANES))
    return v, r, 1.0 / (v + r)


def flag(notes, index):
    return jnp.broadcast_to(notes[pl.ds(index, 1), :], (ROWS, LANES)) == 1


def down(x):
    return jnp.sum(x, axis=0, keepdims=True)


def half(h):
    return slice(h * ROWS, (h + 1) * ROWS)


def added_rows(parts):
    row = iota(0)
    parts = parts + [jnp.zeros((ROWS, LANES), jnp.float32)] * (ROWS - len(parts))
    for d in (4, 2, 1):
        low = (row & d) == 0
        count = len(parts) // 2
        parts = [
            jnp.where(low, parts[n], parts[n + count])
            + pick(jnp.where(low, parts[n + count], parts[n]), row ^ d, 0)
            for n in range(count)
        ]
    return parts[0]


def open_kernel(*refs):
    sources, message, notes, held, ready, arrived, gone = refs[:8], refs[8], refs[9], refs[10:18], *refs[18:]
    copies = [pltpu.make_async_copy(a, b, arrived.at[n]) for n, (a, b) in enumerate(zip(sources, held))]
    for copy in copies:
        copy.start()
    offsets, wigner, directions, coupling, velocity, out_rate, inflow, past_residuals = held
    tiles = wigner.shape[1] // LANES
    per = message.shape[2] // LANES
    row, lane = iota(0), iota(1)
    zero = jnp.zeros((ROWS, LANES), jnp.float32)
    copies[0].wait()
    copies[1].wait()
    for kb in range(tiles):
        off = jnp.broadcast_to(offsets[:, tile(kb)], (ROWS, LANES))
        up, below_at = lane + off, lane - off
        up_in, down_in = up & (LANES - 1), below_at & (LANES - 1)
        for h in range(2):
            here = wigner[half(h), tile(kb)]
            nxt = pick(wigner[half(h), tile(kb + 1)], up_in, 1) if kb + 1 < tiles else zero
            prv = pick(wigner[half(h), tile(kb - 1)], down_in, 1) if kb else zero
            above = jnp.where(up < LANES, pick(here, up_in, 1), nxt)
            below = jnp.where(below_at >= 0, pick(here, down_in, 1), prv)
            ready[kb // per, half(h), tile(kb % per)] = 0.5 * (above + below)
    for copy in copies[2:]:
        copy.wait()
    out = [pltpu.make_async_copy(ready.at[b], message.at[b], gone.at[b]) for b in range(message.shape[0])]
    for kb in range(tiles):
        back = jnp.full((ROWS, LANES), directions[kb], jnp.int32) == 1
        slope = []
        for h in range(2):
            v, _, inv = coefficients(velocity, out_rate, kb, h)
            slope.append(v * inv)
        reach, _, _ = scan_tile(back, slope, None)
        parts = [sum(past_residuals[j, half(h), tile(kb)] * reach[h] for h in range(2)) for j in range(HIST)]
        parts.append(sum(reach[h] * reach[h] for h in range(2)))
        parts.append(sum(reach[h] * wigner[half(h), tile(kb)] for h in range(2)))
        rate = jnp.broadcast_to(out_rate[:, tile(kb)], (ROWS, LANES))
        enters = jnp.broadcast_to(inflow[:, tile(kb)], (ROWS, LANES))
        ready[kb // per, 2 * ROWS :, tile(kb % per)] = jnp.where(
            row == 6, rate, jnp.where(row == 7, enters, added_rows(parts))
        )
        if kb % per == per - 1:
            out[kb // per].start()
    known = [directions[n] for n in range(tiles)] + [coupling[n] for n in range(coupling.shape[0])]
    for q in range(len(known) // ROWS):
        rows = jnp.zeros((ROWS, LANES), jnp.int32)
        for n in range(ROWS):
            rows = jnp.where(row == n, known[q * ROWS + n], rows)
        notes[half(q), :] = rows
    for copy in out:
        copy.wait()


def history_kernel(past_residuals, gram):
    tiles = past_residuals.shape[2] // LANES
    acc = [jnp.zeros((ROWS, LANES), jnp.float32) for _ in PAIRS]
    for kb in range(tiles):
        for h in range(2):
            past = [past_residuals[j, half(h), tile(kb)] for j in range(HIST)]
            for n, (i, j) in enumerate(PAIRS):
                acc[n] = acc[n] + past[i] * past[j]
    gram[...] = jnp.zeros(gram.shape, jnp.float32)
    for n in range(len(PAIRS)):
        gram[6 + n : 7 + n, :] = down(acc[n])


def at_contact(blocks, back, slope, inflow):
    row = iota(0)
    place = jnp.full((ROWS, LANES), lax.axis_index(POS), jnp.int32)
    first = (place == 0) & (row == 0) & jnp.logical_not(back)
    final = (place == blocks - 1) & (row == ROWS - 1) & back
    wide = jnp.broadcast_to(inflow, (ROWS, LANES))
    return [jnp.where(first, slope[0] * wide, 0.0), jnp.where(final, slope[1] * wide, 0.0)]


def fold_kernel(notes, held, velocity, message, *refs):
    bands = held.shape[0]
    own, other, both, ready, gone = refs
    blocks = message.shape[0]
    per = held.shape[2] // LANES
    row, lane = iota(0), iota(1)
    band = lax.axis_index(BAND)
    first = blocks
    chosen = [jnp.broadcast_to(notes[first + s : first + s + 1, :], (ROWS, LANES)) for s in range(bands)]
    out = [
        pltpu.make_async_copy(
            ready.at[pl.ds(kt * bands, bands)], message.at[pl.ds(kt * bands, bands)], gone.at[kt]
        )
        for kt in range(per)
    ]
    for kt in range(per):
        kb = band * per + kt
        back = flag(notes, kb)
        columns = pl.ds(pl.multiple_of(kb * LANES, LANES), LANES)
        speeds = [velocity[half(h), columns] for h in range(2)]
        spread = [[held[s, half(h), tile(kt)] for h in range(2)] for s in range(bands)]
        parts = []
        for s in range(bands):
            tail = held[s, 2 * ROWS :, tile(kt)]
            rate = jnp.broadcast_to(tail[6:7], (ROWS, LANES))
            slope, offset = [], []
            for h in range(2):
                partner = spread[0][h]
                for t in range(1, bands):
                    partner = jnp.where(chosen[s] == t, spread[t][h], partner)
                pair = spread[s][h] + partner
                both[s, half(h), tile(kt)] = pair
                inv = 1.0 / (speeds[h] + rate)
                slope.append(speeds[h] * inv)
                offset.append(rate * 0.5 * pair * inv)
            edge = at_contact(blocks, back, slope, tail[7:8])
            offset = [offset[h] + edge[h] for h in range(2)]
            reach, run, ends = scan_tile(back, slope, offset)
            crossed = jnp.broadcast_to(down(reach[0] * run[0] + reach[1] * run[1]), (ROWS, LANES)) - tail
            parts.append(
                jnp.where(row == 5, crossed, jnp.where(row == 6, ends[0], jnp.where(row == 7, ends[1], tail)))
            )
        for bit in range(3):
            step = 1 << bit
            high = ((lane >> (4 + bit)) & 1) == 1
            swapped = list(parts)
            for s in range(bands):
                if not s & step:
                    swapped[s] = jnp.where(high, pltpu.roll(parts[s + step], GROUP * step, 1), parts[s])
                    swapped[s + step] = jnp.where(high, parts[s + step], pltpu.roll(parts[s], LANES - GROUP * step, 1))
            parts = swapped
        for g in range(bands):
            ready[kt * bands + g] = parts[g]
        out[kt].start()
    for d in range(bands // 2):
        own[d] = both[band ^ (2 * d)]
        other[d] = both[band ^ (2 * d + 1)]
    for copy in out:
        copy.wait()


def settle_kernel(notes, *refs):
    shares = refs[:-9]
    velocity, out_rate, inflow, wigner, past_residuals, early, reach_out, rest, gram = refs[-9:]
    per = rest.shape[2] // LANES
    blocks = velocity.shape[1] // LANES
    band = lax.axis_index(BAND)
    acc = [jnp.zeros((ROWS, LANES), jnp.float32) for _ in range(HIST + 1)]
    for d in range(2 * len(shares)):
        for kt in range(per):
            kb = (band ^ d) * per + kt
            back = flag(notes, kb)
            columns = pl.ds(pl.multiple_of(kb * LANES, LANES), LANES)
            rate = jnp.broadcast_to(out_rate[:, columns], (ROWS, LANES))
            slope, offset = [], []
            for h in range(2):
                v = velocity[half(h), columns]
                inv = 1.0 / (v + rate)
                slope.append(v * inv)
                offset.append(rate * 0.5 * shares[d // 2][d % 2, half(h), tile(kt)] * inv)
            edge = at_contact(blocks, back, slope, inflow[:, columns])
            offset = [offset[h] + edge[h] for h in range(2)]
            reach, run, _ = scan_tile(back, slope, offset)
            for h in range(2):
                left = run[h] - wigner[half(h), columns]
                rest[d, half(h), tile(kt)] = left
                reach_out[d, half(h), tile(kt)] = reach[h]
                for j in range(HIST):
                    acc[j] = acc[j] + past_residuals[j, half(h), columns] * left
                acc[HIST] = acc[HIST] + left * left
    gram[half(0), :] = early[half(0), :] + added_rows(acc)
    gram[half(1), :] = early[half(1), :]


def carry_kernel(notes, sums, carries, terms, forth, counter):
    blocks = sums.shape[0]
    row = iota(0)
    back = flag(notes, lax.axis_index(BAND) * (blocks // ROWS) + lax.axis_index(POS) // ROWS)
    acc = jnp.zeros((ROWS, LANES), jnp.float32)
    carry = jnp.zeros((1, LANES), jnp.float32)
    for step in range(blocks):
        part = jnp.where(back, sums[blocks - 1 - step], sums[step])
        wide = jnp.broadcast_to(carry, (ROWS, LANES))
        forth[step : step + 1, :] = carry
        counter[blocks - 1 - step : blocks - step, :] = carry
        acc = acc + part * jnp.where(row == 4, wide * wide, jnp.where(row == 5, 2.0 * wide, wide))
        carry = part[6:7] * carry + part[7:8]
    for q in range(blocks // ROWS):
        carries[half(q), :] = jnp.where(back, counter[half(q), :], forth[half(q), :])
    terms[...] = jnp.where(row < 6, acc, 0.0)


def message_kernel(carries, terms, gram, message):
    blocks = carries.shape[0]
    row, lane = iota(0), iota(1)
    whole = [gram[half(0), :] + terms[...], gram[half(1), :]]
    line = jnp.zeros((ROWS, LANES), jnp.float32)
    for h in range(2):
        total = jnp.broadcast_to(jnp.sum(whole[h], axis=1, keepdims=True), (ROWS, LANES))
        line = line + jnp.where(lane == GROUP + h * ROWS + row, total, 0.0)
    line = jnp.broadcast_to(down(line), (ROWS, LANES))
    for q in range(blocks // ROWS):
        for s in range(LANES // GROUP):
            turned = pltpu.roll(carries[half(q), :], LANES - GROUP * s, 1) if s else carries[half(q), :]
            message[s * blocks + q * ROWS : s * blocks + (q + 1) * ROWS, :] = jnp.where(lane < GROUP, turned, line)


def mixing_weights(entry):
    count = HIST + 1
    scale = sum(entry(i, i) for i in range(count)) / count
    factor = {}
    for i in range(count):
        for j in range(i + 1):
            value = entry(j, i)
            if i == j:
                value = value + RIDGE_SCALE * scale
            for k in range(j):
                value = value - factor[i, k] * factor[j, k]
            factor[i, j] = jnp.sqrt(value) if i == j else value / factor[j, j]
    forward = []
    for row in range(count):
        partial = jnp.ones_like(scale)
        for inner in range(row):
            partial = partial - factor[row, inner] * forward[inner]
        forward.append(partial / factor[row, row])
    backward = [None] * count
    for row in reversed(range(count)):
        partial = forward[row]
        for inner in range(row + 1, count):
            partial = partial - factor[inner, row] * backward[inner]
        backward[row] = partial / factor[row, row]
    total = sum(backward)
    return [z / total for z in backward]


def finish_kernel(message, *refs):
    reach, rest, wigner, past_iterates, past_residuals, residual, mixed, found, mixes, gone = refs
    cells, moments = wigner.shape
    bands, _, share = rest.shape
    per = share // LANES
    band = lax.axis_index(BAND)
    tiles = moments // LANES
    pieces = 4
    row, lane = iota(0), iota(1)
    out = []
    for n, (source, target) in enumerate(((found, residual), (mixes, mixed))):
        for q in range(pieces):
            columns = pl.ds(q * (moments // pieces), moments // pieces)
            out.append(pltpu.make_async_copy(source.at[:, columns], target.at[:, columns], gone.at[n * pieces + q]))
    total = message[half(0), :]
    for kb in range(1, tiles):
        total = total + message[half(kb), :]
    total = jnp.broadcast_to(down(total), (ROWS, LANES))

    def term(n):
        return pick(total, jnp.full((ROWS, LANES), GROUP + n, jnp.int32), 1)

    def entry(i, j):
        if j == HIST:
            return term(4) + term(5) if i == HIST else term(i)
        return term(6 + PAIRS.index((i, j)))

    for d in range(bands):
        for kt in range(per):
            kb = (band ^ d) * per + kt
            rows = message[pl.ds(pl.multiple_of(kb * ROWS, ROWS), ROWS), :]
            spots = pick(rows, lane & (GROUP - 1), 1)
            carry = jnp.broadcast_to(down(jnp.where((lane >> 4) == row, spots, 0.0)), (ROWS, LANES))
            for h in range(2):
                at = (d, half(h), tile(kt))
                found[half(h), pl.ds(pl.multiple_of(kb * LANES, LANES), LANES)] = rest[at] + reach[at] * carry
    for copy in out[:pieces]:
        copy.start()
    weights = mixing_weights(entry)
    for kb in range(tiles):
        for h in range(2):
            value = weights[HIST] * (wigner[half(h), tile(kb)] + MIX_STEP * found[half(h), tile(kb)])
            for j in range(HIST):
                earlier = past_iterates[j, half(h), tile(kb)] + MIX_STEP * past_residuals[j, half(h), tile(kb)]
                value = value + weights[j] * earlier
            mixes[half(h), tile(kb)] = value
        if (kb + 1) % (tiles // pieces) == 0:
            out[pieces + kb // (tiles // pieces)].start()
    for copy in out:
        copy.wait()


def body(wigner, past_iterates, past_residuals, velocity, out_rate, inflow, offsets, directions, coupling):
    _, cells, moments = wigner.shape
    bands = lax.axis_size(BAND)
    blocks = lax.axis_size(POS)
    wigner = wigner.reshape(cells, moments)
    past_iterates = past_iterates.reshape(HIST, cells, moments)
    past_residuals = past_residuals.reshape(HIST, cells, moments)
    offsets = offsets.reshape(1, moments)
    size = 4 * cells * moments
    share = moments // bands
    field = f32(cells, moments)
    dma = pltpu.SemaphoreType.DMA

    sources = (offsets, wigner, directions, coupling, velocity, out_rate, inflow, past_residuals)
    opened = f32(bands, cells + ROWS, share)
    message, notes = call(
        open_kernel,
        (opened, jax.ShapeDtypeStruct((blocks + bands, LANES), jnp.int32)),
        [HBM] * 8,
        20 * size,
        8 * size,
        [(pltpu.SMEM if x.ndim == 1 else pltpu.VMEM)(x.shape, x.dtype) for x in sources]
        + [pltpu.VMEM(opened.shape, jnp.float32), dma((8,)), dma((bands,))],
        60,
        (HBM, VMEM),
    )(*sources)
    held = lax.all_to_all(message, BAND, 0, 0, tiled=True)
    early = call(history_kernel, f32(16, LANES), [VMEM], 8 * size, 4 * size)(past_residuals)
    held, early = lax.optimization_barrier((held, early))
    chips = lax.axis_size(BAND[0])
    part = f32(chips, cells, share)
    sums, own, other = call(
        fold_kernel,
        (f32(blocks, ROWS, LANES), part, part),
        [VMEM] * 3,
        20 * size,
        5 * size,
        [pltpu.VMEM((bands, cells, share), jnp.float32), pltpu.VMEM((blocks, ROWS, LANES), jnp.float32), dma((4,))],
        out_specs=(HBM, VMEM, VMEM),
    )(notes, held, velocity)
    sums = lax.all_to_all(sums, POS, 0, 0, tiled=True)
    other = lax.ppermute(other, BAND[1], [(0, 1), (1, 0)])
    across = [jnp.stack([own[d], other[d]]) for d in range(chips)]
    across = across[:1] + [
        lax.ppermute(across[d], BAND[0], [(i, i ^ d) for i in range(chips)]) for d in range(1, chips)
    ]
    local = (velocity, out_rate, inflow, wigner, past_residuals)
    reach, rest, gram = call(
        settle_kernel,
        (f32(bands, cells, share), f32(bands, cells, share), f32(16, LANES)),
        [VMEM] * (chips + 7),
        size,
        size,
    )(notes, *across, *local, early)
    carries, terms = call(
        carry_kernel,
        (f32(blocks, LANES), f32(ROWS, LANES)),
        [VMEM] * 2,
        size,
        256 * size,
        [pltpu.VMEM((blocks, LANES), jnp.float32)] * 2,
    )(notes, sums)
    message = call(message_kernel, f32(bands * blocks, LANES), [VMEM] * 3, size, size)(carries, terms, gram)
    message = lax.all_to_all(message, ALL, 0, 0, tiled=True)
    residual, mixed = call(
        finish_kernel,
        (field, field),
        [VMEM] * 6,
        8 * size,
        14 * size,
        [pltpu.VMEM((cells, moments), jnp.float32)] * 2 + [dma((8,))],
        out_specs=(HBM, HBM),
    )(message, reach, rest, wigner, past_iterates, past_residuals)
    return mixed[None], residual[None]


def solution(mesh):
    finer = Mesh(mesh.devices.reshape(4, 2, 4, 8), ("band_0", "band_1", "pos_0", "pos_1"))
    in_specs = (
        P(BAND, POS, None),
        P(None, BAND, POS, None),
        P(None, BAND, POS, None),
        P(POS, None),
        P(BAND, None),
        P(BAND, None),
        P(),
        P(),
        P(),
    )
    out_specs = (P(BAND, POS, None), P(BAND, POS, None))
    return jax.shard_map(body, mesh=finer, in_specs=in_specs, out_specs=out_specs, check_vma=False)
```

```python
import functools

import jax
import jax.numpy as jnp
from jax import lax
from jax.experimental import pallas as pl
from jax.experimental.pallas import tpu as pltpu
from jax.sharding import Mesh
from jax.sharding import PartitionSpec as P

POS = ("pos_0", "pos_1")
BAND = ("band_0", "band_1")
ALL = BAND + POS

MIX_STEP = 0.5
RIDGE_SCALE = 0.0001
LANES = 128
GROUP = 16
ROWS = 8
HIST = 4
PAIRS = [(i, j) for i in range(HIST) for j in range(i, HIST)]

VMEM = pl.BlockSpec(memory_space=pltpu.VMEM)
HBM = pl.BlockSpec(memory_space=pltpu.HBM)


def call(kernel, outs, in_specs, flops, nbytes, scratch=(), mib=24, out_specs=None):
    return pl.pallas_call(
        kernel,
        out_shape=outs,
        in_specs=in_specs,
        out_specs=jax.tree.map(lambda _: VMEM, outs) if out_specs is None else out_specs,
        scratch_shapes=list(scratch),
        compiler_params=pltpu.CompilerParams(vmem_limit_bytes=mib * 2**20),
        cost_estimate=pl.CostEstimate(flops=flops, bytes_accessed=nbytes, transcendentals=0),
    )


def f32(*shape):
    return jax.ShapeDtypeStruct(shape, jnp.float32)


def tile(kb):
    return slice(kb * LANES, (kb + 1) * LANES)


def pick(x, index, axis):
    return jnp.take_along_axis(x, index, axis=axis, mode="promise_in_bounds")


def iota(axis):
    return lax.broadcasted_iota(jnp.int32, (ROWS, LANES), axis)


def scan_tile(back, a, b):
    row = iota(0)
    away = jnp.where(back, ROWS - 1 - row, row)
    a = [jnp.where(back, a[1], a[0]), jnp.where(back, a[0], a[1])]
    if b is not None:
        b = [jnp.where(back, b[1], b[0]), jnp.where(back, b[0], b[1])]
    for d in (1, 2, 4):
        source = jnp.where(back, row + d, row - d) & (ROWS - 1)
        keep = away >= d
        for h in range(2):
            if b is not None:
                b[h] = a[h] * jnp.where(keep, pick(b[h], source, 0), 0.0) + b[h]
            a[h] = a[h] * jnp.where(keep, pick(a[h], source, 0), 1.0)
    last = jnp.where(back, 0, ROWS - 1) + jnp.zeros_like(row)
    if b is not None:
        b[1] = a[1] * pick(b[0], last, 0) + b[1]
    a[1] = a[1] * pick(a[0], last, 0)
    ends = [pick(a[1], last, 0)]
    if b is not None:
        ends.append(pick(b[1], last, 0))
        b = [jnp.where(back, b[1], b[0]), jnp.where(back, b[0], b[1])]
    a = [jnp.where(back, a[1], a[0]), jnp.where(back, a[0], a[1])]
    return a, b, ends


def flag(notes, index):
    return jnp.broadcast_to(notes[pl.ds(index, 1), :], (ROWS, LANES)) == 1


def down(x):
    return jnp.sum(x, axis=0, keepdims=True)


def half(h):
    return slice(h * ROWS, (h + 1) * ROWS)


def added_rows(parts):
    row = iota(0)
    parts = parts + [jnp.zeros((ROWS, LANES), jnp.float32)] * (ROWS - len(parts))
    for d in (4, 2, 1):
        low = (row & d) == 0
        count = len(parts) // 2
        parts = [
            jnp.where(low, parts[n], parts[n + count])
            + pick(jnp.where(low, parts[n + count], parts[n]), row ^ d, 0)
            for n in range(count)
        ]
    return parts[0]


def columns_of(kb):
    return pl.ds(pl.multiple_of(kb * LANES, LANES), LANES)


def open_kernel(*refs):
    sources, own, other, notes, held, arrived = refs[:8], refs[8], refs[9], refs[10], refs[11:19], refs[19]
    offsets, padded, directions, coupling, velocity, out_rate, inflow, past_residuals = held
    moments = offsets.shape[1]
    tiles = moments // LANES
    chips, _, share = own.shape
    per = share // LANES
    places = [padded.at[:, pl.ds(LANES, moments)] if ref is padded else ref for ref in held]
    copies = [pltpu.make_async_copy(a, b, arrived.at[n]) for n, (a, b) in enumerate(zip(sources, places))]
    for copy in copies:
        copy.start()
    band = lax.axis_index(BAND)
    row, lane = iota(0), iota(1)
    for kb in (0, tiles + 1):
        padded[:, tile(kb)] = jnp.zeros((2 * ROWS, LANES), jnp.float32)
    spots = [
        (target, d, t, (band ^ (2 * d + core)) * per + t)
        for core, target in ((1, other), (0, own))
        for d in range(chips)
        for t in range(per)
    ]
    copies[0].wait()
    copies[1].wait()
    for target, d, t, kb in spots:
        off = jnp.broadcast_to(offsets[:, columns_of(kb)], (ROWS, LANES))
        up, low = lane + off, lane - off
        up_in, low_in = up & (LANES - 1), low & (LANES - 1)
        for h in range(2):
            prv, here, nxt = [padded[half(h), columns_of(kb + n)] for n in range(3)]
            above = jnp.where(up < LANES, pick(here, up_in, 1), pick(nxt, up_in, 1))
            below = jnp.where(low >= 0, pick(here, low_in, 1), pick(prv, low_in, 1))
            target[d, half(h), tile(t)] = 0.5 * (above + below)
    for copy in copies[2:]:
        copy.wait()
    for target, d, t, kb in spots:
        back = jnp.full((ROWS, LANES), directions[kb], jnp.int32) == 1
        rate = jnp.broadcast_to(out_rate[:, columns_of(kb)], (ROWS, LANES))
        enters = jnp.broadcast_to(inflow[:, columns_of(kb)], (ROWS, LANES))
        speeds = [velocity[half(h), columns_of(kb)] for h in range(2)]
        reach, _, _ = scan_tile(back, [v * (1.0 / (v + rate)) for v in speeds], None)
        parts = [sum(past_residuals[j, half(h), columns_of(kb)] * reach[h] for h in range(2)) for j in range(HIST)]
        parts.append(sum(reach[h] * reach[h] for h in range(2)))
        parts.append(sum(reach[h] * padded[half(h), columns_of(kb + 1)] for h in range(2)))
        target[d, 2 * ROWS :, tile(t)] = jnp.where(row == 6, rate, jnp.where(row == 7, enters, added_rows(parts)))
    known = [directions[n] for n in range(tiles)] + [coupling[n] for n in range(coupling.shape[0])]
    for q in range(len(known) // ROWS):
        rows = jnp.zeros((ROWS, LANES), jnp.int32)
        for n in range(ROWS):
            rows = jnp.where(row == n, known[q * ROWS + n], rows)
        notes[half(q), :] = rows


def history_kernel(past_residuals, gram):
    tiles = past_residuals.shape[2] // LANES
    acc = [jnp.zeros((ROWS, LANES), jnp.float32) for _ in PAIRS]
    for kb in range(tiles):
        for h in range(2):
            past = [past_residuals[j, half(h), tile(kb)] for j in range(HIST)]
            for n, (i, j) in enumerate(PAIRS):
                acc[n] = acc[n] + past[i] * past[j]
    gram[...] = jnp.zeros(gram.shape, jnp.float32)
    for n in range(len(PAIRS)):
        gram[6 + n : 7 + n, :] = down(acc[n])


def at_contact(blocks, back, slope, inflow):
    row = iota(0)
    place = jnp.full((ROWS, LANES), lax.axis_index(POS), jnp.int32)
    first = (place == 0) & (row == 0) & jnp.logical_not(back)
    final = (place == blocks - 1) & (row == ROWS - 1) & back
    wide = jnp.broadcast_to(inflow, (ROWS, LANES))
    return [jnp.where(first, slope[0] * wide, 0.0), jnp.where(final, slope[1] * wide, 0.0)]


def fold_kernel(notes, velocity, *refs):
    chips = (len(refs) - 4) // 2
    held, message, own, other, across = refs[:chips], *refs[chips : chips + 3], refs[chips + 3 : -2]
    ready, gone = refs[-2:]
    bands = 2 * chips
    blocks = message.shape[0]
    per = own.shape[1] // LANES
    row, lane = iota(0), iota(1)
    band = lax.axis_index(BAND)
    chosen = [
        jnp.broadcast_to(notes[pl.ds(blocks + (band ^ u), 1), :], (ROWS, LANES)) ^ jnp.full((ROWS, LANES), band, jnp.int32)
        for u in range(bands)
    ]
    out = [
        pltpu.make_async_copy(
            ready.at[pl.ds(kt * bands, bands)], message.at[pl.ds(kt * bands, bands)], gone.at[kt]
        )
        for kt in range(per)
    ]
    for kt in range(per):
        kb = band * per + kt
        back = flag(notes, kb)
        speeds = [velocity[half(h), columns_of(kb)] for h in range(2)]
        spread = [[held[u // 2][u % 2, half(h), tile(kt)] for h in range(2)] for u in range(bands)]
        parts = []
        for u in range(bands):
            tail = held[u // 2][u % 2, 2 * ROWS :, tile(kt)]
            rate = jnp.broadcast_to(tail[6:7], (ROWS, LANES))
            slope, offset = [], []
            for h in range(2):
                partner = spread[0][h]
                for t in range(1, bands):
                    partner = jnp.where(chosen[u] == t, spread[t][h], partner)
                pair = spread[u][h] + partner
                if u < 2:
                    (other if u else own)[half(h), tile(kt)] = pair
                else:
                    across[u // 2 - 1][u % 2, half(h), tile(kt)] = pair
                inv = 1.0 / (speeds[h] + rate)
                slope.append(speeds[h] * inv)
                offset.append(rate * 0.5 * pair * inv)
            edge = at_contact(blocks, back, slope, tail[7:8])
            offset = [offset[h] + edge[h] for h in range(2)]
            reach, run, ends = scan_tile(back, slope, offset)
            crossed = jnp.broadcast_to(down(reach[0] * run[0] + reach[1] * run[1]), (ROWS, LANES)) - tail
            parts.append(
                jnp.where(row == 5, crossed, jnp.where(row == 6, ends[0], jnp.where(row == 7, ends[1], tail)))
            )
        for bit in range(3):
            step = 1 << bit
            high = ((lane >> (4 + bit)) & 1) == 1
            swapped = list(parts)
            for u in range(bands):
                if not u & step:
                    swapped[u] = jnp.where(high, pltpu.roll(parts[u + step], GROUP * step, 1), parts[u])
                    swapped[u + step] = jnp.where(high, parts[u + step], pltpu.roll(parts[u], LANES - GROUP * step, 1))
            parts = swapped
        for g in range(bands):
            ready[kt * bands + g] = parts[g]
        out[kt].start()
    for copy in out:
        copy.wait()


def settle_kernel(flip, notes, *refs):
    shares = refs[:-9]
    velocity, out_rate, inflow, wigner, past_residuals, early, reach_out, rest, gram = refs[-9:]
    shares = shares if len(shares) > 1 else [shares[0].at[d] for d in range(shares[0].shape[0])]
    shares = [share if len(share.shape) == 2 else share.at[0] for share in shares]
    per = rest.shape[2] // LANES
    blocks = velocity.shape[1] // LANES
    band = lax.axis_index(BAND)
    acc = [jnp.zeros((ROWS, LANES), jnp.float32) for _ in range(HIST + 1)]
    for d in range(len(shares)):
        for kt in range(per):
            kb = (band ^ (2 * d + flip)) * per + kt
            back = flag(notes, kb)
            columns = pl.ds(pl.multiple_of(kb * LANES, LANES), LANES)
            rate = jnp.broadcast_to(out_rate[:, columns], (ROWS, LANES))
            slope, offset = [], []
            for h in range(2):
                v = velocity[half(h), columns]
                inv = 1.0 / (v + rate)
                slope.append(v * inv)
                offset.append(rate * 0.5 * shares[d][half(h), tile(kt)] * inv)
            edge = at_contact(blocks, back, slope, inflow[:, columns])
            offset = [offset[h] + edge[h] for h in range(2)]
            reach, run, _ = scan_tile(back, slope, offset)
            for h in range(2):
                left = run[h] - wigner[half(h), columns]
                rest[d, half(h), tile(kt)] = left
                reach_out[d, half(h), tile(kt)] = reach[h]
                for j in range(HIST):
                    acc[j] = acc[j] + past_residuals[j, half(h), columns] * left
                acc[HIST] = acc[HIST] + left * left
    gram[half(0), :] = early[half(0), :] + added_rows(acc)
    gram[half(1), :] = early[half(1), :]


def carry_kernel(notes, sums, carries, terms, forth, counter):
    blocks = sums.shape[0]
    row = iota(0)
    back = flag(notes, lax.axis_index(BAND) * (blocks // ROWS) + lax.axis_index(POS) // ROWS)
    acc = jnp.zeros((ROWS, LANES), jnp.float32)
    carry = jnp.zeros((1, LANES), jnp.float32)
    for step in range(blocks):
        part = jnp.where(back, sums[blocks - 1 - step], sums[step])
        wide = jnp.broadcast_to(carry, (ROWS, LANES))
        forth[step : step + 1, :] = carry
        counter[blocks - 1 - step : blocks - step, :] = carry
        acc = acc + part * jnp.where(row == 4, wide * wide, jnp.where(row == 5, 2.0 * wide, wide))
        carry = part[6:7] * carry + part[7:8]
    for q in range(blocks // ROWS):
        carries[half(q), :] = jnp.where(back, counter[half(q), :], forth[half(q), :])
    terms[...] = jnp.where(row < 6, acc, 0.0)


def message_kernel(carries, terms, gram, message):
    blocks = carries.shape[0]
    row, lane = iota(0), iota(1)
    whole = [gram[half(0), :] + terms[...], gram[half(1), :]]
    line = jnp.zeros((ROWS, LANES), jnp.float32)
    for h in range(2):
        total = jnp.broadcast_to(jnp.sum(whole[h], axis=1, keepdims=True), (ROWS, LANES))
        line = line + jnp.where(lane == GROUP + h * ROWS + row, total, 0.0)
    line = jnp.broadcast_to(down(line), (ROWS, LANES))
    band = lax.axis_index(BAND)
    for q in range(blocks // ROWS):
        for u in range(LANES // GROUP):
            turned = pltpu.roll(carries[half(q), :], LANES - GROUP * u, 1) if u else carries[half(q), :]
            start = pl.multiple_of((band ^ u) * blocks + q * ROWS, ROWS)
            message[pl.ds(start, ROWS), :] = jnp.where(lane < GROUP, turned, line)


def mixing_weights(entry):
    count = HIST + 1
    scale = sum(entry(i, i) for i in range(count)) / count
    factor = {}
    for i in range(count):
        for j in range(i + 1):
            value = entry(j, i)
            if i == j:
                value = value + RIDGE_SCALE * scale
            for k in range(j):
                value = value - factor[i, k] * factor[j, k]
            factor[i, j] = jnp.sqrt(value) if i == j else value / factor[j, j]
    forward = []
    for row in range(count):
        partial = jnp.ones_like(scale)
        for inner in range(row):
            partial = partial - factor[row, inner] * forward[inner]
        forward.append(partial / factor[row, row])
    backward = [None] * count
    for row in reversed(range(count)):
        partial = forward[row]
        for inner in range(row + 1, count):
            partial = partial - factor[inner, row] * backward[inner]
        backward[row] = partial / factor[row, row]
    total = sum(backward)
    return [z / total for z in backward]


def finish_kernel(message, *refs):
    reach, rest = (refs[0], refs[2]), (refs[1], refs[3])
    wigner, past_iterates, past_residuals, residual, mixed, found, mixes, gone = refs[4:]
    cells, moments = wigner.shape
    chips, _, share = rest[0].shape
    per = share // LANES
    band = lax.axis_index(BAND)
    tiles = moments // LANES
    pieces = 4
    row, lane = iota(0), iota(1)
    out = []
    for n, (source, target) in enumerate(((found, residual), (mixes, mixed))):
        for q in range(pieces):
            columns = pl.ds(q * (moments // pieces), moments // pieces)
            out.append(pltpu.make_async_copy(source.at[:, columns], target.at[:, columns], gone.at[n * pieces + q]))
    total = message[half(0), :]
    for kb in range(1, tiles):
        total = total + message[half(kb), :]
    total = jnp.broadcast_to(down(total), (ROWS, LANES))

    def term(n):
        return pick(total, jnp.full((ROWS, LANES), GROUP + n, jnp.int32), 1)

    def entry(i, j):
        if j == HIST:
            return term(4) + term(5) if i == HIST else term(i)
        return term(6 + PAIRS.index((i, j)))

    for d in range(2 * chips):
        for kt in range(per):
            kb = (band ^ d) * per + kt
            rows = message[pl.ds(pl.multiple_of(kb * ROWS, ROWS), ROWS), :]
            spots = pick(rows, lane & (GROUP - 1), 1)
            carry = jnp.broadcast_to(down(jnp.where((lane >> 4) == row, spots, 0.0)), (ROWS, LANES))
            for h in range(2):
                at = (d // 2, half(h), tile(kt))
                found[half(h), pl.ds(pl.multiple_of(kb * LANES, LANES), LANES)] = rest[d % 2][at] + reach[d % 2][at] * carry
    for copy in out[:pieces]:
        copy.start()
    weights = mixing_weights(entry)
    for kb in range(tiles):
        for h in range(2):
            value = weights[HIST] * (wigner[half(h), tile(kb)] + MIX_STEP * found[half(h), tile(kb)])
            for j in range(HIST):
                earlier = past_iterates[j, half(h), tile(kb)] + MIX_STEP * past_residuals[j, half(h), tile(kb)]
                value = value + weights[j] * earlier
            mixes[half(h), tile(kb)] = value
        if (kb + 1) % (tiles // pieces) == 0:
            out[pieces + kb // (tiles // pieces)].start()
    for copy in out:
        copy.wait()


def body(wigner, past_iterates, past_residuals, velocity, out_rate, inflow, offsets, directions, coupling):
    _, cells, moments = wigner.shape
    bands = lax.axis_size(BAND)
    blocks = lax.axis_size(POS)
    wigner = wigner.reshape(cells, moments)
    past_iterates = past_iterates.reshape(HIST, cells, moments)
    past_residuals = past_residuals.reshape(HIST, cells, moments)
    offsets = offsets.reshape(1, moments)
    size = 4 * cells * moments
    share = moments // bands
    field = f32(cells, moments)
    dma = pltpu.SemaphoreType.DMA

    chips = lax.axis_size(BAND[0])

    def to_core(x):
        return lax.ppermute(x, BAND[1], [(0, 1), (1, 0)])

    def to_chip(x, d):
        return lax.ppermute(x, BAND[0], [(i, i ^ d) for i in range(chips)])

    sources = (offsets, wigner, directions, coupling, velocity, out_rate, inflow, past_residuals)
    opened = f32(chips, cells + ROWS, share)
    own, other, notes = call(
        open_kernel,
        (opened, opened, jax.ShapeDtypeStruct((blocks + bands, LANES), jnp.int32)),
        [HBM] * 8,
        20 * size,
        8 * size,
        [
            pltpu.SMEM(x.shape, x.dtype)
            if x.ndim == 1
            else pltpu.VMEM((cells, moments + 2 * LANES) if x is wigner else x.shape, x.dtype)
            for x in sources
        ]
        + [dma((8,))],
    )(*[pltpu.with_memory_space_constraint(x, pltpu.HBM) for x in sources])
    other = to_core(other)
    held = [jnp.stack([own[d], other[d]]) for d in range(chips)]
    held = held[:1] + [to_chip(held[d], d) for d in range(1, chips)]
    early = call(history_kernel, f32(16, LANES), [VMEM], 8 * size, 4 * size)(past_residuals)
    *held, early = lax.optimization_barrier((*held, early))
    pair = f32(2, cells, share)
    sums, own, other, *across = call(
        fold_kernel,
        (f32(blocks, ROWS, LANES), f32(cells, share), f32(cells, share)) + (pair,) * (chips - 1),
        [VMEM] * (chips + 2),
        20 * size,
        5 * size,
        [pltpu.VMEM((blocks, ROWS, LANES), jnp.float32), dma((4,))],
        out_specs=(HBM,) + (VMEM,) * (chips + 1),
    )(notes, velocity, *held)
    sums = lax.all_to_all(sums, POS, 0, 0, tiled=True)
    across = [to_chip(across[d - 1], d) for d in range(1, chips)]
    other = to_core(jnp.stack([other] + [x[1] for x in across]))
    local = (velocity, out_rate, inflow, wigner, past_residuals)
    part = f32(chips, cells, share)
    settled = []
    gram = early
    for flip, shares in enumerate(((own, *across), (other,))):
        reach, rest, gram = call(
            functools.partial(settle_kernel, flip),
            (part, part, f32(16, LANES)),
            [VMEM] * (len(shares) + 7),
            size // 64,
            size // 64,
        )(notes, *shares, *local, gram)
        settled += [reach, rest]
    carries, terms = call(
        carry_kernel,
        (f32(blocks, LANES), f32(ROWS, LANES)),
        [VMEM] * 2,
        size,
        256 * size,
        [pltpu.VMEM((blocks, LANES), jnp.float32)] * 2,
    )(notes, sums)
    message = call(message_kernel, f32(bands * blocks, LANES), [VMEM] * 3, size, size)(carries, terms, gram)
    message = lax.all_to_all(message, ALL, 0, 0, tiled=True)
    residual, mixed = call(
        finish_kernel,
        (field, field),
        [VMEM] * 8,
        8 * size,
        14 * size,
        [pltpu.VMEM((cells, moments), jnp.float32)] * 2 + [dma((8,))],
        out_specs=(HBM, HBM),
    )(message, *settled, wigner, past_iterates, past_residuals)
    return mixed[None], residual[None]


def solution(mesh):
    finer = Mesh(mesh.devices.reshape(4, 2, 4, 8), ("band_0", "band_1", "pos_0", "pos_1"))
    in_specs = (
        P(BAND, POS, None),
        P(None, BAND, POS, None),
        P(None, BAND, POS, None),
        P(POS, None),
        P(BAND, None),
        P(BAND, None),
        P(),
        P(),
        P(),
    )
    out_specs = (P(BAND, POS, None), P(BAND, POS, None))
    return jax.shard_map(body, mesh=finer, in_specs=in_specs, out_specs=out_specs, check_vma=False)
```

```python
import functools

import jax
import jax.numpy as jnp
from jax import lax
from jax.experimental import pallas as pl
from jax.experimental.pallas import tpu as pltpu
from jax.sharding import Mesh
from jax.sharding import PartitionSpec as P

POS = ("pos_0", "pos_1")
BAND = ("band_0", "band_1")
ALL = BAND + POS

MIX_STEP = 0.5
RIDGE_SCALE = 0.0001
LANES = 128
GROUP = 16
ROWS = 8
HIST = 4
PAIRS = [(i, j) for i in range(HIST) for j in range(i, HIST)]

VMEM = pl.BlockSpec(memory_space=pltpu.VMEM)
HBM = pl.BlockSpec(memory_space=pltpu.HBM)


def call(kernel, outs, in_specs, flops, nbytes, scratch=(), mib=24, out_specs=None):
    return pl.pallas_call(
        kernel,
        out_shape=outs,
        in_specs=in_specs,
        out_specs=jax.tree.map(lambda _: VMEM, outs) if out_specs is None else out_specs,
        scratch_shapes=list(scratch),
        compiler_params=pltpu.CompilerParams(vmem_limit_bytes=mib * 2**20),
        cost_estimate=pl.CostEstimate(flops=flops, bytes_accessed=nbytes, transcendentals=0),
    )


def f32(*shape):
    return jax.ShapeDtypeStruct(shape, jnp.float32)


def tile(kb):
    return slice(kb * LANES, (kb + 1) * LANES)


def pick(x, index, axis):
    return jnp.take_along_axis(x, index, axis=axis, mode="promise_in_bounds")


def iota(axis):
    return lax.broadcasted_iota(jnp.int32, (ROWS, LANES), axis)


def scan_tile(back, a, b):
    row = iota(0)
    away = jnp.where(back, ROWS - 1 - row, row)
    a = [jnp.where(back, a[1], a[0]), jnp.where(back, a[0], a[1])]
    if b is not None:
        b = [jnp.where(back, b[1], b[0]), jnp.where(back, b[0], b[1])]
    for d in (1, 2, 4):
        source = jnp.where(back, row + d, row - d) & (ROWS - 1)
        keep = away >= d
        for h in range(2):
            if b is not None:
                b[h] = a[h] * jnp.where(keep, pick(b[h], source, 0), 0.0) + b[h]
            a[h] = a[h] * jnp.where(keep, pick(a[h], source, 0), 1.0)
    last = jnp.where(back, 0, ROWS - 1) + jnp.zeros_like(row)
    if b is not None:
        b[1] = a[1] * pick(b[0], last, 0) + b[1]
    a[1] = a[1] * pick(a[0], last, 0)
    ends = [pick(a[1], last, 0)]
    if b is not None:
        ends.append(pick(b[1], last, 0))
        b = [jnp.where(back, b[1], b[0]), jnp.where(back, b[0], b[1])]
    a = [jnp.where(back, a[1], a[0]), jnp.where(back, a[0], a[1])]
    return a, b, ends


def flag(notes, index):
    return jnp.broadcast_to(notes[pl.ds(index, 1), :], (ROWS, LANES)) == 1


def down(x):
    return jnp.sum(x, axis=0, keepdims=True)


def half(h):
    return slice(h * ROWS, (h + 1) * ROWS)


def added_rows(parts):
    row = iota(0)
    parts = parts + [jnp.zeros((ROWS, LANES), jnp.float32)] * (ROWS - len(parts))
    for d in (4, 2, 1):
        low = (row & d) == 0
        count = len(parts) // 2
        parts = [
            jnp.where(low, parts[n], parts[n + count])
            + pick(jnp.where(low, parts[n + count], parts[n]), row ^ d, 0)
            for n in range(count)
        ]
    return parts[0]


def columns_of(kb):
    return pl.ds(pl.multiple_of(kb * LANES, LANES), LANES)


def open_kernel(*refs):
    sources, own, other, notes, held, arrived = refs[:8], refs[8], refs[9], refs[10], refs[11:19], refs[19]
    offsets, padded, directions, coupling, velocity, out_rate, inflow, past_residuals = held
    moments = offsets.shape[1]
    tiles = moments // LANES
    chips, _, share = own.shape
    per = share // LANES
    places = [padded.at[:, pl.ds(LANES, moments)] if ref is padded else ref for ref in held]
    copies = [pltpu.make_async_copy(a, b, arrived.at[n]) for n, (a, b) in enumerate(zip(sources, places))]
    for copy in copies:
        copy.start()
    band = lax.axis_index(BAND)
    row, lane = iota(0), iota(1)
    for kb in (0, tiles + 1):
        padded[:, tile(kb)] = jnp.zeros((2 * ROWS, LANES), jnp.float32)
    spots = [
        (target, d, t, (band ^ (2 * d + core)) * per + t)
        for core, target in ((1, other), (0, own))
        for d in range(chips)
        for t in range(per)
    ]
    copies[0].wait()
    copies[1].wait()
    for target, d, t, kb in spots:
        off = jnp.broadcast_to(offsets[:, columns_of(kb)], (ROWS, LANES))
        up, low = lane + off, lane - off
        up_in, low_in = up & (LANES - 1), low & (LANES - 1)
        for h in range(2):
            prv, here, nxt = [padded[half(h), columns_of(kb + n)] for n in range(3)]
            above = jnp.where(up < LANES, pick(here, up_in, 1), pick(nxt, up_in, 1))
            below = jnp.where(low >= 0, pick(here, low_in, 1), pick(prv, low_in, 1))
            target[d, half(h), tile(t)] = 0.5 * (above + below)
    for copy in copies[2:]:
        copy.wait()
    for target, d, t, kb in spots:
        back = jnp.full((ROWS, LANES), directions[kb], jnp.int32) == 1
        rate = jnp.broadcast_to(out_rate[:, columns_of(kb)], (ROWS, LANES))
        enters = jnp.broadcast_to(inflow[:, columns_of(kb)], (ROWS, LANES))
        speeds = [velocity[half(h), columns_of(kb)] for h in range(2)]
        reach, _, _ = scan_tile(back, [v * (1.0 / (v + rate)) for v in speeds], None)
        parts = [sum(past_residuals[j, half(h), columns_of(kb)] * reach[h] for h in range(2)) for j in range(HIST)]
        parts.append(sum(reach[h] * reach[h] for h in range(2)))
        parts.append(sum(reach[h] * padded[half(h), columns_of(kb + 1)] for h in range(2)))
        target[d, 2 * ROWS :, tile(t)] = jnp.where(row == 6, rate, jnp.where(row == 7, enters, added_rows(parts)))
    known = [directions[n] for n in range(tiles)] + [coupling[n] for n in range(coupling.shape[0])]
    for q in range(len(known) // ROWS):
        rows = jnp.zeros((ROWS, LANES), jnp.int32)
        for n in range(ROWS):
            rows = jnp.where(row == n, known[q * ROWS + n], rows)
        notes[half(q), :] = rows


def history_kernel(past_residuals, gram):
    tiles = past_residuals.shape[2] // LANES
    acc = [jnp.zeros((ROWS, LANES), jnp.float32) for _ in PAIRS]
    for kb in range(tiles):
        for h in range(2):
            past = [past_residuals[j, half(h), tile(kb)] for j in range(HIST)]
            for n, (i, j) in enumerate(PAIRS):
                acc[n] = acc[n] + past[i] * past[j]
    gram[...] = jnp.zeros(gram.shape, jnp.float32)
    for n in range(len(PAIRS)):
        gram[6 + n : 7 + n, :] = down(acc[n])


def at_contact(blocks, back, slope, inflow):
    row = iota(0)
    place = jnp.full((ROWS, LANES), lax.axis_index(POS), jnp.int32)
    first = (place == 0) & (row == 0) & jnp.logical_not(back)
    final = (place == blocks - 1) & (row == ROWS - 1) & back
    wide = jnp.broadcast_to(inflow, (ROWS, LANES))
    return [jnp.where(first, slope[0] * wide, 0.0), jnp.where(final, slope[1] * wide, 0.0)]


def fold_kernel(notes, velocity, *refs):
    chips = (len(refs) - 4) // 2
    held, message, own, other, across = refs[:chips], *refs[chips : chips + 3], refs[chips + 3 : -2]
    ready, gone = refs[-2:]
    bands = 2 * chips
    blocks = message.shape[0]
    per = own.shape[1] // LANES
    row, lane = iota(0), iota(1)
    band = lax.axis_index(BAND)
    chosen = [
        jnp.broadcast_to(notes[pl.ds(blocks + (band ^ u), 1), :], (ROWS, LANES)) ^ jnp.full((ROWS, LANES), band, jnp.int32)
        for u in range(bands)
    ]
    out = [
        pltpu.make_async_copy(
            ready.at[pl.ds(kt * bands, bands)], message.at[pl.ds(kt * bands, bands)], gone.at[kt]
        )
        for kt in range(per)
    ]
    for kt in range(per):
        kb = band * per + kt
        back = flag(notes, kb)
        speeds = [velocity[half(h), columns_of(kb)] for h in range(2)]
        spread = [[held[u // 2][u % 2, half(h), tile(kt)] for h in range(2)] for u in range(bands)]
        parts = []
        for u in range(bands):
            tail = held[u // 2][u % 2, 2 * ROWS :, tile(kt)]
            rate = jnp.broadcast_to(tail[6:7], (ROWS, LANES))
            slope, offset = [], []
            for h in range(2):
                partner = spread[0][h]
                for t in range(1, bands):
                    partner = jnp.where(chosen[u] == t, spread[t][h], partner)
                pair = spread[u][h] + partner
                if u < 2:
                    (other if u else own)[half(h), tile(kt)] = pair
                else:
                    across[u // 2 - 1][u % 2, half(h), tile(kt)] = pair
                inv = 1.0 / (speeds[h] + rate)
                slope.append(speeds[h] * inv)
                offset.append(rate * 0.5 * pair * inv)
            edge = at_contact(blocks, back, slope, tail[7:8])
            offset = [offset[h] + edge[h] for h in range(2)]
            reach, run, ends = scan_tile(back, slope, offset)
            crossed = jnp.broadcast_to(down(reach[0] * run[0] + reach[1] * run[1]), (ROWS, LANES)) - tail
            parts.append(
                jnp.where(row == 5, crossed, jnp.where(row == 6, ends[0], jnp.where(row == 7, ends[1], tail)))
            )
        for bit in range(3):
            step = 1 << bit
            high = ((lane >> (4 + bit)) & 1) == 1
            swapped = list(parts)
            for u in range(bands):
                if not u & step:
                    swapped[u] = jnp.where(high, pltpu.roll(parts[u + step], GROUP * step, 1), parts[u])
                    swapped[u + step] = jnp.where(high, parts[u + step], pltpu.roll(parts[u], LANES - GROUP * step, 1))
            parts = swapped
        for g in range(bands):
            ready[kt * bands + g] = parts[g]
        out[kt].start()
    for copy in out:
        copy.wait()


def settle_kernel(flip, notes, *refs):
    shares = refs[:-9]
    velocity, out_rate, inflow, wigner, past_residuals, early, reach_out, rest, gram = refs[-9:]
    shares = shares if len(shares) > 1 else [shares[0].at[d] for d in range(shares[0].shape[0])]
    shares = [share if len(share.shape) == 2 else share.at[0] for share in shares]
    per = rest.shape[2] // LANES
    blocks = velocity.shape[1] // LANES
    band = lax.axis_index(BAND)
    acc = [jnp.zeros((ROWS, LANES), jnp.float32) for _ in range(HIST + 1)]
    for d in range(len(shares)):
        for kt in range(per):
            kb = (band ^ (2 * d + flip)) * per + kt
            back = flag(notes, kb)
            columns = pl.ds(pl.multiple_of(kb * LANES, LANES), LANES)
            rate = jnp.broadcast_to(out_rate[:, columns], (ROWS, LANES))
            slope, offset = [], []
            for h in range(2):
                v = velocity[half(h), columns]
                inv = 1.0 / (v + rate)
                slope.append(v * inv)
                offset.append(rate * 0.5 * shares[d][half(h), tile(kt)] * inv)
            edge = at_contact(blocks, back, slope, inflow[:, columns])
            offset = [offset[h] + edge[h] for h in range(2)]
            reach, run, _ = scan_tile(back, slope, offset)
            for h in range(2):
                left = run[h] - wigner[half(h), columns]
                rest[d, half(h), tile(kt)] = left
                reach_out[d, half(h), tile(kt)] = reach[h]
                for j in range(HIST):
                    acc[j] = acc[j] + past_residuals[j, half(h), columns] * left
                acc[HIST] = acc[HIST] + left * left
    gram[half(0), :] = early[half(0), :] + added_rows(acc)
    gram[half(1), :] = early[half(1), :]


def carry_kernel(notes, sums, carries, terms, forth, counter):
    blocks = sums.shape[0]
    row = iota(0)
    back = flag(notes, lax.axis_index(BAND) * (blocks // ROWS) + lax.axis_index(POS) // ROWS)
    acc = jnp.zeros((ROWS, LANES), jnp.float32)
    carry = jnp.zeros((1, LANES), jnp.float32)
    for step in range(blocks):
        part = jnp.where(back, sums[blocks - 1 - step], sums[step])
        wide = jnp.broadcast_to(carry, (ROWS, LANES))
        forth[step : step + 1, :] = carry
        counter[blocks - 1 - step : blocks - step, :] = carry
        acc = acc + part * jnp.where(row == 4, wide * wide, jnp.where(row == 5, 2.0 * wide, wide))
        carry = part[6:7] * carry + part[7:8]
    for q in range(blocks // ROWS):
        carries[half(q), :] = jnp.where(back, counter[half(q), :], forth[half(q), :])
    terms[...] = jnp.where(row < 6, acc, 0.0)


def message_kernel(carries, terms, gram, message):
    blocks = carries.shape[0]
    row, lane = iota(0), iota(1)
    whole = [gram[half(0), :] + terms[...], gram[half(1), :]]
    line = jnp.zeros((ROWS, LANES), jnp.float32)
    for h in range(2):
        total = jnp.broadcast_to(jnp.sum(whole[h], axis=1, keepdims=True), (ROWS, LANES))
        line = line + jnp.where(lane == GROUP + h * ROWS + row, total, 0.0)
    line = jnp.broadcast_to(down(line), (ROWS, LANES))
    band = lax.axis_index(BAND)
    for q in range(blocks // ROWS):
        for u in range(LANES // GROUP):
            turned = pltpu.roll(carries[half(q), :], LANES - GROUP * u, 1) if u else carries[half(q), :]
            start = pl.multiple_of((band ^ u) * blocks + q * ROWS, ROWS)
            message[pl.ds(start, ROWS), :] = jnp.where(lane < GROUP, turned, line)


def mixing_weights(entry):
    count = HIST + 1
    scale = sum(entry(i, i) for i in range(count)) / count
    factor = {}
    for i in range(count):
        for j in range(i + 1):
            value = entry(j, i)
            if i == j:
                value = value + RIDGE_SCALE * scale
            for k in range(j):
                value = value - factor[i, k] * factor[j, k]
            factor[i, j] = jnp.sqrt(value) if i == j else value / factor[j, j]
    forward = []
    for row in range(count):
        partial = jnp.ones_like(scale)
        for inner in range(row):
            partial = partial - factor[row, inner] * forward[inner]
        forward.append(partial / factor[row, row])
    backward = [None] * count
    for row in reversed(range(count)):
        partial = forward[row]
        for inner in range(row + 1, count):
            partial = partial - factor[inner, row] * backward[inner]
        backward[row] = partial / factor[row, row]
    total = sum(backward)
    return [z / total for z in backward]


def finish_kernel(message, *refs):
    reach, rest = (refs[0], refs[2]), (refs[1], refs[3])
    wigner, past_iterates, past_residuals, residual, mixed, found, mixes, gone = refs[4:]
    cells, moments = wigner.shape
    chips, _, share = rest[0].shape
    per = share // LANES
    band = lax.axis_index(BAND)
    tiles = moments // LANES
    pieces = 4
    row, lane = iota(0), iota(1)
    out = []
    for n, (source, target) in enumerate(((found, residual), (mixes, mixed))):
        for q in range(pieces):
            columns = pl.ds(q * (moments // pieces), moments // pieces)
            out.append(pltpu.make_async_copy(source.at[:, columns], target.at[:, columns], gone.at[n * pieces + q]))
    total = message[half(0), :]
    for kb in range(1, tiles):
        total = total + message[half(kb), :]
    total = jnp.broadcast_to(down(total), (ROWS, LANES))

    def term(n):
        return pick(total, jnp.full((ROWS, LANES), GROUP + n, jnp.int32), 1)

    def entry(i, j):
        if j == HIST:
            return term(4) + term(5) if i == HIST else term(i)
        return term(6 + PAIRS.index((i, j)))

    for d in range(2 * chips):
        for kt in range(per):
            kb = (band ^ d) * per + kt
            rows = message[pl.ds(pl.multiple_of(kb * ROWS, ROWS), ROWS), :]
            spots = pick(rows, lane & (GROUP - 1), 1)
            carry = jnp.broadcast_to(down(jnp.where((lane >> 4) == row, spots, 0.0)), (ROWS, LANES))
            for h in range(2):
                at = (d // 2, half(h), tile(kt))
                found[half(h), pl.ds(pl.multiple_of(kb * LANES, LANES), LANES)] = rest[d % 2][at] + reach[d % 2][at] * carry
    for copy in out[:pieces]:
        copy.start()
    weights = mixing_weights(entry)
    for kb in range(tiles):
        for h in range(2):
            value = weights[HIST] * (wigner[half(h), tile(kb)] + MIX_STEP * found[half(h), tile(kb)])
            for j in range(HIST):
                earlier = past_iterates[j, half(h), tile(kb)] + MIX_STEP * past_residuals[j, half(h), tile(kb)]
                value = value + weights[j] * earlier
            mixes[half(h), tile(kb)] = value
        if (kb + 1) % (tiles // pieces) == 0:
            out[pieces + kb // (tiles // pieces)].start()
    for copy in out:
        copy.wait()


def body(wigner, past_iterates, past_residuals, velocity, out_rate, inflow, offsets, directions, coupling):
    _, cells, moments = wigner.shape
    bands = lax.axis_size(BAND)
    blocks = lax.axis_size(POS)
    wigner = wigner.reshape(cells, moments)
    past_iterates = past_iterates.reshape(HIST, cells, moments)
    past_residuals = past_residuals.reshape(HIST, cells, moments)
    offsets = offsets.reshape(1, moments)
    size = 4 * cells * moments
    share = moments // bands
    field = f32(cells, moments)
    dma = pltpu.SemaphoreType.DMA

    chips = lax.axis_size(BAND[0])

    def to_core(x):
        return lax.ppermute(x, BAND[1], [(0, 1), (1, 0)])

    def to_chip(x, d):
        return lax.ppermute(x, BAND[0], [(i, i ^ d) for i in range(chips)])

    sources = (offsets, wigner, directions, coupling, velocity, out_rate, inflow, past_residuals)
    opened = f32(chips, cells + ROWS, share)
    own, other, notes = call(
        open_kernel,
        (opened, opened, jax.ShapeDtypeStruct((blocks + bands, LANES), jnp.int32)),
        [HBM] * 8,
        20 * size,
        8 * size,
        [
            pltpu.SMEM(x.shape, x.dtype)
            if x.ndim == 1
            else pltpu.VMEM((cells, moments + 2 * LANES) if x is wigner else x.shape, x.dtype)
            for x in sources
        ]
        + [dma((8,))],
    )(*[pltpu.with_memory_space_constraint(x, pltpu.HBM) for x in sources])
    other = to_core(other)
    held = [jnp.stack([own[d], other[d]]) for d in range(chips)]
    held = held[:1] + [to_chip(held[d], d) for d in range(1, chips)]
    early = call(history_kernel, f32(16, LANES), [VMEM], 8 * size, 4 * size)(past_residuals)
    *held, early = lax.optimization_barrier((*held, early))
    pair = f32(2, cells, share)
    sums, own, other, *across = call(
        fold_kernel,
        (f32(blocks, ROWS, LANES), f32(cells, share), f32(cells, share)) + (pair,) * (chips - 1),
        [VMEM] * (chips + 2),
        20 * size,
        5 * size,
        [pltpu.VMEM((blocks, ROWS, LANES), jnp.float32), dma((4,))],
        out_specs=(HBM,) + (VMEM,) * (chips + 1),
    )(notes, velocity, *held)
    sums = lax.all_to_all(sums, POS, 0, 0, tiled=True)
    across = [to_chip(across[d - 1], d) for d in range(1, chips)]
    others = [to_core(other)] + [to_core(x[1]) for x in across]
    local = (velocity, out_rate, inflow, wigner, past_residuals)
    part = f32(chips, cells, share)
    settled = []
    gram = early
    for flip, shares in enumerate(((own, *across), others)):
        reach, rest, gram = call(
            functools.partial(settle_kernel, flip),
            (part, part, f32(16, LANES)),
            [VMEM] * (len(shares) + 7),
            size // 64,
            size // 64,
        )(notes, *shares, *local, gram)
        settled += [reach, rest]
    carries, terms = call(
        carry_kernel,
        (f32(blocks, LANES), f32(ROWS, LANES)),
        [VMEM] * 2,
        size,
        256 * size,
        [pltpu.VMEM((blocks, LANES), jnp.float32)] * 2,
    )(notes, sums)
    message = call(message_kernel, f32(bands * blocks, LANES), [VMEM] * 3, size, size)(carries, terms, gram)
    message = lax.all_to_all(message, ALL, 0, 0, tiled=True)
    residual, mixed = call(
        finish_kernel,
        (field, field),
        [VMEM] * 8,
        8 * size,
        14 * size,
        [pltpu.VMEM((cells, moments), jnp.float32)] * 2 + [dma((8,))],
        out_specs=(HBM, HBM),
    )(message, *settled, wigner, past_iterates, past_residuals)
    return mixed[None], residual[None]


def solution(mesh):
    finer = Mesh(mesh.devices.reshape(4, 2, 4, 8), ("band_0", "band_1", "pos_0", "pos_1"))
    in_specs = (
        P(BAND, POS, None),
        P(None, BAND, POS, None),
        P(None, BAND, POS, None),
        P(POS, None),
        P(BAND, None),
        P(BAND, None),
        P(),
        P(),
        P(),
    )
    out_specs = (P(BAND, POS, None), P(BAND, POS, None))
    return jax.shard_map(body, mesh=finer, in_specs=in_specs, out_specs=out_specs, check_vma=False)
```

```python
import functools

import jax
import jax.numpy as jnp
from jax import lax
from jax.experimental import pallas as pl
from jax.experimental.pallas import tpu as pltpu
from jax.sharding import Mesh
from jax.sharding import PartitionSpec as P

POS = ("pos_0", "pos_1")
BAND = ("band_0", "band_1")
ALL = BAND + POS

MIX_STEP = 0.5
RIDGE_SCALE = 0.0001
LANES = 128
GROUP = 16
ROWS = 8
HIST = 4
PAIRS = [(i, j) for i in range(HIST) for j in range(i, HIST)]

VMEM = pl.BlockSpec(memory_space=pltpu.VMEM)
HBM = pl.BlockSpec(memory_space=pltpu.HBM)


def call(kernel, outs, in_specs, flops, nbytes, scratch=(), mib=24, out_specs=None):
    return pl.pallas_call(
        kernel,
        out_shape=outs,
        in_specs=in_specs,
        out_specs=jax.tree.map(lambda _: VMEM, outs) if out_specs is None else out_specs,
        scratch_shapes=list(scratch),
        compiler_params=pltpu.CompilerParams(vmem_limit_bytes=mib * 2**20),
        cost_estimate=pl.CostEstimate(flops=flops, bytes_accessed=nbytes, transcendentals=0),
    )


def f32(*shape):
    return jax.ShapeDtypeStruct(shape, jnp.float32)


def tile(kb):
    return slice(kb * LANES, (kb + 1) * LANES)


def pick(x, index, axis):
    return jnp.take_along_axis(x, index, axis=axis, mode="promise_in_bounds")


def iota(axis):
    return lax.broadcasted_iota(jnp.int32, (ROWS, LANES), axis)


def scan_tile(back, a, b):
    row = iota(0)
    away = jnp.where(back, ROWS - 1 - row, row)
    a = [jnp.where(back, a[1], a[0]), jnp.where(back, a[0], a[1])]
    if b is not None:
        b = [jnp.where(back, b[1], b[0]), jnp.where(back, b[0], b[1])]
    for d in (1, 2, 4):
        source = jnp.where(back, row + d, row - d) & (ROWS - 1)
        keep = away >= d
        for h in range(2):
            if b is not None:
                b[h] = a[h] * jnp.where(keep, pick(b[h], source, 0), 0.0) + b[h]
            a[h] = a[h] * jnp.where(keep, pick(a[h], source, 0), 1.0)
    last = jnp.where(back, 0, ROWS - 1) + jnp.zeros_like(row)
    if b is not None:
        b[1] = a[1] * pick(b[0], last, 0) + b[1]
    a[1] = a[1] * pick(a[0], last, 0)
    ends = [pick(a[1], last, 0)]
    if b is not None:
        ends.append(pick(b[1], last, 0))
        b = [jnp.where(back, b[1], b[0]), jnp.where(back, b[0], b[1])]
    a = [jnp.where(back, a[1], a[0]), jnp.where(back, a[0], a[1])]
    return a, b, ends


def flag(notes, index):
    return jnp.broadcast_to(notes[pl.ds(index, 1), :], (ROWS, LANES)) == 1


def down(x):
    return jnp.sum(x, axis=0, keepdims=True)


def half(h):
    return slice(h * ROWS, (h + 1) * ROWS)


def added_rows(parts):
    row = iota(0)
    parts = parts + [jnp.zeros((ROWS, LANES), jnp.float32)] * (ROWS - len(parts))
    for d in (4, 2, 1):
        low = (row & d) == 0
        count = len(parts) // 2
        parts = [
            jnp.where(low, parts[n], parts[n + count])
            + pick(jnp.where(low, parts[n + count], parts[n]), row ^ d, 0)
            for n in range(count)
        ]
    return parts[0]


def columns_of(kb):
    return pl.ds(pl.multiple_of(kb * LANES, LANES), LANES)


def open_kernel(*refs):
    sources, own, other, notes, held, arrived = refs[:8], refs[8], refs[9], refs[10], refs[11:19], refs[19]
    offsets, padded, directions, coupling, velocity, out_rate, inflow, past_residuals = held
    moments = offsets.shape[1]
    tiles = moments // LANES
    chips, _, share = own.shape
    per = share // LANES
    places = [padded.at[:, pl.ds(LANES, moments)] if ref is padded else ref for ref in held]
    copies = [pltpu.make_async_copy(a, b, arrived.at[n]) for n, (a, b) in enumerate(zip(sources, places))]
    for copy in copies:
        copy.start()
    band = lax.axis_index(BAND)
    row, lane = iota(0), iota(1)
    for kb in (0, tiles + 1):
        padded[:, tile(kb)] = jnp.zeros((2 * ROWS, LANES), jnp.float32)
    spots = [
        (target, d, t, (band ^ (2 * d + core)) * per + t)
        for core, target in ((1, other), (0, own))
        for d in range(chips)
        for t in range(per)
    ]
    copies[0].wait()
    copies[1].wait()
    for target, d, t, kb in spots:
        off = jnp.broadcast_to(offsets[:, columns_of(kb)], (ROWS, LANES))
        up, low = lane + off, lane - off
        up_in, low_in = up & (LANES - 1), low & (LANES - 1)
        for h in range(2):
            prv, here, nxt = [padded[half(h), columns_of(kb + n)] for n in range(3)]
            above = jnp.where(up < LANES, pick(here, up_in, 1), pick(nxt, up_in, 1))
            below = jnp.where(low >= 0, pick(here, low_in, 1), pick(prv, low_in, 1))
            target[d, half(h), tile(t)] = 0.5 * (above + below)
    for copy in copies[2:]:
        copy.wait()
    for target, d, t, kb in spots:
        back = jnp.full((ROWS, LANES), directions[kb], jnp.int32) == 1
        rate = jnp.broadcast_to(out_rate[:, columns_of(kb)], (ROWS, LANES))
        enters = jnp.broadcast_to(inflow[:, columns_of(kb)], (ROWS, LANES))
        speeds = [velocity[half(h), columns_of(kb)] for h in range(2)]
        reach, _, _ = scan_tile(back, [v * (1.0 / (v + rate)) for v in speeds], None)
        parts = [sum(past_residuals[j, half(h), columns_of(kb)] * reach[h] for h in range(2)) for j in range(HIST)]
        parts.append(sum(reach[h] * reach[h] for h in range(2)))
        parts.append(sum(reach[h] * padded[half(h), columns_of(kb + 1)] for h in range(2)))
        target[d, 2 * ROWS :, tile(t)] = jnp.where(row == 6, rate, jnp.where(row == 7, enters, added_rows(parts)))
    known = [directions[n] for n in range(tiles)] + [coupling[n] for n in range(coupling.shape[0])]
    for q in range(len(known) // ROWS):
        rows = jnp.zeros((ROWS, LANES), jnp.int32)
        for n in range(ROWS):
            rows = jnp.where(row == n, known[q * ROWS + n], rows)
        notes[half(q), :] = rows


def history_kernel(past_residuals, gram):
    tiles = past_residuals.shape[2] // LANES
    acc = [jnp.zeros((ROWS, LANES), jnp.float32) for _ in PAIRS]
    for kb in range(tiles):
        for h in range(2):
            past = [past_residuals[j, half(h), tile(kb)] for j in range(HIST)]
            for n, (i, j) in enumerate(PAIRS):
                acc[n] = acc[n] + past[i] * past[j]
    gram[...] = jnp.zeros(gram.shape, jnp.float32)
    for n in range(len(PAIRS)):
        gram[6 + n : 7 + n, :] = down(acc[n])


def at_contact(blocks, back, slope, inflow):
    row = iota(0)
    place = jnp.full((ROWS, LANES), lax.axis_index(POS), jnp.int32)
    first = (place == 0) & (row == 0) & jnp.logical_not(back)
    final = (place == blocks - 1) & (row == ROWS - 1) & back
    wide = jnp.broadcast_to(inflow, (ROWS, LANES))
    return [jnp.where(first, slope[0] * wide, 0.0), jnp.where(final, slope[1] * wide, 0.0)]


def fold_kernel(notes, velocity, *refs):
    chips = (len(refs) - 4) // 2
    held, message, own, other, across = refs[:chips], *refs[chips : chips + 3], refs[chips + 3 : -2]
    ready, gone = refs[-2:]
    bands = 2 * chips
    blocks = message.shape[0]
    per = own.shape[1] // LANES
    row, lane = iota(0), iota(1)
    band = lax.axis_index(BAND)
    chosen = [
        jnp.broadcast_to(notes[pl.ds(blocks + (band ^ u), 1), :], (ROWS, LANES)) ^ jnp.full((ROWS, LANES), band, jnp.int32)
        for u in range(bands)
    ]
    out = [
        pltpu.make_async_copy(
            ready.at[pl.ds(kt * bands, bands)], message.at[pl.ds(kt * bands, bands)], gone.at[kt]
        )
        for kt in range(per)
    ]
    for kt in range(per):
        kb = band * per + kt
        back = flag(notes, kb)
        speeds = [velocity[half(h), columns_of(kb)] for h in range(2)]
        spread = [[held[u // 2][u % 2, half(h), tile(kt)] for h in range(2)] for u in range(bands)]
        parts = []
        for u in range(bands):
            tail = held[u // 2][u % 2, 2 * ROWS :, tile(kt)]
            rate = jnp.broadcast_to(tail[6:7], (ROWS, LANES))
            slope, offset = [], []
            for h in range(2):
                partner = spread[0][h]
                for t in range(1, bands):
                    partner = jnp.where(chosen[u] == t, spread[t][h], partner)
                pair = spread[u][h] + partner
                if u < 2:
                    (other if u else own)[half(h), tile(kt)] = pair
                else:
                    across[u // 2 - 1][u % 2, half(h), tile(kt)] = pair
                inv = 1.0 / (speeds[h] + rate)
                slope.append(speeds[h] * inv)
                offset.append(rate * 0.5 * pair * inv)
            edge = at_contact(blocks, back, slope, tail[7:8])
            offset = [offset[h] + edge[h] for h in range(2)]
            reach, run, ends = scan_tile(back, slope, offset)
            crossed = jnp.broadcast_to(down(reach[0] * run[0] + reach[1] * run[1]), (ROWS, LANES)) - tail
            parts.append(
                jnp.where(row == 5, crossed, jnp.where(row == 6, ends[0], jnp.where(row == 7, ends[1], tail)))
            )
        for bit in range(3):
            step = 1 << bit
            high = ((lane >> (4 + bit)) & 1) == 1
            swapped = list(parts)
            for u in range(bands):
                if not u & step:
                    swapped[u] = jnp.where(high, pltpu.roll(parts[u + step], GROUP * step, 1), parts[u])
                    swapped[u + step] = jnp.where(high, parts[u + step], pltpu.roll(parts[u], LANES - GROUP * step, 1))
            parts = swapped
        for g in range(bands):
            ready[kt * bands + g] = parts[g]
        out[kt].start()
    for copy in out:
        copy.wait()


def settle_kernel(plan, notes, *refs):
    shares = refs[:-9]
    velocity, out_rate, inflow, wigner, past_residuals, early, reach_out, rest, gram = refs[-9:]
    per = rest.shape[2] // LANES
    blocks = velocity.shape[1] // LANES
    band = lax.axis_index(BAND)
    acc = [jnp.zeros((ROWS, LANES), jnp.float32) for _ in range(HIST + 1)]
    for which, place, u in plan:
        d = u // 2
        source = shares[which] if len(shares[which].shape) == 2 else shares[which].at[place]
        for kt in range(per):
            kb = (band ^ u) * per + kt
            back = flag(notes, kb)
            columns = pl.ds(pl.multiple_of(kb * LANES, LANES), LANES)
            rate = jnp.broadcast_to(out_rate[:, columns], (ROWS, LANES))
            slope, offset = [], []
            for h in range(2):
                v = velocity[half(h), columns]
                inv = 1.0 / (v + rate)
                slope.append(v * inv)
                offset.append(rate * 0.5 * source[half(h), tile(kt)] * inv)
            edge = at_contact(blocks, back, slope, inflow[:, columns])
            offset = [offset[h] + edge[h] for h in range(2)]
            reach, run, _ = scan_tile(back, slope, offset)
            for h in range(2):
                left = run[h] - wigner[half(h), columns]
                rest[d, half(h), tile(kt)] = left
                reach_out[d, half(h), tile(kt)] = reach[h]
                for j in range(HIST):
                    acc[j] = acc[j] + past_residuals[j, half(h), columns] * left
                acc[HIST] = acc[HIST] + left * left
    gram[half(0), :] = early[half(0), :] + added_rows(acc)
    gram[half(1), :] = early[half(1), :]


def carry_kernel(notes, sums, carries, terms, forth, counter):
    blocks = sums.shape[0]
    row = iota(0)
    back = flag(notes, lax.axis_index(BAND) * (blocks // ROWS) + lax.axis_index(POS) // ROWS)
    acc = jnp.zeros((ROWS, LANES), jnp.float32)
    carry = jnp.zeros((1, LANES), jnp.float32)
    for step in range(blocks):
        part = jnp.where(back, sums[blocks - 1 - step], sums[step])
        wide = jnp.broadcast_to(carry, (ROWS, LANES))
        forth[step : step + 1, :] = carry
        counter[blocks - 1 - step : blocks - step, :] = carry
        acc = acc + part * jnp.where(row == 4, wide * wide, jnp.where(row == 5, 2.0 * wide, wide))
        carry = part[6:7] * carry + part[7:8]
    for q in range(blocks // ROWS):
        carries[half(q), :] = jnp.where(back, counter[half(q), :], forth[half(q), :])
    terms[...] = jnp.where(row < 6, acc, 0.0)


def message_kernel(carries, terms, gram, message):
    blocks = carries.shape[0]
    row, lane = iota(0), iota(1)
    whole = [gram[half(0), :] + terms[...], gram[half(1), :]]
    line = jnp.zeros((ROWS, LANES), jnp.float32)
    for h in range(2):
        total = jnp.broadcast_to(jnp.sum(whole[h], axis=1, keepdims=True), (ROWS, LANES))
        line = line + jnp.where(lane == GROUP + h * ROWS + row, total, 0.0)
    line = jnp.broadcast_to(down(line), (ROWS, LANES))
    band = lax.axis_index(BAND)
    for q in range(blocks // ROWS):
        for u in range(LANES // GROUP):
            turned = pltpu.roll(carries[half(q), :], LANES - GROUP * u, 1) if u else carries[half(q), :]
            start = pl.multiple_of((band ^ u) * blocks + q * ROWS, ROWS)
            message[pl.ds(start, ROWS), :] = jnp.where(lane < GROUP, turned, line)


def mixing_weights(entry):
    count = HIST + 1
    scale = sum(entry(i, i) for i in range(count)) / count
    factor = {}
    for i in range(count):
        for j in range(i + 1):
            value = entry(j, i)
            if i == j:
                value = value + RIDGE_SCALE * scale
            for k in range(j):
                value = value - factor[i, k] * factor[j, k]
            factor[i, j] = jnp.sqrt(value) if i == j else value / factor[j, j]
    forward = []
    for row in range(count):
        partial = jnp.ones_like(scale)
        for inner in range(row):
            partial = partial - factor[row, inner] * forward[inner]
        forward.append(partial / factor[row, row])
    backward = [None] * count
    for row in reversed(range(count)):
        partial = forward[row]
        for inner in range(row + 1, count):
            partial = partial - factor[inner, row] * backward[inner]
        backward[row] = partial / factor[row, row]
    total = sum(backward)
    return [z / total for z in backward]


def finish_kernel(message, *refs):
    reach, rest = (refs[0], refs[2]), (refs[1], refs[3])
    wigner, past_iterates, past_residuals, residual, mixed, found, mixes, gone = refs[4:]
    cells, moments = wigner.shape
    chips, _, share = rest[0].shape
    per = share // LANES
    band = lax.axis_index(BAND)
    tiles = moments // LANES
    pieces = 4
    row, lane = iota(0), iota(1)
    out = []
    for n, (source, target) in enumerate(((found, residual), (mixes, mixed))):
        for q in range(pieces):
            columns = pl.ds(q * (moments // pieces), moments // pieces)
            out.append(pltpu.make_async_copy(source.at[:, columns], target.at[:, columns], gone.at[n * pieces + q]))
    total = message[half(0), :]
    for kb in range(1, tiles):
        total = total + message[half(kb), :]
    total = jnp.broadcast_to(down(total), (ROWS, LANES))

    def term(n):
        return pick(total, jnp.full((ROWS, LANES), GROUP + n, jnp.int32), 1)

    def entry(i, j):
        if j == HIST:
            return term(4) + term(5) if i == HIST else term(i)
        return term(6 + PAIRS.index((i, j)))

    for d in range(2 * chips):
        for kt in range(per):
            kb = (band ^ d) * per + kt
            rows = message[pl.ds(pl.multiple_of(kb * ROWS, ROWS), ROWS), :]
            spots = pick(rows, lane & (GROUP - 1), 1)
            carry = jnp.broadcast_to(down(jnp.where((lane >> 4) == row, spots, 0.0)), (ROWS, LANES))
            for h in range(2):
                at = (d // 2, half(h), tile(kt))
                found[half(h), pl.ds(pl.multiple_of(kb * LANES, LANES), LANES)] = rest[d % 2][at] + reach[d % 2][at] * carry
    for copy in out[:pieces]:
        copy.start()
    weights = mixing_weights(entry)
    for kb in range(tiles):
        for h in range(2):
            value = weights[HIST] * (wigner[half(h), tile(kb)] + MIX_STEP * found[half(h), tile(kb)])
            for j in range(HIST):
                earlier = past_iterates[j, half(h), tile(kb)] + MIX_STEP * past_residuals[j, half(h), tile(kb)]
                value = value + weights[j] * earlier
            mixes[half(h), tile(kb)] = value
        if (kb + 1) % (tiles // pieces) == 0:
            out[pieces + kb // (tiles // pieces)].start()
    for copy in out:
        copy.wait()


def body(wigner, past_iterates, past_residuals, velocity, out_rate, inflow, offsets, directions, coupling):
    _, cells, moments = wigner.shape
    bands = lax.axis_size(BAND)
    blocks = lax.axis_size(POS)
    wigner = wigner.reshape(cells, moments)
    past_iterates = past_iterates.reshape(HIST, cells, moments)
    past_residuals = past_residuals.reshape(HIST, cells, moments)
    offsets = offsets.reshape(1, moments)
    size = 4 * cells * moments
    share = moments // bands
    field = f32(cells, moments)
    dma = pltpu.SemaphoreType.DMA

    chips = lax.axis_size(BAND[0])

    def to_core(x):
        return lax.ppermute(x, BAND[1], [(0, 1), (1, 0)])

    def to_chip(x, d):
        return lax.ppermute(x, BAND[0], [(i, i ^ d) for i in range(chips)])

    sources = (offsets, wigner, directions, coupling, velocity, out_rate, inflow, past_residuals)
    opened = f32(chips, cells + ROWS, share)
    own, other, notes = call(
        open_kernel,
        (opened, opened, jax.ShapeDtypeStruct((blocks + bands, LANES), jnp.int32)),
        [HBM] * 8,
        20 * size,
        8 * size,
        [
            pltpu.SMEM(x.shape, x.dtype)
            if x.ndim == 1
            else pltpu.VMEM((cells, moments + 2 * LANES) if x is wigner else x.shape, x.dtype)
            for x in sources
        ]
        + [dma((8,))],
    )(*[pltpu.with_memory_space_constraint(x, pltpu.HBM) for x in sources])
    other = to_core(other)
    held = [jnp.stack([own[d], other[d]]) for d in range(chips)]
    held = held[:1] + [to_chip(held[d], d) for d in range(1, chips)]
    early = call(history_kernel, f32(16, LANES), [VMEM], 8 * size, 4 * size)(past_residuals)
    *held, early = lax.optimization_barrier((*held, early))
    pair = f32(2, cells, share)
    sums, own, other, *across = call(
        fold_kernel,
        (f32(blocks, ROWS, LANES), f32(cells, share), f32(cells, share)) + (pair,) * (chips - 1),
        [VMEM] * (chips + 2),
        20 * size,
        5 * size,
        [pltpu.VMEM((blocks, ROWS, LANES), jnp.float32), dma((4,))],
        out_specs=(HBM,) + (VMEM,) * (chips + 1),
    )(notes, velocity, *held)
    sums = lax.all_to_all(sums, POS, 0, 0, tiled=True)
    across = [to_chip(across[d - 1], d) for d in range(1, chips)]
    other = [other] + [x[1] for x in across]
    groups = [[0, 2, 3], [1]]
    others = [to_core(jnp.stack([other[d] for d in group])) for group in groups]
    local = (velocity, out_rate, inflow, wigner, past_residuals)
    part = f32(chips, cells, share)
    settled = []
    gram = early
    plans = [(n, 0, 2 * n) for n in range(chips)], [(n, m, 2 * d + 1) for n, g in enumerate(groups) for m, d in enumerate(g)]
    for plan, shares in zip(plans, ((own, *across), others)):
        reach, rest, gram = call(
            functools.partial(settle_kernel, plan),
            (part, part, f32(16, LANES)),
            [VMEM] * (len(shares) + 7),
            size // 64,
            size // 64,
        )(notes, *shares, *local, gram)
        settled += [reach, rest]
    carries, terms = call(
        carry_kernel,
        (f32(blocks, LANES), f32(ROWS, LANES)),
        [VMEM] * 2,
        size,
        256 * size,
        [pltpu.VMEM((blocks, LANES), jnp.float32)] * 2,
    )(notes, sums)
    message = call(message_kernel, f32(bands * blocks, LANES), [VMEM] * 3, size, size)(carries, terms, gram)
    message = lax.all_to_all(message, ALL, 0, 0, tiled=True)
    residual, mixed = call(
        finish_kernel,
        (field, field),
        [VMEM] * 8,
        8 * size,
        14 * size,
        [pltpu.VMEM((cells, moments), jnp.float32)] * 2 + [dma((8,))],
        out_specs=(HBM, HBM),
    )(message, *settled, wigner, past_iterates, past_residuals)
    return mixed[None], residual[None]


def solution(mesh):
    finer = Mesh(mesh.devices.reshape(4, 2, 4, 8), ("band_0", "band_1", "pos_0", "pos_1"))
    in_specs = (
        P(BAND, POS, None),
        P(None, BAND, POS, None),
        P(None, BAND, POS, None),
        P(POS, None),
        P(BAND, None),
        P(BAND, None),
        P(),
        P(),
        P(),
    )
    out_specs = (P(BAND, POS, None), P(BAND, POS, None))
    return jax.shard_map(body, mesh=finer, in_specs=in_specs, out_specs=out_specs, check_vma=False)
```

```python
import functools

import jax
import jax.numpy as jnp
from jax import lax
from jax.experimental import pallas as pl
from jax.experimental.pallas import tpu as pltpu
from jax.sharding import Mesh
from jax.sharding import PartitionSpec as P

POS = ("pos_0", "pos_1")
BAND = ("band_0", "band_1")
ALL = BAND + POS

MIX_STEP = 0.5
RIDGE_SCALE = 0.0001
LANES = 128
FARTHEST_FIRST = (2, 1, 3)
GROUP = 16
ROWS = 8
HIST = 4
PAIRS = [(i, j) for i in range(HIST) for j in range(i, HIST)]

VMEM = pl.BlockSpec(memory_space=pltpu.VMEM)
HBM = pl.BlockSpec(memory_space=pltpu.HBM)


def call(kernel, outs, in_specs, flops, nbytes, scratch=(), mib=24, out_specs=None):
    return pl.pallas_call(
        kernel,
        out_shape=outs,
        in_specs=in_specs,
        out_specs=jax.tree.map(lambda _: VMEM, outs) if out_specs is None else out_specs,
        scratch_shapes=list(scratch),
        compiler_params=pltpu.CompilerParams(vmem_limit_bytes=mib * 2**20),
        cost_estimate=pl.CostEstimate(flops=flops, bytes_accessed=nbytes, transcendentals=0),
    )


def f32(*shape):
    return jax.ShapeDtypeStruct(shape, jnp.float32)


def tile(kb):
    return slice(kb * LANES, (kb + 1) * LANES)


def pick(x, index, axis):
    return jnp.take_along_axis(x, index, axis=axis, mode="promise_in_bounds")


def iota(axis):
    return lax.broadcasted_iota(jnp.int32, (ROWS, LANES), axis)


def scan_tile(back, a, b):
    row = iota(0)
    away = jnp.where(back, ROWS - 1 - row, row)
    a = [jnp.where(back, a[1], a[0]), jnp.where(back, a[0], a[1])]
    if b is not None:
        b = [jnp.where(back, b[1], b[0]), jnp.where(back, b[0], b[1])]
    for d in (1, 2, 4):
        source = jnp.where(back, row + d, row - d) & (ROWS - 1)
        keep = away >= d
        for h in range(2):
            if b is not None:
                b[h] = a[h] * jnp.where(keep, pick(b[h], source, 0), 0.0) + b[h]
            a[h] = a[h] * jnp.where(keep, pick(a[h], source, 0), 1.0)
    last = jnp.where(back, 0, ROWS - 1) + jnp.zeros_like(row)
    if b is not None:
        b[1] = a[1] * pick(b[0], last, 0) + b[1]
    a[1] = a[1] * pick(a[0], last, 0)
    ends = [pick(a[1], last, 0)]
    if b is not None:
        ends.append(pick(b[1], last, 0))
        b = [jnp.where(back, b[1], b[0]), jnp.where(back, b[0], b[1])]
    a = [jnp.where(back, a[1], a[0]), jnp.where(back, a[0], a[1])]
    return a, b, ends


def flag(notes, index):
    return jnp.broadcast_to(notes[pl.ds(index, 1), :], (ROWS, LANES)) == 1


def down(x):
    return jnp.sum(x, axis=0, keepdims=True)


def half(h):
    return slice(h * ROWS, (h + 1) * ROWS)


def added_rows(parts):
    row = iota(0)
    parts = parts + [jnp.zeros((ROWS, LANES), jnp.float32)] * (ROWS - len(parts))
    for d in (4, 2, 1):
        low = (row & d) == 0
        count = len(parts) // 2
        parts = [
            jnp.where(low, parts[n], parts[n + count])
            + pick(jnp.where(low, parts[n + count], parts[n]), row ^ d, 0)
            for n in range(count)
        ]
    return parts[0]


def columns_of(kb):
    return pl.ds(pl.multiple_of(kb * LANES, LANES), LANES)


def open_kernel(*refs):
    sources, own, other, notes, held, arrived = refs[:8], refs[8], refs[9], refs[10], refs[11:19], refs[19]
    offsets, padded, directions, coupling, velocity, out_rate, inflow, past_residuals = held
    moments = offsets.shape[1]
    tiles = moments // LANES
    chips, _, share = own.shape
    per = share // LANES
    places = [padded.at[:, pl.ds(LANES, moments)] if ref is padded else ref for ref in held]
    copies = [pltpu.make_async_copy(a, b, arrived.at[n]) for n, (a, b) in enumerate(zip(sources, places))]
    for copy in copies:
        copy.start()
    band = lax.axis_index(BAND)
    row, lane = iota(0), iota(1)
    for kb in (0, tiles + 1):
        padded[:, tile(kb)] = jnp.zeros((2 * ROWS, LANES), jnp.float32)
    spots = [
        (target, d, t, (band ^ (2 * d + core)) * per + t)
        for core, target in ((1, other), (0, own))
        for d in range(chips)
        for t in range(per)
    ]
    copies[0].wait()
    copies[1].wait()
    for target, d, t, kb in spots:
        off = jnp.broadcast_to(offsets[:, columns_of(kb)], (ROWS, LANES))
        up, low = lane + off, lane - off
        up_in, low_in = up & (LANES - 1), low & (LANES - 1)
        for h in range(2):
            prv, here, nxt = [padded[half(h), columns_of(kb + n)] for n in range(3)]
            above = jnp.where(up < LANES, pick(here, up_in, 1), pick(nxt, up_in, 1))
            below = jnp.where(low >= 0, pick(here, low_in, 1), pick(prv, low_in, 1))
            target[d, half(h), tile(t)] = 0.5 * (above + below)
    for copy in copies[2:]:
        copy.wait()
    for target, d, t, kb in spots:
        back = jnp.full((ROWS, LANES), directions[kb], jnp.int32) == 1
        rate = jnp.broadcast_to(out_rate[:, columns_of(kb)], (ROWS, LANES))
        enters = jnp.broadcast_to(inflow[:, columns_of(kb)], (ROWS, LANES))
        speeds = [velocity[half(h), columns_of(kb)] for h in range(2)]
        reach, _, _ = scan_tile(back, [v * (1.0 / (v + rate)) for v in speeds], None)
        parts = [sum(past_residuals[j, half(h), columns_of(kb)] * reach[h] for h in range(2)) for j in range(HIST)]
        parts.append(sum(reach[h] * reach[h] for h in range(2)))
        parts.append(sum(reach[h] * padded[half(h), columns_of(kb + 1)] for h in range(2)))
        target[d, 2 * ROWS :, tile(t)] = jnp.where(row == 6, rate, jnp.where(row == 7, enters, added_rows(parts)))
    known = [directions[n] for n in range(tiles)] + [coupling[n] for n in range(coupling.shape[0])]
    for q in range(len(known) // ROWS):
        rows = jnp.zeros((ROWS, LANES), jnp.int32)
        for n in range(ROWS):
            rows = jnp.where(row == n, known[q * ROWS + n], rows)
        notes[half(q), :] = rows


def history_kernel(past_residuals, gram):
    tiles = past_residuals.shape[2] // LANES
    acc = [jnp.zeros((ROWS, LANES), jnp.float32) for _ in PAIRS]
    for kb in range(tiles):
        for h in range(2):
            past = [past_residuals[j, half(h), tile(kb)] for j in range(HIST)]
            for n, (i, j) in enumerate(PAIRS):
                acc[n] = acc[n] + past[i] * past[j]
    gram[...] = jnp.zeros(gram.shape, jnp.float32)
    for n in range(len(PAIRS)):
        gram[6 + n : 7 + n, :] = down(acc[n])


def at_contact(blocks, back, slope, inflow):
    row = iota(0)
    place = jnp.full((ROWS, LANES), lax.axis_index(POS), jnp.int32)
    first = (place == 0) & (row == 0) & jnp.logical_not(back)
    final = (place == blocks - 1) & (row == ROWS - 1) & back
    wide = jnp.broadcast_to(inflow, (ROWS, LANES))
    return [jnp.where(first, slope[0] * wide, 0.0), jnp.where(final, slope[1] * wide, 0.0)]


def fold_kernel(notes, velocity, *refs):
    chips = (len(refs) - 4) // 2
    held, message, own, other, across = refs[:chips], *refs[chips : chips + 3], refs[chips + 3 : -2]
    held = [held[0]] + [held[1 + FARTHEST_FIRST.index(d)] for d in range(1, chips)]
    ready, gone = refs[-2:]
    bands = 2 * chips
    blocks = message.shape[0]
    per = own.shape[1] // LANES
    row, lane = iota(0), iota(1)
    band = lax.axis_index(BAND)
    chosen = [
        jnp.broadcast_to(notes[pl.ds(blocks + (band ^ u), 1), :], (ROWS, LANES)) ^ jnp.full((ROWS, LANES), band, jnp.int32)
        for u in range(bands)
    ]
    out = [
        pltpu.make_async_copy(
            ready.at[pl.ds(kt * bands, bands)], message.at[pl.ds(kt * bands, bands)], gone.at[kt]
        )
        for kt in range(per)
    ]
    for kt in range(per):
        kb = band * per + kt
        back = flag(notes, kb)
        speeds = [velocity[half(h), columns_of(kb)] for h in range(2)]
        spread = [[held[u // 2][u % 2, half(h), tile(kt)] for h in range(2)] for u in range(bands)]
        parts = []
        for u in range(bands):
            tail = held[u // 2][u % 2, 2 * ROWS :, tile(kt)]
            rate = jnp.broadcast_to(tail[6:7], (ROWS, LANES))
            slope, offset = [], []
            for h in range(2):
                partner = spread[0][h]
                for t in range(1, bands):
                    partner = jnp.where(chosen[u] == t, spread[t][h], partner)
                pair = spread[u][h] + partner
                if u < 2:
                    (other if u else own)[half(h), tile(kt)] = pair
                else:
                    across[u // 2 - 1][u % 2, half(h), tile(kt)] = pair
                inv = 1.0 / (speeds[h] + rate)
                slope.append(speeds[h] * inv)
                offset.append(rate * 0.5 * pair * inv)
            edge = at_contact(blocks, back, slope, tail[7:8])
            offset = [offset[h] + edge[h] for h in range(2)]
            reach, run, ends = scan_tile(back, slope, offset)
            crossed = jnp.broadcast_to(down(reach[0] * run[0] + reach[1] * run[1]), (ROWS, LANES)) - tail
            parts.append(
                jnp.where(row == 5, crossed, jnp.where(row == 6, ends[0], jnp.where(row == 7, ends[1], tail)))
            )
        for bit in range(3):
            step = 1 << bit
            high = ((lane >> (4 + bit)) & 1) == 1
            swapped = list(parts)
            for u in range(bands):
                if not u & step:
                    swapped[u] = jnp.where(high, pltpu.roll(parts[u + step], GROUP * step, 1), parts[u])
                    swapped[u + step] = jnp.where(high, parts[u + step], pltpu.roll(parts[u], LANES - GROUP * step, 1))
            parts = swapped
        for g in range(bands):
            ready[kt * bands + g] = parts[g]
        out[kt].start()
    for copy in out:
        copy.wait()


def settle_kernel(plan, notes, *refs):
    shares = refs[:-9]
    velocity, out_rate, inflow, wigner, past_residuals, early, reach_out, rest, gram = refs[-9:]
    per = rest.shape[2] // LANES
    blocks = velocity.shape[1] // LANES
    band = lax.axis_index(BAND)
    acc = [jnp.zeros((ROWS, LANES), jnp.float32) for _ in range(HIST + 1)]
    for which, place, u in plan:
        d = u // 2
        source = shares[which] if len(shares[which].shape) == 2 else shares[which].at[place]
        for kt in range(per):
            kb = (band ^ u) * per + kt
            back = flag(notes, kb)
            columns = pl.ds(pl.multiple_of(kb * LANES, LANES), LANES)
            rate = jnp.broadcast_to(out_rate[:, columns], (ROWS, LANES))
            slope, offset = [], []
            for h in range(2):
                v = velocity[half(h), columns]
                inv = 1.0 / (v + rate)
                slope.append(v * inv)
                offset.append(rate * 0.5 * source[half(h), tile(kt)] * inv)
            edge = at_contact(blocks, back, slope, inflow[:, columns])
            offset = [offset[h] + edge[h] for h in range(2)]
            reach, run, _ = scan_tile(back, slope, offset)
            for h in range(2):
                left = run[h] - wigner[half(h), columns]
                rest[d, half(h), tile(kt)] = left
                reach_out[d, half(h), tile(kt)] = reach[h]
                for j in range(HIST):
                    acc[j] = acc[j] + past_residuals[j, half(h), columns] * left
                acc[HIST] = acc[HIST] + left * left
    gram[half(0), :] = early[half(0), :] + added_rows(acc)
    gram[half(1), :] = early[half(1), :]


def carry_kernel(notes, sums, carries, terms, forth, counter):
    blocks = sums.shape[0]
    row = iota(0)
    back = flag(notes, lax.axis_index(BAND) * (blocks // ROWS) + lax.axis_index(POS) // ROWS)
    acc = jnp.zeros((ROWS, LANES), jnp.float32)
    carry = jnp.zeros((1, LANES), jnp.float32)
    for step in range(blocks):
        part = jnp.where(back, sums[blocks - 1 - step], sums[step])
        wide = jnp.broadcast_to(carry, (ROWS, LANES))
        forth[step : step + 1, :] = carry
        counter[blocks - 1 - step : blocks - step, :] = carry
        acc = acc + part * jnp.where(row == 4, wide * wide, jnp.where(row == 5, 2.0 * wide, wide))
        carry = part[6:7] * carry + part[7:8]
    for q in range(blocks // ROWS):
        carries[half(q), :] = jnp.where(back, counter[half(q), :], forth[half(q), :])
    terms[...] = jnp.where(row < 6, acc, 0.0)


def message_kernel(carries, terms, gram, message):
    blocks = carries.shape[0]
    row, lane = iota(0), iota(1)
    whole = [gram[half(0), :] + terms[...], gram[half(1), :]]
    line = jnp.zeros((ROWS, LANES), jnp.float32)
    for h in range(2):
        total = jnp.broadcast_to(jnp.sum(whole[h], axis=1, keepdims=True), (ROWS, LANES))
        line = line + jnp.where(lane == GROUP + h * ROWS + row, total, 0.0)
    line = jnp.broadcast_to(down(line), (ROWS, LANES))
    band = lax.axis_index(BAND)
    for q in range(blocks // ROWS):
        for u in range(LANES // GROUP):
            turned = pltpu.roll(carries[half(q), :], LANES - GROUP * u, 1) if u else carries[half(q), :]
            start = pl.multiple_of((band ^ u) * blocks + q * ROWS, ROWS)
            message[pl.ds(start, ROWS), :] = jnp.where(lane < GROUP, turned, line)


def mixing_weights(entry):
    count = HIST + 1
    scale = sum(entry(i, i) for i in range(count)) / count
    factor = {}
    for i in range(count):
        for j in range(i + 1):
            value = entry(j, i)
            if i == j:
                value = value + RIDGE_SCALE * scale
            for k in range(j):
                value = value - factor[i, k] * factor[j, k]
            factor[i, j] = jnp.sqrt(value) if i == j else value / factor[j, j]
    forward = []
    for row in range(count):
        partial = jnp.ones_like(scale)
        for inner in range(row):
            partial = partial - factor[row, inner] * forward[inner]
        forward.append(partial / factor[row, row])
    backward = [None] * count
    for row in reversed(range(count)):
        partial = forward[row]
        for inner in range(row + 1, count):
            partial = partial - factor[inner, row] * backward[inner]
        backward[row] = partial / factor[row, row]
    total = sum(backward)
    return [z / total for z in backward]


def finish_kernel(message, *refs):
    reach, rest = (refs[0], refs[2]), (refs[1], refs[3])
    wigner, past_iterates, past_residuals, residual, mixed, found, mixes, gone = refs[4:]
    cells, moments = wigner.shape
    chips, _, share = rest[0].shape
    per = share // LANES
    band = lax.axis_index(BAND)
    tiles = moments // LANES
    pieces = 4
    row, lane = iota(0), iota(1)
    out = []
    for n, (source, target) in enumerate(((found, residual), (mixes, mixed))):
        for q in range(pieces):
            columns = pl.ds(q * (moments // pieces), moments // pieces)
            out.append(pltpu.make_async_copy(source.at[:, columns], target.at[:, columns], gone.at[n * pieces + q]))
    total = message[half(0), :]
    for kb in range(1, tiles):
        total = total + message[half(kb), :]
    total = jnp.broadcast_to(down(total), (ROWS, LANES))

    def term(n):
        return pick(total, jnp.full((ROWS, LANES), GROUP + n, jnp.int32), 1)

    def entry(i, j):
        if j == HIST:
            return term(4) + term(5) if i == HIST else term(i)
        return term(6 + PAIRS.index((i, j)))

    for d in range(2 * chips):
        for kt in range(per):
            kb = (band ^ d) * per + kt
            rows = message[pl.ds(pl.multiple_of(kb * ROWS, ROWS), ROWS), :]
            spots = pick(rows, lane & (GROUP - 1), 1)
            carry = jnp.broadcast_to(down(jnp.where((lane >> 4) == row, spots, 0.0)), (ROWS, LANES))
            for h in range(2):
                at = (d // 2, half(h), tile(kt))
                found[half(h), pl.ds(pl.multiple_of(kb * LANES, LANES), LANES)] = rest[d % 2][at] + reach[d % 2][at] * carry
    for copy in out[:pieces]:
        copy.start()
    weights = mixing_weights(entry)
    for kb in range(tiles):
        for h in range(2):
            value = weights[HIST] * (wigner[half(h), tile(kb)] + MIX_STEP * found[half(h), tile(kb)])
            for j in range(HIST):
                earlier = past_iterates[j, half(h), tile(kb)] + MIX_STEP * past_residuals[j, half(h), tile(kb)]
                value = value + weights[j] * earlier
            mixes[half(h), tile(kb)] = value
        if (kb + 1) % (tiles // pieces) == 0:
            out[pieces + kb // (tiles // pieces)].start()
    for copy in out:
        copy.wait()


def body(wigner, past_iterates, past_residuals, velocity, out_rate, inflow, offsets, directions, coupling):
    _, cells, moments = wigner.shape
    bands = lax.axis_size(BAND)
    blocks = lax.axis_size(POS)
    wigner = wigner.reshape(cells, moments)
    past_iterates = past_iterates.reshape(HIST, cells, moments)
    past_residuals = past_residuals.reshape(HIST, cells, moments)
    offsets = offsets.reshape(1, moments)
    size = 4 * cells * moments
    share = moments // bands
    field = f32(cells, moments)
    dma = pltpu.SemaphoreType.DMA

    chips = lax.axis_size(BAND[0])

    def to_core(x):
        return lax.ppermute(x, BAND[1], [(0, 1), (1, 0)])

    def to_chip(x, d):
        return lax.ppermute(x, BAND[0], [(i, i ^ d) for i in range(chips)])

    sources = (offsets, wigner, directions, coupling, velocity, out_rate, inflow, past_residuals)
    opened = f32(chips, cells + ROWS, share)
    own, other, notes = call(
        open_kernel,
        (opened, opened, jax.ShapeDtypeStruct((blocks + bands, LANES), jnp.int32)),
        [HBM] * 8,
        20 * size,
        8 * size,
        [
            pltpu.SMEM(x.shape, x.dtype)
            if x.ndim == 1
            else pltpu.VMEM((cells, moments + 2 * LANES) if x is wigner else x.shape, x.dtype)
            for x in sources
        ]
        + [dma((8,))],
    )(*[pltpu.with_memory_space_constraint(x, pltpu.HBM) for x in sources])
    other = to_core(other)
    held = [jnp.stack([own[d], other[d]]) for d in range(chips)]
    held = [held[0]] + [to_chip(held[d], d) for d in FARTHEST_FIRST]
    early = call(history_kernel, f32(16, LANES), [VMEM], 8 * size, 4 * size)(past_residuals)
    *held, early = lax.optimization_barrier((*held, early))
    pair = f32(2, cells, share)
    sums, own, other, *across = call(
        fold_kernel,
        (f32(blocks, ROWS, LANES), f32(cells, share), f32(cells, share)) + (pair,) * (chips - 1),
        [VMEM] * (chips + 2),
        20 * size,
        5 * size,
        [pltpu.VMEM((blocks, ROWS, LANES), jnp.float32), dma((4,))],
        out_specs=(HBM,) + (VMEM,) * (chips + 1),
    )(notes, velocity, *held)
    sums = lax.all_to_all(sums, POS, 0, 0, tiled=True)
    across = [to_chip(across[d - 1], d) for d in range(1, chips)]
    other = [other] + [x[1] for x in across]
    groups = [[0, 2, 3], [1]]
    others = [to_core(jnp.stack([other[d] for d in group])) for group in groups]
    local = (velocity, out_rate, inflow, wigner, past_residuals)
    part = f32(chips, cells, share)
    settled = []
    gram = early
    plans = [(n, 0, 2 * n) for n in range(chips)], [(n, m, 2 * d + 1) for n, g in enumerate(groups) for m, d in enumerate(g)]
    for plan, shares in zip(plans, ((own, *across), others)):
        reach, rest, gram = call(
            functools.partial(settle_kernel, plan),
            (part, part, f32(16, LANES)),
            [VMEM] * (len(shares) + 7),
            size // 64,
            size // 64,
        )(notes, *shares, *local, gram)
        settled += [reach, rest]
    carries, terms = call(
        carry_kernel,
        (f32(blocks, LANES), f32(ROWS, LANES)),
        [VMEM] * 2,
        size,
        256 * size,
        [pltpu.VMEM((blocks, LANES), jnp.float32)] * 2,
    )(notes, sums)
    message = call(message_kernel, f32(bands * blocks, LANES), [VMEM] * 3, size, size)(carries, terms, gram)
    message = lax.all_to_all(message, ALL, 0, 0, tiled=True)
    residual, mixed = call(
        finish_kernel,
        (field, field),
        [VMEM] * 8,
        8 * size,
        14 * size,
        [pltpu.VMEM((cells, moments), jnp.float32)] * 2 + [dma((8,))],
        out_specs=(HBM, HBM),
    )(message, *settled, wigner, past_iterates, past_residuals)
    return mixed[None], residual[None]


def solution(mesh):
    finer = Mesh(mesh.devices.reshape(4, 2, 4, 8), ("band_0", "band_1", "pos_0", "pos_1"))
    in_specs = (
        P(BAND, POS, None),
        P(None, BAND, POS, None),
        P(None, BAND, POS, None),
        P(POS, None),
        P(BAND, None),
        P(BAND, None),
        P(),
        P(),
        P(),
    )
    out_specs = (P(BAND, POS, None), P(BAND, POS, None))
    return jax.shard_map(body, mesh=finer, in_specs=in_specs, out_specs=out_specs, check_vma=False)
```

```python
import functools

import jax
import jax.numpy as jnp
from jax import lax
from jax.experimental import pallas as pl
from jax.experimental.pallas import tpu as pltpu
from jax.sharding import Mesh
from jax.sharding import PartitionSpec as P

POS = ("pos_0", "pos_1")
BAND = ("band_0", "band_1")
ALL = BAND + POS

MIX_STEP = 0.5
RIDGE_SCALE = 0.0001
LANES = 128
GROUP = 16
ROWS = 8
HIST = 4
PAIRS = [(i, j) for i in range(HIST) for j in range(i, HIST)]

VMEM = pl.BlockSpec(memory_space=pltpu.VMEM)
HBM = pl.BlockSpec(memory_space=pltpu.HBM)


def call(kernel, outs, in_specs, flops, nbytes, scratch=(), mib=24, out_specs=None):
    return pl.pallas_call(
        kernel,
        out_shape=outs,
        in_specs=in_specs,
        out_specs=jax.tree.map(lambda _: VMEM, outs) if out_specs is None else out_specs,
        scratch_shapes=list(scratch),
        compiler_params=pltpu.CompilerParams(vmem_limit_bytes=mib * 2**20),
        cost_estimate=pl.CostEstimate(flops=flops, bytes_accessed=nbytes, transcendentals=0),
    )


def f32(*shape):
    return jax.ShapeDtypeStruct(shape, jnp.float32)


def tile(kb):
    return slice(kb * LANES, (kb + 1) * LANES)


def pick(x, index, axis):
    return jnp.take_along_axis(x, index, axis=axis, mode="promise_in_bounds")


def iota(axis):
    return lax.broadcasted_iota(jnp.int32, (ROWS, LANES), axis)


def scan_tile(back, a, b):
    row = iota(0)
    away = jnp.where(back, ROWS - 1 - row, row)
    a = [jnp.where(back, a[1], a[0]), jnp.where(back, a[0], a[1])]
    if b is not None:
        b = [jnp.where(back, b[1], b[0]), jnp.where(back, b[0], b[1])]
    for d in (1, 2, 4):
        source = jnp.where(back, row + d, row - d) & (ROWS - 1)
        keep = away >= d
        for h in range(2):
            if b is not None:
                b[h] = a[h] * jnp.where(keep, pick(b[h], source, 0), 0.0) + b[h]
            a[h] = a[h] * jnp.where(keep, pick(a[h], source, 0), 1.0)
    last = jnp.where(back, 0, ROWS - 1) + jnp.zeros_like(row)
    if b is not None:
        b[1] = a[1] * pick(b[0], last, 0) + b[1]
    a[1] = a[1] * pick(a[0], last, 0)
    ends = [pick(a[1], last, 0)]
    if b is not None:
        ends.append(pick(b[1], last, 0))
        b = [jnp.where(back, b[1], b[0]), jnp.where(back, b[0], b[1])]
    a = [jnp.where(back, a[1], a[0]), jnp.where(back, a[0], a[1])]
    return a, b, ends


def flag(notes, index):
    return jnp.broadcast_to(notes[pl.ds(index, 1), :], (ROWS, LANES)) == 1


def down(x):
    return jnp.sum(x, axis=0, keepdims=True)


def half(h):
    return slice(h * ROWS, (h + 1) * ROWS)


def added_rows(parts):
    row = iota(0)
    parts = parts + [jnp.zeros((ROWS, LANES), jnp.float32)] * (ROWS - len(parts))
    for d in (4, 2, 1):
        low = (row & d) == 0
        count = len(parts) // 2
        parts = [
            jnp.where(low, parts[n], parts[n + count])
            + pick(jnp.where(low, parts[n + count], parts[n]), row ^ d, 0)
            for n in range(count)
        ]
    return parts[0]


def columns_of(kb):
    return pl.ds(pl.multiple_of(kb * LANES, LANES), LANES)


def open_kernel(*refs):
    sources, own, other, notes, held, arrived = refs[:8], refs[8], refs[9], refs[10], refs[11:19], refs[19]
    offsets, padded, directions, coupling, velocity, out_rate, inflow, past_residuals = held
    moments = offsets.shape[1]
    tiles = moments // LANES
    chips, _, share = own.shape
    per = share // LANES
    places = [padded.at[:, pl.ds(LANES, moments)] if ref is padded else ref for ref in held]
    copies = [pltpu.make_async_copy(a, b, arrived.at[n]) for n, (a, b) in enumerate(zip(sources, places))]
    for copy in copies:
        copy.start()
    band = lax.axis_index(BAND)
    row, lane = iota(0), iota(1)
    for kb in (0, tiles + 1):
        padded[:, tile(kb)] = jnp.zeros((2 * ROWS, LANES), jnp.float32)
    spots = [
        (target, d, t, (band ^ (2 * d + core)) * per + t)
        for core, target in ((1, other), (0, own))
        for d in range(chips)
        for t in range(per)
    ]
    copies[0].wait()
    copies[1].wait()
    for target, d, t, kb in spots:
        off = jnp.broadcast_to(offsets[:, columns_of(kb)], (ROWS, LANES))
        up, low = lane + off, lane - off
        up_in, low_in = up & (LANES - 1), low & (LANES - 1)
        for h in range(2):
            prv, here, nxt = [padded[half(h), columns_of(kb + n)] for n in range(3)]
            above = jnp.where(up < LANES, pick(here, up_in, 1), pick(nxt, up_in, 1))
            below = jnp.where(low >= 0, pick(here, low_in, 1), pick(prv, low_in, 1))
            target[d, half(h), tile(t)] = 0.5 * (above + below)
    for copy in copies[2:]:
        copy.wait()
    for target, d, t, kb in spots:
        back = jnp.full((ROWS, LANES), directions[kb], jnp.int32) == 1
        rate = jnp.broadcast_to(out_rate[:, columns_of(kb)], (ROWS, LANES))
        enters = jnp.broadcast_to(inflow[:, columns_of(kb)], (ROWS, LANES))
        speeds = [velocity[half(h), columns_of(kb)] for h in range(2)]
        reach, _, _ = scan_tile(back, [v * (1.0 / (v + rate)) for v in speeds], None)
        parts = [sum(past_residuals[j, half(h), columns_of(kb)] * reach[h] for h in range(2)) for j in range(HIST)]
        parts.append(sum(reach[h] * reach[h] for h in range(2)))
        parts.append(sum(reach[h] * padded[half(h), columns_of(kb + 1)] for h in range(2)))
        target[d, 2 * ROWS :, tile(t)] = jnp.where(row == 6, rate, jnp.where(row == 7, enters, added_rows(parts)))
    known = [directions[n] for n in range(tiles)] + [coupling[n] for n in range(coupling.shape[0])]
    for q in range(len(known) // ROWS):
        rows = jnp.zeros((ROWS, LANES), jnp.int32)
        for n in range(ROWS):
            rows = jnp.where(row == n, known[q * ROWS + n], rows)
        notes[half(q), :] = rows


def history_kernel(past_residuals, gram):
    tiles = past_residuals.shape[2] // LANES
    acc = [jnp.zeros((ROWS, LANES), jnp.float32) for _ in PAIRS]
    for kb in range(tiles):
        for h in range(2):
            past = [past_residuals[j, half(h), tile(kb)] for j in range(HIST)]
            for n, (i, j) in enumerate(PAIRS):
                acc[n] = acc[n] + past[i] * past[j]
    gram[...] = jnp.zeros(gram.shape, jnp.float32)
    for n in range(len(PAIRS)):
        gram[6 + n : 7 + n, :] = down(acc[n])


def at_contact(blocks, back, slope, inflow):
    row = iota(0)
    place = jnp.full((ROWS, LANES), lax.axis_index(POS), jnp.int32)
    first = (place == 0) & (row == 0) & jnp.logical_not(back)
    final = (place == blocks - 1) & (row == ROWS - 1) & back
    wide = jnp.broadcast_to(inflow, (ROWS, LANES))
    return [jnp.where(first, slope[0] * wide, 0.0), jnp.where(final, slope[1] * wide, 0.0)]


def fold_kernel(notes, velocity, *refs):
    chips = (len(refs) - 4) // 2
    held, message, own, other, across = refs[:chips], *refs[chips : chips + 3], refs[chips + 3 : -2]
    ready, gone = refs[-2:]
    bands = 2 * chips
    blocks = message.shape[0]
    per = own.shape[1] // LANES
    row, lane = iota(0), iota(1)
    band = lax.axis_index(BAND)
    chosen = [
        jnp.broadcast_to(notes[pl.ds(blocks + (band ^ u), 1), :], (ROWS, LANES)) ^ jnp.full((ROWS, LANES), band, jnp.int32)
        for u in range(bands)
    ]
    out = [
        pltpu.make_async_copy(
            ready.at[pl.ds(kt * bands, bands)], message.at[pl.ds(kt * bands, bands)], gone.at[kt]
        )
        for kt in range(per)
    ]
    for kt in range(per):
        kb = band * per + kt
        back = flag(notes, kb)
        speeds = [velocity[half(h), columns_of(kb)] for h in range(2)]
        spread = [[held[u // 2][u % 2, half(h), tile(kt)] for h in range(2)] for u in range(bands)]
        parts = []
        for u in range(bands):
            tail = held[u // 2][u % 2, 2 * ROWS :, tile(kt)]
            rate = jnp.broadcast_to(tail[6:7], (ROWS, LANES))
            slope, offset = [], []
            for h in range(2):
                partner = spread[0][h]
                for t in range(1, bands):
                    partner = jnp.where(chosen[u] == t, spread[t][h], partner)
                pair = spread[u][h] + partner
                if u < 2:
                    (other if u else own)[half(h), tile(kt)] = pair
                else:
                    across[u // 2 - 1][u % 2, half(h), tile(kt)] = pair
                inv = 1.0 / (speeds[h] + rate)
                slope.append(speeds[h] * inv)
                offset.append(rate * 0.5 * pair * inv)
            edge = at_contact(blocks, back, slope, tail[7:8])
            offset = [offset[h] + edge[h] for h in range(2)]
            reach, run, ends = scan_tile(back, slope, offset)
            crossed = jnp.broadcast_to(down(reach[0] * run[0] + reach[1] * run[1]), (ROWS, LANES)) - tail
            parts.append(
                jnp.where(row == 5, crossed, jnp.where(row == 6, ends[0], jnp.where(row == 7, ends[1], tail)))
            )
        for bit in range(3):
            step = 1 << bit
            high = ((lane >> (4 + bit)) & 1) == 1
            swapped = list(parts)
            for u in range(bands):
                if not u & step:
                    swapped[u] = jnp.where(high, pltpu.roll(parts[u + step], GROUP * step, 1), parts[u])
                    swapped[u + step] = jnp.where(high, parts[u + step], pltpu.roll(parts[u], LANES - GROUP * step, 1))
            parts = swapped
        for g in range(bands):
            ready[kt * bands + g] = parts[g]
        out[kt].start()
    for copy in out:
        copy.wait()


def settle_kernel(plan, notes, *refs):
    shares = refs[:-9]
    velocity, out_rate, inflow, wigner, past_residuals, early, reach_out, rest, gram = refs[-9:]
    per = rest.shape[2] // LANES
    blocks = velocity.shape[1] // LANES
    band = lax.axis_index(BAND)
    acc = [jnp.zeros((ROWS, LANES), jnp.float32) for _ in range(HIST + 1)]
    for which, place, u in plan:
        d = u // 2
        source = shares[which] if len(shares[which].shape) == 2 else shares[which].at[place]
        for kt in range(per):
            kb = (band ^ u) * per + kt
            back = flag(notes, kb)
            columns = pl.ds(pl.multiple_of(kb * LANES, LANES), LANES)
            rate = jnp.broadcast_to(out_rate[:, columns], (ROWS, LANES))
            slope, offset = [], []
            for h in range(2):
                v = velocity[half(h), columns]
                inv = 1.0 / (v + rate)
                slope.append(v * inv)
                offset.append(rate * 0.5 * source[half(h), tile(kt)] * inv)
            edge = at_contact(blocks, back, slope, inflow[:, columns])
            offset = [offset[h] + edge[h] for h in range(2)]
            reach, run, _ = scan_tile(back, slope, offset)
            for h in range(2):
                left = run[h] - wigner[half(h), columns]
                rest[d, half(h), tile(kt)] = left
                reach_out[d, half(h), tile(kt)] = reach[h]
                for j in range(HIST):
                    acc[j] = acc[j] + past_residuals[j, half(h), columns] * left
                acc[HIST] = acc[HIST] + left * left
    gram[half(0), :] = early[half(0), :] + added_rows(acc)
    gram[half(1), :] = early[half(1), :]


def carry_kernel(notes, sums, carries, terms, forth, counter):
    blocks = sums.shape[0]
    row = iota(0)
    back = flag(notes, lax.axis_index(BAND) * (blocks // ROWS) + lax.axis_index(POS) // ROWS)
    acc = jnp.zeros((ROWS, LANES), jnp.float32)
    carry = jnp.zeros((1, LANES), jnp.float32)
    for step in range(blocks):
        part = jnp.where(back, sums[blocks - 1 - step], sums[step])
        wide = jnp.broadcast_to(carry, (ROWS, LANES))
        forth[step : step + 1, :] = carry
        counter[blocks - 1 - step : blocks - step, :] = carry
        acc = acc + part * jnp.where(row == 4, wide * wide, jnp.where(row == 5, 2.0 * wide, wide))
        carry = part[6:7] * carry + part[7:8]
    for q in range(blocks // ROWS):
        carries[half(q), :] = jnp.where(back, counter[half(q), :], forth[half(q), :])
    terms[...] = jnp.where(row < 6, acc, 0.0)


def message_kernel(carries, terms, gram, message):
    blocks = carries.shape[0]
    row, lane = iota(0), iota(1)
    whole = [gram[half(0), :] + terms[...], gram[half(1), :]]
    line = jnp.zeros((ROWS, LANES), jnp.float32)
    for h in range(2):
        total = jnp.broadcast_to(jnp.sum(whole[h], axis=1, keepdims=True), (ROWS, LANES))
        line = line + jnp.where(lane == GROUP + h * ROWS + row, total, 0.0)
    line = jnp.broadcast_to(down(line), (ROWS, LANES))
    band = lax.axis_index(BAND)
    for q in range(blocks // ROWS):
        for u in range(LANES // GROUP):
            turned = pltpu.roll(carries[half(q), :], LANES - GROUP * u, 1) if u else carries[half(q), :]
            start = pl.multiple_of((band ^ u) * blocks + q * ROWS, ROWS)
            message[pl.ds(start, ROWS), :] = jnp.where(lane < GROUP, turned, line)


def mixing_weights(entry):
    count = HIST + 1
    scale = sum(entry(i, i) for i in range(count)) / count
    factor = {}
    for i in range(count):
        for j in range(i + 1):
            value = entry(j, i)
            if i == j:
                value = value + RIDGE_SCALE * scale
            for k in range(j):
                value = value - factor[i, k] * factor[j, k]
            factor[i, j] = jnp.sqrt(value) if i == j else value / factor[j, j]
    forward = []
    for row in range(count):
        partial = jnp.ones_like(scale)
        for inner in range(row):
            partial = partial - factor[row, inner] * forward[inner]
        forward.append(partial / factor[row, row])
    backward = [None] * count
    for row in reversed(range(count)):
        partial = forward[row]
        for inner in range(row + 1, count):
            partial = partial - factor[inner, row] * backward[inner]
        backward[row] = partial / factor[row, row]
    total = sum(backward)
    return [z / total for z in backward]


def finish_kernel(message, *refs):
    reach, rest = (refs[0], refs[2]), (refs[1], refs[3])
    wigner, past_iterates, past_residuals, residual, mixed, found, mixes, gone = refs[4:]
    cells, moments = wigner.shape
    chips, _, share = rest[0].shape
    per = share // LANES
    band = lax.axis_index(BAND)
    tiles = moments // LANES
    pieces = 4
    row, lane = iota(0), iota(1)
    out = []
    for n, (source, target) in enumerate(((found, residual), (mixes, mixed))):
        for q in range(pieces):
            columns = pl.ds(q * (moments // pieces), moments // pieces)
            out.append(pltpu.make_async_copy(source.at[:, columns], target.at[:, columns], gone.at[n * pieces + q]))
    total = message[half(0), :]
    for kb in range(1, tiles):
        total = total + message[half(kb), :]
    total = jnp.broadcast_to(down(total), (ROWS, LANES))

    def term(n):
        return pick(total, jnp.full((ROWS, LANES), GROUP + n, jnp.int32), 1)

    def entry(i, j):
        if j == HIST:
            return term(4) + term(5) if i == HIST else term(i)
        return term(6 + PAIRS.index((i, j)))

    for d in range(2 * chips):
        for kt in range(per):
            kb = (band ^ d) * per + kt
            rows = message[pl.ds(pl.multiple_of(kb * ROWS, ROWS), ROWS), :]
            spots = pick(rows, lane & (GROUP - 1), 1)
            carry = jnp.broadcast_to(down(jnp.where((lane >> 4) == row, spots, 0.0)), (ROWS, LANES))
            for h in range(2):
                at = (d // 2, half(h), tile(kt))
                found[half(h), pl.ds(pl.multiple_of(kb * LANES, LANES), LANES)] = rest[d % 2][at] + reach[d % 2][at] * carry
    for copy in out[:pieces]:
        copy.start()
    weights = mixing_weights(entry)
    for kb in range(tiles):
        for h in range(2):
            value = weights[HIST] * (wigner[half(h), tile(kb)] + MIX_STEP * found[half(h), tile(kb)])
            for j in range(HIST):
                earlier = past_iterates[j, half(h), tile(kb)] + MIX_STEP * past_residuals[j, half(h), tile(kb)]
                value = value + weights[j] * earlier
            mixes[half(h), tile(kb)] = value
        if (kb + 1) % (tiles // pieces) == 0:
            out[pieces + kb // (tiles // pieces)].start()
    for copy in out:
        copy.wait()


def body(wigner, past_iterates, past_residuals, velocity, out_rate, inflow, offsets, directions, coupling):
    _, cells, moments = wigner.shape
    bands = lax.axis_size(BAND)
    blocks = lax.axis_size(POS)
    wigner = wigner.reshape(cells, moments)
    past_iterates = past_iterates.reshape(HIST, cells, moments)
    past_residuals = past_residuals.reshape(HIST, cells, moments)
    offsets = offsets.reshape(1, moments)
    size = 4 * cells * moments
    share = moments // bands
    field = f32(cells, moments)
    dma = pltpu.SemaphoreType.DMA

    chips = lax.axis_size(BAND[0])

    def to_core(x):
        return lax.ppermute(x, BAND[1], [(0, 1), (1, 0)])

    def to_chip(x, d):
        return lax.ppermute(x, BAND[0], [(i, i ^ d) for i in range(chips)])

    sources = (offsets, wigner, directions, coupling, velocity, out_rate, inflow, past_residuals)
    opened = f32(chips, cells + ROWS, share)
    own, other, notes = call(
        open_kernel,
        (opened, opened, jax.ShapeDtypeStruct((blocks + bands, LANES), jnp.int32)),
        [HBM] * 8,
        20 * size,
        8 * size,
        [
            pltpu.SMEM(x.shape, x.dtype)
            if x.ndim == 1
            else pltpu.VMEM((cells, moments + 2 * LANES) if x is wigner else x.shape, x.dtype)
            for x in sources
        ]
        + [dma((8,))],
    )(*[pltpu.with_memory_space_constraint(x, pltpu.HBM) for x in sources])
    other = to_core(other)
    held = [jnp.stack([own[d], other[d]]) for d in range(chips)]
    held = held[:1] + [to_chip(held[d], d) for d in range(1, chips)]
    early = call(history_kernel, f32(16, LANES), [VMEM], 8 * size, 4 * size)(past_residuals)
    *held, early = lax.optimization_barrier((*held, early))
    pair = f32(2, cells, share)
    sums, own, other, *across = call(
        fold_kernel,
        (f32(blocks, ROWS, LANES), f32(cells, share), f32(cells, share)) + (pair,) * (chips - 1),
        [VMEM] * (chips + 2),
        20 * size,
        5 * size,
        [pltpu.VMEM((blocks, ROWS, LANES), jnp.float32), dma((4,))],
        out_specs=(HBM,) + (VMEM,) * (chips + 1),
    )(notes, velocity, *held)
    sums = lax.all_to_all(sums, POS, 0, 0, tiled=True)
    across = [to_chip(across[d - 1], d) for d in range(1, chips)]
    other = [other] + [x[1] for x in across]
    groups = [[0, 1, 2], [3]]
    others = [to_core(jnp.stack([other[d] for d in group])) for group in groups]
    local = (velocity, out_rate, inflow, wigner, past_residuals)
    part = f32(chips, cells, share)
    settled = []
    gram = early
    plans = [(n, 0, 2 * n) for n in range(chips)], [(n, m, 2 * d + 1) for n, g in enumerate(groups) for m, d in enumerate(g)]
    for plan, shares in zip(plans, ((own, *across), others)):
        reach, rest, gram = call(
            functools.partial(settle_kernel, plan),
            (part, part, f32(16, LANES)),
            [VMEM] * (len(shares) + 7),
            size // 64,
            size // 64,
        )(notes, *shares, *local, gram)
        settled += [reach, rest]
    carries, terms = call(
        carry_kernel,
        (f32(blocks, LANES), f32(ROWS, LANES)),
        [VMEM] * 2,
        size,
        256 * size,
        [pltpu.VMEM((blocks, LANES), jnp.float32)] * 2,
    )(notes, sums)
    message = call(message_kernel, f32(bands * blocks, LANES), [VMEM] * 3, size, size)(carries, terms, gram)
    message = lax.all_to_all(message, ALL, 0, 0, tiled=True)
    residual, mixed = call(
        finish_kernel,
        (field, field),
        [VMEM] * 8,
        8 * size,
        14 * size,
        [pltpu.VMEM((cells, moments), jnp.float32)] * 2 + [dma((8,))],
        out_specs=(HBM, HBM),
    )(message, *settled, wigner, past_iterates, past_residuals)
    return mixed[None], residual[None]


def solution(mesh):
    finer = Mesh(mesh.devices.reshape(4, 2, 4, 8), ("band_0", "band_1", "pos_0", "pos_1"))
    in_specs = (
        P(BAND, POS, None),
        P(None, BAND, POS, None),
        P(None, BAND, POS, None),
        P(POS, None),
        P(BAND, None),
        P(BAND, None),
        P(),
        P(),
        P(),
    )
    out_specs = (P(BAND, POS, None), P(BAND, POS, None))
    return jax.shard_map(body, mesh=finer, in_specs=in_specs, out_specs=out_specs, check_vma=False)
```

```python
import functools

import jax
import jax.numpy as jnp
from jax import lax
from jax.experimental import pallas as pl
from jax.experimental.pallas import tpu as pltpu
from jax.sharding import Mesh
from jax.sharding import PartitionSpec as P

POS = ("pos_0", "pos_1")
BAND = ("band_0", "band_1")
ALL = BAND + POS

MIX_STEP = 0.5
RIDGE_SCALE = 0.0001
LANES = 128
GROUP = 16
ROWS = 8
HIST = 4
PAIRS = [(i, j) for i in range(HIST) for j in range(i, HIST)]

VMEM = pl.BlockSpec(memory_space=pltpu.VMEM)
HBM = pl.BlockSpec(memory_space=pltpu.HBM)


def call(kernel, outs, in_specs, flops, nbytes, scratch=(), mib=24, out_specs=None):
    return pl.pallas_call(
        kernel,
        out_shape=outs,
        in_specs=in_specs,
        out_specs=jax.tree.map(lambda _: VMEM, outs) if out_specs is None else out_specs,
        scratch_shapes=list(scratch),
        compiler_params=pltpu.CompilerParams(vmem_limit_bytes=mib * 2**20),
        cost_estimate=pl.CostEstimate(flops=flops, bytes_accessed=nbytes, transcendentals=0),
    )


def f32(*shape):
    return jax.ShapeDtypeStruct(shape, jnp.float32)


def tile(kb):
    return slice(kb * LANES, (kb + 1) * LANES)


def pick(x, index, axis):
    return jnp.take_along_axis(x, index, axis=axis, mode="promise_in_bounds")


def iota(axis):
    return lax.broadcasted_iota(jnp.int32, (ROWS, LANES), axis)


def scan_tile(back, a, b):
    row = iota(0)
    away = jnp.where(back, ROWS - 1 - row, row)
    a = [jnp.where(back, a[1], a[0]), jnp.where(back, a[0], a[1])]
    if b is not None:
        b = [jnp.where(back, b[1], b[0]), jnp.where(back, b[0], b[1])]
    for d in (1, 2, 4):
        source = jnp.where(back, row + d, row - d) & (ROWS - 1)
        keep = away >= d
        for h in range(2):
            if b is not None:
                b[h] = a[h] * jnp.where(keep, pick(b[h], source, 0), 0.0) + b[h]
            a[h] = a[h] * jnp.where(keep, pick(a[h], source, 0), 1.0)
    last = jnp.where(back, 0, ROWS - 1) + jnp.zeros_like(row)
    if b is not None:
        b[1] = a[1] * pick(b[0], last, 0) + b[1]
    a[1] = a[1] * pick(a[0], last, 0)
    ends = [pick(a[1], last, 0)]
    if b is not None:
        ends.append(pick(b[1], last, 0))
        b = [jnp.where(back, b[1], b[0]), jnp.where(back, b[0], b[1])]
    a = [jnp.where(back, a[1], a[0]), jnp.where(back, a[0], a[1])]
    return a, b, ends


def flag(notes, index):
    return jnp.broadcast_to(notes[pl.ds(index, 1), :], (ROWS, LANES)) == 1


def down(x):
    return jnp.sum(x, axis=0, keepdims=True)


def half(h):
    return slice(h * ROWS, (h + 1) * ROWS)


def added_rows(parts):
    row = iota(0)
    parts = parts + [jnp.zeros((ROWS, LANES), jnp.float32)] * (ROWS - len(parts))
    for d in (4, 2, 1):
        low = (row & d) == 0
        count = len(parts) // 2
        parts = [
            jnp.where(low, parts[n], parts[n + count])
            + pick(jnp.where(low, parts[n + count], parts[n]), row ^ d, 0)
            for n in range(count)
        ]
    return parts[0]


def columns_of(kb):
    return pl.ds(pl.multiple_of(kb * LANES, LANES), LANES)


def open_kernel(*refs):
    sources, own, other, notes, held, arrived = refs[:8], refs[8], refs[9], refs[10], refs[11:19], refs[19]
    offsets, padded, directions, coupling, velocity, out_rate, inflow, past_residuals = held
    moments = offsets.shape[1]
    tiles = moments // LANES
    chips, _, share = own.shape
    per = share // LANES
    places = [padded.at[:, pl.ds(LANES, moments)] if ref is padded else ref for ref in held]
    copies = [pltpu.make_async_copy(a, b, arrived.at[n]) for n, (a, b) in enumerate(zip(sources, places))]
    for copy in copies:
        copy.start()
    band = lax.axis_index(BAND)
    row, lane = iota(0), iota(1)
    for kb in (0, tiles + 1):
        padded[:, tile(kb)] = jnp.zeros((2 * ROWS, LANES), jnp.float32)
    spots = [
        (target, d, t, (band ^ (2 * d + core)) * per + t)
        for core, target in ((1, other), (0, own))
        for d in range(chips)
        for t in range(per)
    ]
    copies[0].wait()
    copies[1].wait()
    for target, d, t, kb in spots:
        off = jnp.broadcast_to(offsets[:, columns_of(kb)], (ROWS, LANES))
        up, low = lane + off, lane - off
        up_in, low_in = up & (LANES - 1), low & (LANES - 1)
        for h in range(2):
            prv, here, nxt = [padded[half(h), columns_of(kb + n)] for n in range(3)]
            above = jnp.where(up < LANES, pick(here, up_in, 1), pick(nxt, up_in, 1))
            below = jnp.where(low >= 0, pick(here, low_in, 1), pick(prv, low_in, 1))
            target[d, half(h), tile(t)] = 0.5 * (above + below)
    for copy in copies[2:]:
        copy.wait()
    for target, d, t, kb in spots:
        back = jnp.full((ROWS, LANES), directions[kb], jnp.int32) == 1
        rate = jnp.broadcast_to(out_rate[:, columns_of(kb)], (ROWS, LANES))
        enters = jnp.broadcast_to(inflow[:, columns_of(kb)], (ROWS, LANES))
        speeds = [velocity[half(h), columns_of(kb)] for h in range(2)]
        reach, _, _ = scan_tile(back, [v * (1.0 / (v + rate)) for v in speeds], None)
        parts = [sum(past_residuals[j, half(h), columns_of(kb)] * reach[h] for h in range(2)) for j in range(HIST)]
        parts.append(sum(reach[h] * reach[h] for h in range(2)))
        parts.append(sum(reach[h] * padded[half(h), columns_of(kb + 1)] for h in range(2)))
        target[d, 2 * ROWS :, tile(t)] = jnp.where(row == 6, rate, jnp.where(row == 7, enters, added_rows(parts)))
    known = [directions[n] for n in range(tiles)] + [coupling[n] for n in range(coupling.shape[0])]
    for q in range(len(known) // ROWS):
        rows = jnp.zeros((ROWS, LANES), jnp.int32)
        for n in range(ROWS):
            rows = jnp.where(row == n, known[q * ROWS + n], rows)
        notes[half(q), :] = rows


def history_kernel(past_residuals, gram):
    tiles = past_residuals.shape[2] // LANES
    acc = [jnp.zeros((ROWS, LANES), jnp.float32) for _ in PAIRS]
    for kb in range(tiles):
        for h in range(2):
            past = [past_residuals[j, half(h), tile(kb)] for j in range(HIST)]
            for n, (i, j) in enumerate(PAIRS):
                acc[n] = acc[n] + past[i] * past[j]
    gram[...] = jnp.zeros(gram.shape, jnp.float32)
    for n in range(len(PAIRS)):
        gram[6 + n : 7 + n, :] = down(acc[n])


def at_contact(blocks, back, slope, inflow):
    row = iota(0)
    place = jnp.full((ROWS, LANES), lax.axis_index(POS), jnp.int32)
    first = (place == 0) & (row == 0) & jnp.logical_not(back)
    final = (place == blocks - 1) & (row == ROWS - 1) & back
    wide = jnp.broadcast_to(inflow, (ROWS, LANES))
    return [jnp.where(first, slope[0] * wide, 0.0), jnp.where(final, slope[1] * wide, 0.0)]


def fold_kernel(notes, velocity, *refs):
    chips = (len(refs) - 4) // 2
    held, message, own, other, across = refs[:chips], *refs[chips : chips + 3], refs[chips + 3 : -2]
    ready, gone = refs[-2:]
    bands = 2 * chips
    blocks = message.shape[0]
    per = own.shape[1] // LANES
    row, lane = iota(0), iota(1)
    band = lax.axis_index(BAND)
    chosen = [
        jnp.broadcast_to(notes[pl.ds(blocks + (band ^ u), 1), :], (ROWS, LANES)) ^ jnp.full((ROWS, LANES), band, jnp.int32)
        for u in range(bands)
    ]
    out = [
        pltpu.make_async_copy(
            ready.at[pl.ds(kt * bands, bands)], message.at[pl.ds(kt * bands, bands)], gone.at[kt]
        )
        for kt in range(per)
    ]
    for kt in range(per):
        kb = band * per + kt
        back = flag(notes, kb)
        speeds = [velocity[half(h), columns_of(kb)] for h in range(2)]
        spread = [[held[u // 2][u % 2, half(h), tile(kt)] for h in range(2)] for u in range(bands)]
        parts = []
        for u in range(bands):
            tail = held[u // 2][u % 2, 2 * ROWS :, tile(kt)]
            rate = jnp.broadcast_to(tail[6:7], (ROWS, LANES))
            slope, offset = [], []
            for h in range(2):
                partner = spread[0][h]
                for t in range(1, bands):
                    partner = jnp.where(chosen[u] == t, spread[t][h], partner)
                pair = spread[u][h] + partner
                if u < 2:
                    (other if u else own)[half(h), tile(kt)] = pair
                else:
                    across[u // 2 - 1][u % 2, half(h), tile(kt)] = pair
                inv = 1.0 / (speeds[h] + rate)
                slope.append(speeds[h] * inv)
                offset.append(rate * 0.5 * pair * inv)
            edge = at_contact(blocks, back, slope, tail[7:8])
            offset = [offset[h] + edge[h] for h in range(2)]
            reach, run, ends = scan_tile(back, slope, offset)
            crossed = jnp.broadcast_to(down(reach[0] * run[0] + reach[1] * run[1]), (ROWS, LANES)) - tail
            parts.append(
                jnp.where(row == 5, crossed, jnp.where(row == 6, ends[0], jnp.where(row == 7, ends[1], tail)))
            )
        for bit in range(3):
            step = 1 << bit
            high = ((lane >> (4 + bit)) & 1) == 1
            swapped = list(parts)
            for u in range(bands):
                if not u & step:
                    swapped[u] = jnp.where(high, pltpu.roll(parts[u + step], GROUP * step, 1), parts[u])
                    swapped[u + step] = jnp.where(high, parts[u + step], pltpu.roll(parts[u], LANES - GROUP * step, 1))
            parts = swapped
        for g in range(bands):
            ready[kt * bands + g] = parts[g]
        out[kt].start()
    for copy in out:
        copy.wait()


def settle_kernel(plan, notes, *refs):
    shares = refs[:-9]
    velocity, out_rate, inflow, wigner, past_residuals, early, reach_out, rest, gram = refs[-9:]
    per = rest.shape[2] // LANES
    blocks = velocity.shape[1] // LANES
    band = lax.axis_index(BAND)
    acc = [jnp.zeros((ROWS, LANES), jnp.float32) for _ in range(HIST + 1)]
    for which, place, u in plan:
        d = u // 2
        source = shares[which] if len(shares[which].shape) == 2 else shares[which].at[place]
        for kt in range(per):
            kb = (band ^ u) * per + kt
            back = flag(notes, kb)
            columns = pl.ds(pl.multiple_of(kb * LANES, LANES), LANES)
            rate = jnp.broadcast_to(out_rate[:, columns], (ROWS, LANES))
            slope, offset = [], []
            for h in range(2):
                v = velocity[half(h), columns]
                inv = 1.0 / (v + rate)
                slope.append(v * inv)
                offset.append(rate * 0.5 * source[half(h), tile(kt)] * inv)
            edge = at_contact(blocks, back, slope, inflow[:, columns])
            offset = [offset[h] + edge[h] for h in range(2)]
            reach, run, _ = scan_tile(back, slope, offset)
            for h in range(2):
                left = run[h] - wigner[half(h), columns]
                rest[d, half(h), tile(kt)] = left
                reach_out[d, half(h), tile(kt)] = reach[h]
                for j in range(HIST):
                    acc[j] = acc[j] + past_residuals[j, half(h), columns] * left
                acc[HIST] = acc[HIST] + left * left
    gram[half(0), :] = early[half(0), :] + added_rows(acc)
    gram[half(1), :] = early[half(1), :]


def carry_kernel(notes, sums, carries, terms, forth, counter):
    blocks = sums.shape[0]
    row = iota(0)
    back = flag(notes, lax.axis_index(BAND) * (blocks // ROWS) + lax.axis_index(POS) // ROWS)
    acc = jnp.zeros((ROWS, LANES), jnp.float32)
    carry = jnp.zeros((1, LANES), jnp.float32)
    for step in range(blocks):
        part = jnp.where(back, sums[blocks - 1 - step], sums[step])
        wide = jnp.broadcast_to(carry, (ROWS, LANES))
        forth[step : step + 1, :] = carry
        counter[blocks - 1 - step : blocks - step, :] = carry
        acc = acc + part * jnp.where(row == 4, wide * wide, jnp.where(row == 5, 2.0 * wide, wide))
        carry = part[6:7] * carry + part[7:8]
    for q in range(blocks // ROWS):
        carries[half(q), :] = jnp.where(back, counter[half(q), :], forth[half(q), :])
    terms[...] = jnp.where(row < 6, acc, 0.0)


def message_kernel(carries, terms, gram, message):
    blocks = carries.shape[0]
    row, lane = iota(0), iota(1)
    whole = [gram[half(0), :] + terms[...], gram[half(1), :]]
    line = jnp.zeros((ROWS, LANES), jnp.float32)
    for h in range(2):
        total = jnp.broadcast_to(jnp.sum(whole[h], axis=1, keepdims=True), (ROWS, LANES))
        line = line + jnp.where(lane == GROUP + h * ROWS + row, total, 0.0)
    line = jnp.broadcast_to(down(line), (ROWS, LANES))
    band = lax.axis_index(BAND)
    for q in range(blocks // ROWS):
        for u in range(LANES // GROUP):
            turned = pltpu.roll(carries[half(q), :], LANES - GROUP * u, 1) if u else carries[half(q), :]
            start = pl.multiple_of((band ^ u) * blocks + q * ROWS, ROWS)
            message[pl.ds(start, ROWS), :] = jnp.where(lane < GROUP, turned, line)


def mixing_weights(entry):
    count = HIST + 1
    scale = sum(entry(i, i) for i in range(count)) / count
    factor = {}
    for i in range(count):
        for j in range(i + 1):
            value = entry(j, i)
            if i == j:
                value = value + RIDGE_SCALE * scale
            for k in range(j):
                value = value - factor[i, k] * factor[j, k]
            factor[i, j] = jnp.sqrt(value) if i == j else value / factor[j, j]
    forward = []
    for row in range(count):
        partial = jnp.ones_like(scale)
        for inner in range(row):
            partial = partial - factor[row, inner] * forward[inner]
        forward.append(partial / factor[row, row])
    backward = [None] * count
    for row in reversed(range(count)):
        partial = forward[row]
        for inner in range(row + 1, count):
            partial = partial - factor[inner, row] * backward[inner]
        backward[row] = partial / factor[row, row]
    total = sum(backward)
    return [z / total for z in backward]


def finish_kernel(message, *refs):
    reach, rest = (refs[0], refs[2]), (refs[1], refs[3])
    wigner, past_iterates, past_residuals, residual, mixed, found, mixes, gone = refs[4:]
    cells, moments = wigner.shape
    chips, _, share = rest[0].shape
    per = share // LANES
    band = lax.axis_index(BAND)
    tiles = moments // LANES
    pieces = 4
    row, lane = iota(0), iota(1)
    out = []
    for n, (source, target) in enumerate(((found, residual), (mixes, mixed))):
        for q in range(pieces):
            columns = pl.ds(q * (moments // pieces), moments // pieces)
            out.append(pltpu.make_async_copy(source.at[:, columns], target.at[:, columns], gone.at[n * pieces + q]))
    total = message[half(0), :]
    for kb in range(1, tiles):
        total = total + message[half(kb), :]
    total = jnp.broadcast_to(down(total), (ROWS, LANES))

    def term(n):
        return pick(total, jnp.full((ROWS, LANES), GROUP + n, jnp.int32), 1)

    def entry(i, j):
        if j == HIST:
            return term(4) + term(5) if i == HIST else term(i)
        return term(6 + PAIRS.index((i, j)))

    for d in range(2 * chips):
        for kt in range(per):
            kb = (band ^ d) * per + kt
            rows = message[pl.ds(pl.multiple_of(kb * ROWS, ROWS), ROWS), :]
            spots = pick(rows, lane & (GROUP - 1), 1)
            carry = jnp.broadcast_to(down(jnp.where((lane >> 4) == row, spots, 0.0)), (ROWS, LANES))
            for h in range(2):
                at = (d // 2, half(h), tile(kt))
                found[half(h), pl.ds(pl.multiple_of(kb * LANES, LANES), LANES)] = rest[d % 2][at] + reach[d % 2][at] * carry
    for copy in out[:pieces]:
        copy.start()
    weights = mixing_weights(entry)
    for kb in range(tiles):
        for h in range(2):
            value = weights[HIST] * (wigner[half(h), tile(kb)] + MIX_STEP * found[half(h), tile(kb)])
            for j in range(HIST):
                earlier = past_iterates[j, half(h), tile(kb)] + MIX_STEP * past_residuals[j, half(h), tile(kb)]
                value = value + weights[j] * earlier
            mixes[half(h), tile(kb)] = value
        if (kb + 1) % (tiles // pieces) == 0:
            out[pieces + kb // (tiles // pieces)].start()
    for copy in out:
        copy.wait()


def body(wigner, past_iterates, past_residuals, velocity, out_rate, inflow, offsets, directions, coupling):
    _, cells, moments = wigner.shape
    bands = lax.axis_size(BAND)
    blocks = lax.axis_size(POS)
    wigner = wigner.reshape(cells, moments)
    past_iterates = past_iterates.reshape(HIST, cells, moments)
    past_residuals = past_residuals.reshape(HIST, cells, moments)
    offsets = offsets.reshape(1, moments)
    size = 4 * cells * moments
    share = moments // bands
    field = f32(cells, moments)
    dma = pltpu.SemaphoreType.DMA

    chips = lax.axis_size(BAND[0])

    def to_core(x):
        return lax.ppermute(x, BAND[1], [(0, 1), (1, 0)])

    def to_chip(x, d):
        return lax.ppermute(x, BAND[0], [(i, i ^ d) for i in range(chips)])

    sources = (offsets, wigner, directions, coupling, velocity, out_rate, inflow, past_residuals)
    opened = f32(chips, cells + ROWS, share)
    own, other, notes = call(
        open_kernel,
        (opened, opened, jax.ShapeDtypeStruct((blocks + bands, LANES), jnp.int32)),
        [HBM] * 8,
        20 * size,
        8 * size,
        [
            pltpu.SMEM(x.shape, x.dtype)
            if x.ndim == 1
            else pltpu.VMEM((cells, moments + 2 * LANES) if x is wigner else x.shape, x.dtype)
            for x in sources
        ]
        + [dma((8,))],
    )(*[pltpu.with_memory_space_constraint(x, pltpu.HBM) for x in sources])
    other = to_core(other)
    held = [jnp.stack([own[d], other[d]]) for d in range(chips)]
    held = held[:1] + [to_chip(held[d], d) for d in range(1, chips)]
    early = call(history_kernel, f32(16, LANES), [VMEM], 8 * size, 4 * size)(past_residuals)
    *held, early = lax.optimization_barrier((*held, early))
    pair = f32(2, cells, share)
    sums, own, other, *across = call(
        fold_kernel,
        (f32(blocks, ROWS, LANES), f32(cells, share), f32(cells, share)) + (pair,) * (chips - 1),
        [VMEM] * (chips + 2),
        20 * size,
        5 * size,
        [pltpu.VMEM((blocks, ROWS, LANES), jnp.float32), dma((4,))],
        out_specs=(HBM,) + (VMEM,) * (chips + 1),
    )(notes, velocity, *held)
    sums = lax.all_to_all(sums, POS, 0, 0, tiled=True)
    across = [to_chip(across[d - 1], d) for d in range(1, chips)]
    other = [other] + [x[1] for x in across]
    groups = [[0, 3, 2], [1]]
    others = [to_core(jnp.stack([other[d] for d in group])) for group in groups]
    local = (velocity, out_rate, inflow, wigner, past_residuals)
    part = f32(chips, cells, share)
    settled = []
    gram = early
    plans = [(n, 0, 2 * n) for n in range(chips)], [(n, m, 2 * d + 1) for n, g in enumerate(groups) for m, d in enumerate(g)]
    for plan, shares in zip(plans, ((own, *across), others)):
        reach, rest, gram = call(
            functools.partial(settle_kernel, plan),
            (part, part, f32(16, LANES)),
            [VMEM] * (len(shares) + 7),
            size // 64,
            size // 64,
        )(notes, *shares, *local, gram)
        settled += [reach, rest]
    carries, terms = call(
        carry_kernel,
        (f32(blocks, LANES), f32(ROWS, LANES)),
        [VMEM] * 2,
        size,
        256 * size,
        [pltpu.VMEM((blocks, LANES), jnp.float32)] * 2,
    )(notes, sums)
    message = call(message_kernel, f32(bands * blocks, LANES), [VMEM] * 3, size, size)(carries, terms, gram)
    message = lax.all_to_all(message, ALL, 0, 0, tiled=True)
    residual, mixed = call(
        finish_kernel,
        (field, field),
        [VMEM] * 8,
        8 * size,
        14 * size,
        [pltpu.VMEM((cells, moments), jnp.float32)] * 2 + [dma((8,))],
        out_specs=(HBM, HBM),
    )(message, *settled, wigner, past_iterates, past_residuals)
    return mixed[None], residual[None]


def solution(mesh):
    finer = Mesh(mesh.devices.reshape(4, 2, 4, 8), ("band_0", "band_1", "pos_0", "pos_1"))
    in_specs = (
        P(BAND, POS, None),
        P(None, BAND, POS, None),
        P(None, BAND, POS, None),
        P(POS, None),
        P(BAND, None),
        P(BAND, None),
        P(),
        P(),
        P(),
    )
    out_specs = (P(BAND, POS, None), P(BAND, POS, None))
    return jax.shard_map(body, mesh=finer, in_specs=in_specs, out_specs=out_specs, check_vma=False)
```
